128 devices in a mesh: seq: 16 (over y, x), dp: 8 (over z, core).
Axes of the slice: x: 4, y: 4, z: 4, core: 2. Of those that a mesh axis runs over, the one named last changes fastest.
Arguments:
- block_in: bfloat16 [16, 2048, 1536], P('dp', 'seq'), may hold values from -6 to 6
- cotangent: bfloat16 [16, 2048, 1536], P('dp', 'seq'), may hold values from -6 to 6
- in_master: float32 [1536, 6448], P(('seq', 'dp')), may hold values from -0.15625 to 0.15625
- in_moment1: float32 [1536, 6448], P(('seq', 'dp')), may hold values from -64 to 64
- in_moment2: float32 [1536, 6448], P(('seq', 'dp')), may hold values from 216.2688 to 3440.64
- out_master: float32 [3072, 1536], P(('seq', 'dp')), may hold values from -0.109375 to 0.109375
- out_moment1: float32 [3072, 1536], P(('seq', 'dp')), may hold values from -128 to 128
- out_moment2: float32 [3072, 1536], P(('seq', 'dp')), may hold values from 851.968 to 13762.56
- conv_master: float32 [5, 3328], P(None, ('seq', 'dp')), may hold values from -3 to 3
- conv_moment1: float32 [5, 3328], P(None, ('seq', 'dp')), may hold values from -64 to 64
- conv_moment2: float32 [5, 3328], P(None, ('seq', 'dp')), may hold values from 216.2688 to 3440.64
- gain_master: float32 [4608], P(('seq', 'dp')), may hold values from 0.1 to 1.9
- gain_moment1: float32 [4608], P(('seq', 'dp')), may hold values from -128 to 128
- gain_moment2: float32 [4608], P(('seq', 'dp')), may hold values from 851.968 to 13762.56
- head_master: float32 [3, 48], replicated, may hold values from -9.5 to 1.5
- head_moment1: float32 [3, 48], replicated, may hold values from -256 to 256
- head_moment2: float32 [3, 48], replicated, may hold values from 5033.165 to 79691.77
Outputs:
- block_out: bfloat16 [16, 2048, 1536], P('dp', 'seq')
- input_grad: float32 [16, 2048, 1536], P('dp', 'seq')
- in_moment1_next: float32 [1536, 6448], P(('seq', 'dp'))
- in_moment2_next: float32 [1536, 6448], P(('seq', 'dp'))
- in_master_next: float32 [1536, 6448], P(('seq', 'dp'))
- out_moment1_next: float32 [3072, 1536], P(('seq', 'dp'))
- out_moment2_next: float32 [3072, 1536], P(('seq', 'dp'))
- out_master_next: float32 [3072, 1536], P(('seq', 'dp'))
- conv_moment1_next: float32 [5, 3328], P(None, ('seq', 'dp'))
- conv_moment2_next: float32 [5, 3328], P(None, ('seq', 'dp'))
- conv_master_next: float32 [5, 3328], P(None, ('seq', 'dp'))
- gain_moment1_next: float32 [4608], P(('seq', 'dp'))
- gain_moment2_next: float32 [4608], P(('seq', 'dp'))
- gain_master_next: float32 [4608], P(('seq', 'dp'))
- head_moment1_next: float32 [3, 48], replicated
- head_moment2_next: float32 [3, 48], replicated
- head_master_next: float32 [3, 48], replicated
The draws below stay inside these ranges and needn't reach their ends.
All inputs are finite; a program needn't handle non-finite values.
Results may differ from the reference program's by a relative error of at most 0.012.
The reference program's roundings to bfloat16 on the way count: a program that leaves them out, or rounds other values in their place, can miss the bound.
Values may be sent and summed in bfloat16 or wider, within the bound.
No kernel may reach another device: no remote copies, remote signals or barrier semaphores. Data moves between devices by JAX's collectives and lax.ppermute only.
A program may use at most 256 MiB of HBM per device.

```python
import math
import jax
import jax.numpy as jnp
from jax import lax

D = 1536
INNER = 3072
STATE = 128
HEADDIM = 64
KERNEL = 4
STEP = 5
HEADS = 48
CONV = 3328
PROJ = 6448
GAINS = 4608
SEQUENCES = 16
LENGTH = 2048
TOKENS = 32768


def draw_head_master(key, part):
    key = jax.random.fold_in(key, 11)
    subkeys = jax.random.split(key, 3)
    log_rates = jax.random.uniform(subkeys[0], (HEADS,), jnp.float32, -8.0, -1.0)
    dt_bias = jax.random.uniform(subkeys[1], (HEADS,), jnp.float32, -3.5, -2.5)
    skip_gain = jax.random.uniform(subkeys[2], (HEADS,), jnp.float32, 0.5, 1.5)
    return jnp.stack([log_rates, dt_bias, skip_gain])


def level_of(own_key, extent, cuts, low, top_value):
    def one(axis_at, shards_of):
        draws = jax.random.uniform(jax.random.fold_in(jax.random.fold_in(own_key, 6), axis_at), (shards_of,), jnp.float32, low / len(cuts), top_value / len(cuts))
        return jnp.repeat(jnp.exp(draws), extent[axis_at] // shards_of).reshape((-1,) + (1,) * (len(extent) - axis_at - 1))

    factor_of = one(*cuts[0])
    for cut in cuts[1:]:
        factor_of = factor_of * one(*cut)
    return factor_of


def normal_values(key, shape, deviation, reach, cuts=(), kind=jnp.bfloat16):
    loudness = level_of(key, shape, cuts, -0.22, 0.18) if cuts else 1.0
    drawn = jax.random.normal(key, shape, jnp.float32) * deviation * loudness
    return jnp.minimum(jnp.maximum(drawn, -reach), reach).astype(kind)


def setup_inputs(seed: int = 0) -> dict:
    keys = jax.random.split(jax.random.key(seed), 18)
    block_in = normal_values(keys[0], (SEQUENCES, LENGTH, D), 1.0, 6.0, ((0, 8), (1, 16)))
    cotangent = normal_values(keys[1], (SEQUENCES, LENGTH, D), 1.0, 6.0, ((0, 8), (1, 16)))
    in_master = normal_values(keys[2], (D, PROJ), D ** -0.5, 0.15625, ((0, 128),), jnp.float32)
    in_moment1 = normal_values(keys[3], (D, PROJ), (0.055 * TOKENS ** 0.5), 64.0, ((0, 128),), jnp.float32)
    in_moment2 = jnp.clip(jnp.exp(math.log(3440.64) - 2.7668907 * jax.random.uniform(keys[4], (D, PROJ), jnp.float32) ** level_of(keys[4], (D, PROJ), ((0, 128),), -0.2, 0.2)), 216.2688, 3440.64)
    out_master = normal_values(keys[5], (INNER, D), INNER ** -0.5, 0.109375, ((0, 128),), jnp.float32)
    out_moment1 = normal_values(keys[6], (INNER, D), (0.11 * TOKENS ** 0.5), 128.0, ((0, 128),), jnp.float32)
    out_moment2 = jnp.clip(jnp.exp(math.log(13762.56) - 2.7821581 * jax.random.uniform(keys[7], (INNER, D), jnp.float32) ** level_of(keys[7], (INNER, D), ((0, 128),), -0.2, 0.2)), 851.968, 13762.56)
    conv_master = normal_values(keys[8], (KERNEL + 1, CONV), 0.5, 3.0, ((1, 128),), jnp.float32)
    conv_moment1 = normal_values(keys[9], (KERNEL + 1, CONV), (0.055 * TOKENS ** 0.5), 64.0, ((1, 128),), jnp.float32)
    conv_moment2 = jnp.clip(jnp.exp(math.log(3440.64) - 2.7668907 * jax.random.uniform(keys[10], (KERNEL + 1, CONV), jnp.float32) ** level_of(keys[10], (KERNEL + 1, CONV), ((1, 128),), -0.2, 0.2)), 216.2688, 3440.64)
    gain_master = jnp.clip(1.0 + 0.18 * jax.random.normal(keys[11], (GAINS,), jnp.float32), 0.1, 1.9)
    gain_moment1 = normal_values(keys[12], (GAINS,), (0.11 * TOKENS ** 0.5), 128.0, ((0, 128),), jnp.float32)
    gain_moment2 = jnp.clip(jnp.exp(math.log(13762.56) - 2.7821581 * jax.random.uniform(keys[13], (GAINS,), jnp.float32) ** level_of(keys[13], (GAINS,), ((0, 128),), -0.2, 0.2)), 851.968, 13762.56)
    head_master = draw_head_master(jax.random.fold_in(keys[17], 71), 0)
    head_moment1 = normal_values(keys[15], (3, HEADS), (0.033 * (TOKENS * HEADDIM) ** 0.5), 256.0, (), jnp.float32)
    head_moment2 = jnp.clip(jnp.exp(jax.random.uniform(keys[16], (3, HEADS), jnp.float32, math.log(5033.165), math.log(79691.77))), 5033.165, 79691.77)
    return {"block_in": block_in, "cotangent": cotangent, "in_master": in_master, "in_moment1": in_moment1, "in_moment2": in_moment2, "out_master": out_master, "out_moment1": out_moment1, "out_moment2": out_moment2, "conv_master": conv_master, "conv_moment1": conv_moment1, "conv_moment2": conv_moment2, "gain_master": gain_master, "gain_moment1": gain_moment1, "gain_moment2": gain_moment2, "head_master": head_master, "head_moment1": head_moment1, "head_moment2": head_moment2}


@jax.custom_vjp
def low(v):
    return lax.optimization_barrier(v.astype(jnp.bfloat16)).astype(jnp.float32)

@jax.custom_vjp
def low_back(v):
    return v

def low_keep(v):
    return (low(v), None)

def low_pass(kept, grad):
    return (grad,)

def back_keep(v):
    return (v, None)

def back_low(kept, grad):
    return (low(grad),)
low.defvjp(low_keep, low_pass)
low_back.defvjp(back_keep, back_low)
NORM_EPS = 1e-05
PRECISE = lax.Precision.HIGHEST
BETA_ONE = 0.9
BETA_TWO = 0.95
ADAM_EPS = 1e-08
MATRIX_RATE = 0.05
SMALL_RATE = 0.5
MATRIX_DECAY = 0.1

def rms_scale(values, gain):
    return values * lax.rsqrt(lax.optimization_barrier(jnp.mean(values * values, axis=-1, keepdims=True)) + NORM_EPS) * gain

def ssd_block(carried_in, pieces):
    head_x, step_size, b_proj, c_proj, log_decay, skip_gain = pieces
    cumulative = jnp.cumsum(log_decay, axis=0)
    length = head_x.shape[0]
    row_ids = lax.broadcasted_iota(jnp.int32, (length, length), 0)
    col_ids = lax.broadcasted_iota(jnp.int32, (length, length), 1)
    causal = row_ids >= col_ids
    by_head = cumulative.T
    differ = by_head[:, :, None] - by_head[:, None, :]
    decay_mask = jnp.where(causal, jnp.exp(jnp.where(causal, differ, 0.0)), 0.0)
    scores = jnp.dot(c_proj, b_proj.T, precision=PRECISE, preferred_element_type=jnp.float32)
    mixing = scores[None] * decay_mask * step_size.T[:, None, :]
    within = jnp.einsum('hlm,mhp->lhp', mixing, head_x, precision=PRECISE)
    carried = jnp.einsum('ln,hpn->lhp', c_proj, carried_in, precision=PRECISE) * jnp.exp(cumulative)[:, :, None]
    outputs = within + carried + skip_gain[None, :, None] * head_x
    tail_weight = jnp.exp(cumulative[-1][None, :] - cumulative) * step_size
    leaving = jnp.exp(cumulative[-1])[:, None, None] * carried_in + jnp.einsum('mh,mhp,mn->hpn', tail_weight, head_x, b_proj, precision=PRECISE)
    return (leaving, outputs)

def sequence_forward(tokens, w_in, w_out, conv_weights, gain_values, head_params):
    normed = low(rms_scale(tokens, gain_values[:D]))
    projected = low_back(jnp.dot(normed, w_in, precision=PRECISE, preferred_element_type=jnp.float32))
    gate_proj = projected[:, :INNER]
    conv_input = projected[:, INNER:INNER + CONV]
    dt_raw = projected[:, INNER + CONV:]
    padded = jnp.pad(conv_input, ((KERNEL - 1, 0), (0, 0)))
    preact = conv_weights[KERNEL] + conv_weights[0] * padded[0:LENGTH]
    for offset in range(1, KERNEL):
        preact = preact + conv_weights[offset] * padded[offset:offset + LENGTH]
    activated = jax.nn.silu(preact)
    head_x = activated[:, :INNER].reshape(LENGTH, HEADS, HEADDIM)
    b_proj = activated[:, INNER:INNER + STATE]
    c_proj = activated[:, INNER + STATE:]
    step_size = jax.nn.softplus(dt_raw + head_params[1])
    log_decay = step_size * -jnp.exp(head_params[0])
    block_len = math.gcd(LENGTH, 256)
    blocks = LENGTH // block_len
    pieces = (head_x.reshape(blocks, block_len, HEADS, HEADDIM), step_size.reshape(blocks, block_len, HEADS), b_proj.reshape(blocks, block_len, STATE), c_proj.reshape(blocks, block_len, STATE), log_decay.reshape(blocks, block_len, HEADS))
    skip_gain = head_params[2]

    def advance(carried_in, piece):
        return ssd_block(carried_in, piece + (skip_gain,))
    zero_state = jnp.zeros((HEADS, HEADDIM, STATE), jnp.float32)
    unused, results = lax.scan(jax.checkpoint(advance), zero_state, pieces)
    mixed_out = results.reshape(LENGTH, INNER)
    gated = mixed_out * jax.nn.silu(gate_proj)
    gated_low = low(rms_scale(gated, gain_values[D:]))
    return tokens + jnp.dot(gated_low, w_out, precision=PRECISE, preferred_element_type=jnp.float32)

def adamw_step(weight, gradient, moment_one, moment_two, step_rate, weight_decay):
    one_next = BETA_ONE * moment_one + (1.0 - BETA_ONE) * gradient
    two_next = BETA_TWO * moment_two + (1.0 - BETA_TWO) * gradient * gradient
    corrected = one_next / (1.0 - BETA_ONE ** STEP)
    scale_next = jnp.sqrt(two_next / (1.0 - BETA_TWO ** STEP)) + ADAM_EPS
    weight_next = weight - step_rate * (corrected / scale_next + weight_decay * weight)
    return (one_next, two_next, weight_next)

def reference(block_in, cotangent, in_master, in_moment1, in_moment2, out_master, out_moment1, out_moment2, conv_master, conv_moment1, conv_moment2, gain_master, gain_moment1, gain_moment2, head_master, head_moment1, head_moment2):
    tokens = block_in.astype(jnp.float32)
    upstream = cotangent.astype(jnp.float32)

    def forward(all_tokens, in_weight, out_weight, conv_weight, gain_weight, head_weight):
        w_in = low(in_weight)
        w_out = low(out_weight)
        conv_weights = low(conv_weight)
        gain_values = low(gain_weight)

        def per_sequence(carried_in, seq_tokens):
            return (carried_in, sequence_forward(seq_tokens, w_in, w_out, conv_weights, gain_values, head_weight))
        unused, results = lax.scan(jax.checkpoint(per_sequence), jnp.zeros((), jnp.float32), all_tokens)
        return results
    result, pullback = jax.vjp(forward, tokens, in_master, out_master, conv_master, gain_master, head_master)
    gradients = pullback(upstream)
    block_out = result.astype(jnp.bfloat16)
    input_grad = gradients[0]
    in_next = adamw_step(in_master, gradients[1], in_moment1, in_moment2, MATRIX_RATE, MATRIX_DECAY)
    out_next = adamw_step(out_master, gradients[2], out_moment1, out_moment2, MATRIX_RATE, MATRIX_DECAY)
    conv_next = adamw_step(conv_master, gradients[3], conv_moment1, conv_moment2, SMALL_RATE, 0.0)
    gain_next = adamw_step(gain_master, gradients[4], gain_moment1, gain_moment2, SMALL_RATE, 0.0)
    head_next = adamw_step(head_master, gradients[5], head_moment1, head_moment2, SMALL_RATE, 0.0)
    return (block_out, input_grad, in_next[0], in_next[1], in_next[2], out_next[0], out_next[1], out_next[2], conv_next[0], conv_next[1], conv_next[2], gain_next[0], gain_next[1], gain_next[2], head_next[0], head_next[1], head_next[2])
```

```python
import jax
import jax.numpy as jnp
from jax import lax
from jax.sharding import Mesh
from jax.sharding import PartitionSpec as P

WIDTH = 1536
INNER = 3072
STATE = 128
HEADDIM = 64
KERNEL = 4
STEP = 5
HEADS = 48
CONV = 3328
PROJ = 6448

HALF = INNER // 2
HALF_HEADS = HEADS // 2
TOKENS = 512
OWN = TOKENS // 2
HALO = 16
ROWS_IN = TOKENS + HALO
CHUNK = 128
CHUNKS = TOKENS // CHUNK
LANES = 128
ACT = HALF + 2 * STATE
CRIT = ACT + LANES
PART = 1024
ROWS = 24

NORM_EPS = 1e-05
PRECISE = lax.Precision.HIGH
EXACT = lax.Precision.HIGHEST
BETA_ONE = 0.9
BETA_TWO = 0.95
ADAM_EPS = 1e-08
MATRIX_RATE = 0.05
SMALL_RATE = 0.5
MATRIX_DECAY = 0.1
BF16 = jnp.bfloat16
F32 = jnp.float32
CHIPS = ("y", "x", "z")
ALL = ("y", "x", "z", "c")


def mm(a, b, dims=((1,), (0,))):
    return lax.dot_general(
        a.astype(BF16), b.astype(BF16), (dims, ((), ())), preferred_element_type=F32
    )


def exact(a, b, dims=((1,), (0,))):
    return lax.dot_general(a, b, (dims, ((), ())), precision=PRECISE, preferred_element_type=F32)


NT = ((1,), (1,))
TN = ((0,), (0,))


def rounded(v):
    return lax.reduce_precision(v, 8, 7)


def iota(shape, dim):
    return lax.broadcasted_iota(jnp.int32, shape, dim)


def sigmoid(v):
    return 1.0 / (1.0 + jnp.exp(-v))


def spread_matrix():
    return (iota((LANES, HALF), 1) // HEADDIM == iota((LANES, HALF), 0)).astype(F32)


def adamw_step(weight, gradient, moment_one, moment_two, step_rate, weight_decay):
    one_next = BETA_ONE * moment_one + (1.0 - BETA_ONE) * gradient
    two_next = BETA_TWO * moment_two + (1.0 - BETA_TWO) * gradient * gradient
    corrected = one_next / (1.0 - BETA_ONE**STEP)
    scale_next = jnp.sqrt(two_next / (1.0 - BETA_TWO**STEP)) + ADAM_EPS
    weight_next = weight - step_rate * (corrected / scale_next + weight_decay * weight)
    return (one_next, two_next, weight_next)


def swap_cores(value):
    return lax.ppermute(value, "c", [(0, 1), (1, 0)])


def regroup(value, turn):
    pairs = [
        (x * 2 + c, (2 * c + (x + turn) % 2) * 2 + x // 2) for x in range(4) for c in range(2)
    ]
    return lax.ppermute(value, ("x", "c"), pairs)


def cross_halves(value):
    pairs = []
    for y in range(4):
        for c in range(2):
            to = (y, c) if y // 2 == c else (y ^ 2, 1 - c)
            pairs.append((y * 2 + c, to[0] * 2 + to[1]))
    return lax.ppermute(value, ("y", "c"), pairs)


def along_y(value, steps):
    return lax.ppermute(value, "y", [(y, y + steps) for y in range(4) if 0 <= y + steps < 4])


def partner(axis, turn):
    pairs = []
    for i in range(4):
        for c in range(2):
            pairs.append((i * 2 + c, (i ^ (1 if (turn + c) % 2 == 0 else 3)) * 2 + c))
    return (axis, "c"), pairs


def exchange(value, axis, turn):
    axes, pairs = partner(axis, turn)
    return lax.ppermute(value, axes, pairs)


def block_order(order):
    first = jnp.where(lax.axis_index("c") == 0, 1, 3)
    second = 4 - first
    block = jnp.arange(64)
    place = {a: lax.axis_index(a) for a in CHIPS}
    for at, axis in enumerate(order):
        high = (block >> (5 - 2 * at)) & 1
        low = (block >> (4 - 2 * at)) & 1
        place[axis] = place[axis] ^ (high * first) ^ (low * second)
    return [place[a] + jnp.zeros((64,), jnp.int32) for a in CHIPS]


def rows_of(blocks):
    return (blocks[:, None] * ROWS + jnp.arange(ROWS)[None, :]).reshape(-1)


def in_rows(order):
    y, x, z = block_order(order)
    return rows_of((y * 4 + x) * 4 + z)


def out_rows(order):
    y, x, z = block_order(order)
    return rows_of((((y % 2) * 4 + x) * 4 + z) * 2 + y // 2)


def pick(rows):
    return (rows[:, None] == iota((1536, 1536), 1)).astype(BF16)


def reduce_scatter(sends, keeps, orders):
    for step in range(6):
        arrived = []
        for send, order in zip(sends, orders):
            arrived.append(exchange(send.astype(BF16), order[step // 2], step % 2))
        totals = [keep.astype(F32) + got.astype(F32) for keep, got in zip(keeps, arrived)]
        half = totals[0].shape[0] // 2
        if step < 5:
            sends = [t[half:] for t in totals]
            keeps = [t[:half] for t in totals]
    return totals


PAIRS = HALF_HEADS // 2


def product(terms, a, b):
    return jnp.einsum(terms, a, b, preferred_element_type=F32)


def by_pair(value):
    return value.reshape(CHUNKS, CHUNK, PAIRS, LANES).transpose(0, 2, 1, 3)


def from_pairs(value):
    return value.transpose(0, 2, 1, 3).reshape(TOKENS, HALF)


def one_head(value):
    left = iota((2, 1, LANES), 2) // HEADDIM == iota((2, 1, LANES), 0)
    return jnp.where(left, value[:, :, None], jnp.zeros((), value.dtype))


def decays(cl):
    heads = cl[:, :HALF_HEADS].reshape(CHUNKS, CHUNK, PAIRS, 2).transpose(0, 2, 3, 1)
    causal = iota((CHUNK, CHUNK), 0) >= iota((CHUNK, CHUNK), 1)
    differ = jnp.where(causal, heads[..., :, None] - heads[..., None, :], 0.0)
    return jnp.where(causal, jnp.exp(differ), 0.0)


def pack_state(state, decay):
    high = rounded(decay)
    middle = rounded(decay - high)
    low = rounded(decay - high - middle)
    at = iota((16, LANES), 0)
    rows = jnp.where(at == 0, high, jnp.where(at == 1, middle, 0.0))
    rows = jnp.where(at == 2, low, rows)
    return jnp.concatenate([state, rows], axis=0).astype(BF16)


def unpack_state(packed):
    rows = packed[HALF : HALF + 3].astype(F32)
    return packed[:HALF].astype(F32), rows[0] + rows[1] + rows[2]


def per_row(head_values):
    heads = head_values[..., :HALF_HEADS, None]
    wide = jnp.broadcast_to(heads, heads.shape[:-1] + (HEADDIM,))
    return wide.reshape(head_values.shape[:-1] + (HALF, 1))


def combine(packed, way, unpack):
    near, far, farthest = [unpack(along_y(packed, way * k)) for k in (1, 2, 3)]
    return near[0] + per_row(near[1]) * (far[0] + per_row(far[1]) * farthest[0])


def pack_full(state, decay):
    return jnp.concatenate([state, jnp.broadcast_to(decay[None], (8, LANES))], axis=0)


def unpack_full(packed):
    return packed[:HALF], packed[HALF]


def chunked(value):
    return value.reshape(CHUNKS, CHUNK, value.shape[-1])


def flat(value):
    return value.reshape(TOKENS, value.shape[-1])


def sum_all_chips(value):
    for axis in CHIPS:
        for turn in range(2):
            value = value + exchange(value, axis, turn)
    return value


def on_device(
    block_in,
    cotangent,
    in_master,
    in_moment1,
    in_moment2,
    out_master,
    out_moment1,
    out_moment2,
    conv_master,
    conv_moment1,
    conv_moment2,
    gain_master,
    gain_moment1,
    gain_moment2,
    head_master,
    head_moment1,
    head_moment2,
):
    core = lax.axis_index("c")
    x_at = lax.axis_index("x")
    first_core = core == 0
    even_x = x_at % 2 == 0

    def ordered(flag, mine, other, axis=0):
        return jnp.where(
            flag, jnp.concatenate([mine, other], axis=axis), jnp.concatenate([other, mine], axis=axis)
        )

    def half_columns(c):
        return jnp.concatenate(
            [
                in_master[:, INNER + c * HALF : INNER + (c + 1) * HALF],
                in_master[:, 2 * INNER : INNER + CONV],
                in_master[:, INNER + CONV + c * HALF_HEADS : INNER + CONV + (c + 1) * HALF_HEADS],
                jnp.zeros((12, LANES - HALF_HEADS), F32),
                in_master[:, c * HALF : (c + 1) * HALF],
            ],
            axis=1,
        )

    halves = [half_columns(0), half_columns(1)]
    mine = jnp.where(first_core, halves[0], halves[1])
    theirs = jnp.where(first_core, halves[1], halves[0])
    in_rows_low = ordered(first_core, mine, swap_cores(theirs)).astype(BF16)
    out_rows_low = cross_halves(out_master).astype(BF16)
    small = jnp.zeros((8, LANES), F32)
    small = small.at[:5, :26].set(rounded(conv_master))
    small = small.at[5, :36].set(rounded(gain_master))
    small_all = lax.all_gather(small, ALL, axis=0, tiled=False)
    gathered = lax.all_gather(
        jnp.concatenate([in_rows_low, out_rows_low], axis=1), CHIPS, axis=0, tiled=True
    )
    w_crit = gathered[:, :CRIT]
    w_gate = gathered[:, CRIT : CRIT + HALF]
    w_out = (
        gathered[:, CRIT + HALF :]
        .reshape(2, 2, 16, ROWS, WIDTH)
        .transpose(1, 2, 0, 3, 4)
        .reshape(HALF, WIDTH)
    )
    conv_all = small_all[:, :5, :26].transpose(1, 0, 2).reshape(5, CONV)
    gain_all = small_all[:, 5, :36].reshape(-1)
    norm_gain = gain_all[:WIDTH]
    gate_gain = lax.dynamic_slice(gain_all, (WIDTH + core * HALF,), (HALF,))
    conv_weights = jnp.concatenate(
        [lax.dynamic_slice(conv_all, (0, core * HALF), (5, HALF)), conv_all[:, INNER:]], axis=1
    )
    head_half = jnp.pad(
        lax.dynamic_slice(head_master, (0, core * HALF_HEADS), (3, HALF_HEADS)),
        ((0, 0), (0, LANES - HALF_HEADS)),
    )
    decay_rate = -jnp.exp(head_half[0])

    both = jnp.stack([block_in, cotangent], axis=1)
    flipped = both[::-1]
    got = [regroup(jnp.where(even_x, both, flipped)[k], k) for k in range(2)]
    own_both = ordered(even_x, got[0], got[1], axis=1)
    all_both = ordered(first_core, own_both, swap_cores(own_both), axis=1)
    own_in, own_cot = own_both[0], own_both[1]
    tokens, cot = all_both[0], all_both[1]
    halo = along_y(tokens[TOKENS - HALO :], 1)
    extended = jnp.concatenate([tokens, halo], axis=0).astype(F32)
    inv = lax.rsqrt(jnp.mean(extended * extended, axis=1, keepdims=True) + NORM_EPS)
    normed = (extended * inv * norm_gain).astype(BF16)

    crit = mm(normed, w_crit)
    ext = jnp.concatenate([crit[TOKENS + 8 :, :ACT], crit[:TOKENS, :ACT]], axis=0)
    preact = conv_weights[KERNEL] + sum(
        conv_weights[k] * ext[5 + k : 5 + k + TOKENS] for k in range(KERNEL)
    )
    gate_of_act = sigmoid(preact)
    act = preact * gate_of_act
    head_x = act[:, :HALF]
    bc = act[:, HALF:]
    dt_in = crit[:TOKENS, ACT:] + head_half[1]
    real = iota((1, LANES), 1) < HALF_HEADS
    dt = jnp.where(real, jax.nn.softplus(dt_in), 0.0)
    log_decay = dt * decay_rate
    below = (iota((CHUNK, CHUNK), 0) >= iota((CHUNK, CHUNK), 1)).astype(F32)
    below = jnp.broadcast_to(below[None], (CHUNKS, CHUNK, CHUNK))
    cl = jnp.einsum("kts,ksh->kth", below, chunked(log_decay), precision=EXACT)
    spread = spread_matrix()
    u = head_x * exact(dt, spread)
    u_low = rounded(u)
    lasts = cl[:, -1]
    to_end = flat(jnp.exp(lasts[:, None] - cl))
    cl = flat(cl)
    to_end_wide = exact(to_end, spread)
    from_start_wide = exact(jnp.exp(cl), spread)
    u_wide = u * to_end_wide
    b_proj, c_proj = chunked(bc[:, :STATE]), chunked(bc[:, STATE:])
    b_low, c_low = b_proj.astype(BF16), c_proj.astype(BF16)
    own = jnp.einsum("ktr,ktn->krn", chunked(u_wide), b_proj, precision=PRECISE)
    def between(i, j):
        return per_row(jnp.exp(sum(lasts[i:j])) if j > i else jnp.ones((LANES,), F32))

    local = [jnp.zeros_like(own[0])]
    for k in range(CHUNKS):
        local.append(sum(between(i + 1, k + 1) * own[i] for i in range(k + 1)))
    piece_decay = jnp.exp(jnp.sum(lasts, axis=0))
    incoming = combine(pack_full(local[CHUNKS], piece_decay), 1, unpack_full)
    decay = decays(cl)
    scores = jnp.einsum("ktn,ksn->kts", c_proj, b_proj, precision=PRECISE)
    mixes = (scores[:, None, None] * decay).astype(BF16)
    u_pairs = one_head(by_pair(u_low.astype(BF16)))
    y_chunk = from_pairs(product("kpjts,kpjsc->kptc", mixes, u_pairs))

    starts = jnp.stack([between(0, k) * incoming + local[k] for k in range(CHUNKS)])
    state_end = between(0, CHUNKS) * incoming + local[CHUNKS]
    y_state = flat(jnp.einsum("ktn,krn->ktr", c_proj, starts, precision=PRECISE)) * from_start_wide
    y_ssd = y_chunk + y_state
    skip_wide = exact(head_half[2:3], spread)
    mixed = y_ssd + skip_wide * head_x

    gate = mm(normed[:TOKENS], w_gate)
    gate_sig = sigmoid(gate)
    gate_silu = gate * gate_sig
    d_gated = mm(cot, w_out, NT)
    g = mixed * gate_silu
    e = d_gated * gate_gain
    sums = jnp.concatenate(
        [jnp.sum(g * g, axis=1, keepdims=True), jnp.sum(e * g, axis=1, keepdims=True)], axis=1
    )
    sums = (sums + swap_cores(sums)) / INNER
    r = lax.rsqrt(sums[:, :1] + NORM_EPS)
    gated_low = (g * r * gate_gain).astype(BF16)
    d_g = r * e - (r * r * r) * g * sums[:, 1:]
    d_gate_gain = jnp.sum(d_gated * g * r, axis=0)
    dy = d_g * gate_silu
    d_gate = (d_g * mixed * (gate_sig * (1.0 + gate * (1.0 - gate_sig)))).astype(BF16)
    dy_low = rounded(dy)

    dy_start = chunked(dy * from_start_wide)
    chunk_backs = jnp.einsum("ktr,ktn->krn", dy_start, c_proj, precision=PRECISE)
    back = [None] * CHUNKS
    for k in range(CHUNKS):
        back[k] = sum((between(k + 1, i) * chunk_backs[i] for i in range(k + 1, CHUNKS)), jnp.zeros_like(own[0]))
    to_before = sum(between(0, i) * chunk_backs[i] for i in range(CHUNKS))
    leaving = combine(pack_state(to_before, piece_decay), -1, unpack_state)
    dy_pairs = by_pair(dy_low.astype(BF16))
    du_chunk = from_pairs(product("kpjts,kpjtc->kpsc", mixes, one_head(dy_pairs)))
    both = product("kptc,kpjsc->kpjts", dy_pairs, u_pairs)
    d_scores = jnp.sum(decay * both, axis=(1, 2)).astype(BF16)
    db_chunk = product("kts,ktn->ksn", d_scores, c_low)
    dc_chunk = product("kts,ksn->ktn", d_scores, b_low)

    part_out = mm(gated_low, w_out)

    def own_rows(value):
        return jnp.where(first_core, value[:OWN], value[OWN:]), jnp.where(
            first_core, value[OWN:], value[:OWN]
        )

    def to_owner(value):
        low, high = value[:CHUNK], value[CHUNK:]
        sent = [jnp.where(even_x, low, high), jnp.where(even_x, high, low)]
        back0, back1 = regroup(sent[0], 0), regroup(sent[1], 1)
        return jnp.where(even_x, jnp.stack([back0, back1]), jnp.stack([back1, back0]))

    kept, other = own_rows(part_out)
    own_out = own_in.astype(F32) + (kept + swap_cores(other))
    block_out = to_owner(own_out.astype(BF16))

    order_a, order_b = ("y", "x", "z"), ("x", "y", "z")
    pick_in_a, pick_in_b = pick(in_rows(order_a)), pick(in_rows(order_b))
    pick_out_b = pick(out_rows(order_b))
    normed_a = mm(pick_in_a, normed, NT).astype(BF16)
    normed_b = mm(pick_in_b, normed, NT).astype(BF16)
    gated_b = mm(pick_out_b, gated_low, NT).astype(BF16)
    middle = WIDTH // 2
    gate_rows, out_rows_grad = reduce_scatter(
        [mm(normed_a[middle:, :TOKENS], d_gate), mm(gated_b[middle:], cot)],
        [mm(normed_a[:middle, :TOKENS], d_gate), mm(gated_b[:middle], cot)],
        [order_a, order_b],
    )

    ends = jnp.stack([between(k + 1, CHUNKS) * leaving + back[k] for k in range(CHUNKS)])
    du = du_chunk + flat(jnp.einsum("ktn,krn->ktr", b_proj, ends, precision=PRECISE)) * to_end_wide
    d_b = flat(db_chunk + jnp.einsum("ktr,krn->ktn", chunked(u_wide), ends, precision=PRECISE))
    d_c = flat(dc_chunk + jnp.einsum("ktr,krn->ktn", dy_start, starts, precision=PRECISE))
    d_bc = jnp.concatenate([d_b, d_c], axis=1)
    nexts = jnp.concatenate([starts[1:], state_end[None]], axis=0)
    carries = exact(jnp.sum(ends * nexts, axis=2), spread, NT)
    d_cl = chunked(exact(dy_low * y_ssd - u_low * du, spread, NT))
    d_log_decay = flat(jnp.einsum("kts,kth->ksh", below, d_cl, precision=PRECISE) + carries[:, None])
    d_dt = exact(head_x * du, spread, NT) + d_log_decay * decay_rate
    d_dt_raw = jnp.where(real, d_dt * sigmoid(dt_in), 0.0)
    d_head = jnp.stack(
        [
            jnp.sum(d_log_decay * log_decay, axis=0),
            jnp.sum(d_dt_raw, axis=0),
            exact(jnp.sum(dy * head_x, axis=0, keepdims=True), spread, NT)[0],
        ]
    )
    d_x = exact(dt, spread) * du + skip_wide * dy
    d_act = jnp.concatenate([d_x, d_bc], axis=1)
    d_pre = d_act * (gate_of_act * (1.0 + preact * (1.0 - gate_of_act)))
    d_ext = sum(
        conv_weights[k] * jnp.pad(d_pre, ((5 + k, 3 - k), (0, 0))) for k in range(KERNEL)
    )
    d_conv = jnp.where(iota((8, ACT), 0) == KERNEL, jnp.sum(d_pre, axis=0)[None], 0.0)
    for k in range(KERNEL):
        tap = jnp.sum(d_pre * ext[5 + k : 5 + k + TOKENS], axis=0)
        d_conv = jnp.where(iota((8, ACT), 0) == k, tap[None], d_conv)
    d_ext = jnp.concatenate([d_ext[8:], jnp.zeros((8, ACT), F32), d_ext[:8]], axis=0)
    d_crit = jnp.concatenate(
        [d_ext, jnp.pad(d_dt_raw, ((0, HALO), (0, 0)))], axis=1
    ).astype(BF16)

    y_of, x_of, z_of = block_order(order_b)
    row_at = rows_of((y_of * 4 + x_of) * 4 + z_of)[:, None]
    device_of, slot_of = row_at // 12, row_at % 12
    conv_x = d_conv[:, :HALF]
    conv_full = jnp.concatenate(
        [ordered(first_core, conv_x, jnp.zeros_like(conv_x), axis=1), d_conv[:, HALF:]], axis=1
    )
    slot_pick = (slot_of == iota((1536, 8), 1)).astype(F32)
    conv_cols = iota((1536, CONV), 1)
    conv_spread = jnp.where(conv_cols // 26 == device_of, exact(slot_pick, conv_full), 0.0)
    fold = (iota((CONV, LANES), 0) % 26 + HALF_HEADS == iota((CONV, LANES), 1)).astype(BF16)
    gain_at = WIDTH + core * HALF + iota((1536, HALF), 1)
    gain_spread = jnp.where((gain_at // 36 == device_of) & (slot_of == 5), d_gate_gain[None, :], 0.0)
    gain_fold = (
        (WIDTH + core * HALF + iota((HALF, LANES), 0)) % 36 + HALF_HEADS == iota((HALF, LANES), 1)
    ).astype(BF16)
    riders = mm(conv_spread, fold) + mm(gain_spread, gain_fold)

    crit_b = jnp.concatenate([d_crit[:, PART:]], axis=1)

    def part_b(rows):
        with_riders = jnp.pad(riders[rows], ((0, 0), (CRIT - PART - LANES, 0)))
        return mm(normed_b[rows], crit_b) + with_riders

    rows_a, rows_b = reduce_scatter(
        [mm(normed_a[middle:], d_crit[:, :PART]), part_b(slice(middle, None))],
        [mm(normed_a[:middle], d_crit[:, :PART]), part_b(slice(0, middle))],
        [order_a, order_b],
    )
    head_own = sum_all_chips(jnp.pad(d_head, ((0, 5), (0, 0))))
    head_other = swap_cores(head_own)

    d_normed = mm(d_crit, w_crit, NT)
    d_halo = along_y(d_normed[TOKENS:], -1)
    d_normed = d_normed[:TOKENS] + mm(d_gate, w_gate, NT)
    d_normed = jnp.concatenate(
        [d_normed[: TOKENS - HALO], d_normed[TOKENS - HALO :] + d_halo], axis=0
    )
    kept, other = own_rows(d_normed)
    d_own = kept + swap_cores(other)
    own = own_in.astype(F32)
    own_inv = lax.rsqrt(jnp.mean(own * own, axis=1, keepdims=True) + NORM_EPS)
    d_own = d_own * norm_gain
    d_tokens = own_inv * d_own - (own_inv * own_inv * own_inv) * own * jnp.mean(
        own * d_own, axis=1, keepdims=True
    )
    input_grad = to_owner(own_cot.astype(F32) + d_tokens)

    rows = jnp.concatenate([rows_a, rows_b, gate_rows], axis=1)
    mine = jnp.where(first_core, rows[:12], rows[12:])
    theirs = jnp.where(first_core, rows[12:], rows[:12])
    theirs = swap_cores(theirs)
    h0 = jnp.where(first_core, mine, theirs)
    h1 = jnp.where(first_core, theirs, mine)
    in_share = jnp.concatenate(
        [
            h0[:, CRIT:],
            h1[:, CRIT:],
            h0[:, :HALF],
            h1[:, :HALF],
            h0[:, HALF:ACT] + h1[:, HALF:ACT],
            h0[:, ACT : ACT + HALF_HEADS],
            h1[:, ACT : ACT + HALF_HEADS],
        ],
        axis=1,
    )
    riding = h0[:, ACT + HALF_HEADS : CRIT] + h1[:, ACT + HALF_HEADS : CRIT]
    conv_share = riding[:5, :26]
    out_share = cross_halves(out_rows_grad)
    at_device = ((lax.axis_index("y") * 4 + x_at) * 4 + lax.axis_index("z")) * 2 + core
    w_own = rounded(in_master)
    own_gain = lax.dynamic_slice(norm_gain, (at_device * 12,), (12,))
    gain_rows = jnp.sum(w_own * in_share, axis=1) / own_gain
    thirds = [
        lax.ppermute(gain_rows, ALL, [(3 * d + k, d) for d in range(128) if 3 * d + k < 128])
        for k in range(3)
    ]
    gain_share = jnp.concatenate(thirds) + riding[5, :36]
    head_share = ordered(
        first_core, head_own[:3, :HALF_HEADS], head_other[:3, :HALF_HEADS], axis=1
    )

    in_next = adamw_step(in_master, in_share, in_moment1, in_moment2, MATRIX_RATE, MATRIX_DECAY)
    out_next = adamw_step(
        out_master, out_share, out_moment1, out_moment2, MATRIX_RATE, MATRIX_DECAY
    )
    conv_next = adamw_step(conv_master, conv_share, conv_moment1, conv_moment2, SMALL_RATE, 0.0)
    gain_next = adamw_step(gain_master, gain_share, gain_moment1, gain_moment2, SMALL_RATE, 0.0)
    head_next = adamw_step(head_master, head_share, head_moment1, head_moment2, SMALL_RATE, 0.0)
    return (
        block_out,
        input_grad,
        *in_next,
        *out_next,
        *conv_next,
        *gain_next,
        *head_next,
    )


def solution(mesh):
    fine = Mesh(mesh.devices.reshape(4, 4, 4, 2), ALL)
    tokens = P(("z", "c"), ("y", "x"), None)
    rows = P(ALL, None)
    columns = P(None, ALL)
    flat = P(ALL)
    return jax.shard_map(
        on_device,
        mesh=fine,
        in_specs=(tokens, tokens) + (rows,) * 6 + (columns,) * 3 + (flat,) * 3 + (P(),) * 3,
        out_specs=(tokens, tokens) + (rows,) * 6 + (columns,) * 3 + (flat,) * 3 + (P(),) * 3,
        check_vma=False,
    )
```

```python
import jax
import jax.numpy as jnp
from jax import lax
from jax.sharding import Mesh
from jax.sharding import PartitionSpec as P

WIDTH = 1536
INNER = 3072
STATE = 128
HEADDIM = 64
KERNEL = 4
STEP = 5
HEADS = 48
CONV = 3328
PROJ = 6448

HALF = INNER // 2
HALF_HEADS = HEADS // 2
TOKENS = 512
OWN = TOKENS // 2
HALO = 16
ROWS_IN = TOKENS + HALO
CHUNK = 128
CHUNKS = TOKENS // CHUNK
LANES = 128
ACT = HALF + 2 * STATE
CRIT = ACT + LANES
PART = 1024
ROWS = 24

NORM_EPS = 1e-05
PRECISE = lax.Precision.HIGH
EXACT = lax.Precision.HIGHEST
BETA_ONE = 0.9
BETA_TWO = 0.95
ADAM_EPS = 1e-08
MATRIX_RATE = 0.05
SMALL_RATE = 0.5
MATRIX_DECAY = 0.1
BF16 = jnp.bfloat16
F32 = jnp.float32
CHIPS = ("y", "x", "z")
ALL = ("y", "x", "z", "c")


def mm(a, b, dims=((1,), (0,))):
    return lax.dot_general(
        a.astype(BF16), b.astype(BF16), (dims, ((), ())), preferred_element_type=F32
    )


def exact(a, b, dims=((1,), (0,))):
    return lax.dot_general(a, b, (dims, ((), ())), precision=PRECISE, preferred_element_type=F32)


NT = ((1,), (1,))
TN = ((0,), (0,))


def rounded(v):
    return lax.reduce_precision(v, 8, 7)


def hold(*values):
    return lax.optimization_barrier(values)


def iota(shape, dim):
    return lax.broadcasted_iota(jnp.int32, shape, dim)


def sigmoid(v):
    return 1.0 / (1.0 + jnp.exp(-v))


def spread_matrix():
    return (iota((LANES, HALF), 1) // HEADDIM == iota((LANES, HALF), 0)).astype(F32)


def adamw_step(weight, gradient, moment_one, moment_two, step_rate, weight_decay):
    one_next = BETA_ONE * moment_one + (1.0 - BETA_ONE) * gradient
    two_next = BETA_TWO * moment_two + (1.0 - BETA_TWO) * gradient * gradient
    corrected = one_next / (1.0 - BETA_ONE**STEP)
    scale_next = jnp.sqrt(two_next / (1.0 - BETA_TWO**STEP)) + ADAM_EPS
    weight_next = weight - step_rate * (corrected / scale_next + weight_decay * weight)
    return (one_next, two_next, weight_next)


def swap_cores(value):
    return lax.ppermute(value, "c", [(0, 1), (1, 0)])


def regroup(value, turn):
    pairs = [
        (x * 2 + c, (2 * c + (x + turn) % 2) * 2 + x // 2) for x in range(4) for c in range(2)
    ]
    return lax.ppermute(value, ("x", "c"), pairs)


def cross_halves(value):
    pairs = []
    for y in range(4):
        for c in range(2):
            to = (y, c) if y // 2 == c else (y ^ 2, 1 - c)
            pairs.append((y * 2 + c, to[0] * 2 + to[1]))
    return lax.ppermute(value, ("y", "c"), pairs)


def along_y(value, steps):
    return lax.ppermute(value, "y", [(y, y + steps) for y in range(4) if 0 <= y + steps < 4])


def partner(axis, turn):
    pairs = []
    for i in range(4):
        for c in range(2):
            pairs.append((i * 2 + c, (i ^ (1 if (turn + c) % 2 == 0 else 3)) * 2 + c))
    return (axis, "c"), pairs


def exchange(value, axis, turn):
    axes, pairs = partner(axis, turn)
    return lax.ppermute(value, axes, pairs)


def block_order(order):
    first = jnp.where(lax.axis_index("c") == 0, 1, 3)
    second = 4 - first
    block = jnp.arange(64)
    place = {a: lax.axis_index(a) for a in CHIPS}
    for at, axis in enumerate(order):
        high = (block >> (5 - 2 * at)) & 1
        low = (block >> (4 - 2 * at)) & 1
        place[axis] = place[axis] ^ (high * first) ^ (low * second)
    return [place[a] + jnp.zeros((64,), jnp.int32) for a in CHIPS]


def rows_of(blocks):
    return (blocks[:, None] * ROWS + jnp.arange(ROWS)[None, :]).reshape(-1)


def in_rows(order):
    y, x, z = block_order(order)
    return rows_of((y * 4 + x) * 4 + z)


def out_rows(order):
    y, x, z = block_order(order)
    return rows_of((((y % 2) * 4 + x) * 4 + z) * 2 + y // 2)


def pick(rows):
    return (rows[:, None] == iota((1536, 1536), 1)).astype(BF16)


class Halving:
    def __init__(self, sends, keeps, orders):
        self.sends = [v.astype(BF16) for v in sends]
        self.keeps, self.orders, self.step = keeps, orders, 0
        self.start()

    def start(self):
        self.arrived = [
            exchange(v, order[self.step // 2], self.step % 2)
            for v, order in zip(self.sends, self.orders)
        ]

    def add(self):
        totals = [keep + got.astype(F32) for keep, got in zip(self.keeps, self.arrived)]
        self.step += 1
        if self.step == 6:
            self.totals = totals
            return
        half = totals[0].shape[0] // 2
        self.sends = [t[half:].astype(BF16) for t in totals]
        self.keeps = [t[:half] for t in totals]
        self.start()


def wait(halvings, *values):
    held = [h.arrived for h in halvings], [h.keeps for h in halvings], values
    arrived, keeps, values = lax.optimization_barrier(held)
    for h, a, k in zip(halvings, arrived, keeps):
        h.arrived, h.keeps = a, k
        h.add()
    return values


PAIRS = HALF_HEADS // 2


def product(terms, a, b):
    return jnp.einsum(terms, a, b, preferred_element_type=F32)


def by_pair(value):
    return value.reshape(CHUNKS, CHUNK, PAIRS, LANES).transpose(0, 2, 1, 3)


def from_pairs(value):
    return value.transpose(0, 2, 1, 3).reshape(TOKENS, HALF)


def one_head(value):
    left = iota((2, 1, LANES), 2) // HEADDIM == iota((2, 1, LANES), 0)
    return jnp.where(left, value[:, :, None], jnp.zeros((), value.dtype))


def decays(cl):
    heads = cl[:, :HALF_HEADS].reshape(CHUNKS, CHUNK, PAIRS, 2).transpose(0, 2, 3, 1)
    causal = iota((CHUNK, CHUNK), 0) >= iota((CHUNK, CHUNK), 1)
    differ = jnp.where(causal, heads[..., :, None] - heads[..., None, :], 0.0)
    return jnp.where(causal, jnp.exp(differ), 0.0)


def pack_state(state, decay):
    high = rounded(decay)
    middle = rounded(decay - high)
    low = rounded(decay - high - middle)
    at = iota((16, LANES), 0)
    rows = jnp.where(at == 0, high, jnp.where(at == 1, middle, 0.0))
    rows = jnp.where(at == 2, low, rows)
    return jnp.concatenate([state, rows], axis=0).astype(BF16)


def unpack_state(packed):
    rows = packed[HALF : HALF + 3].astype(F32)
    return packed[:HALF].astype(F32), rows[0] + rows[1] + rows[2]


def per_row(head_values):
    heads = head_values[..., :HALF_HEADS, None]
    wide = jnp.broadcast_to(heads, heads.shape[:-1] + (HEADDIM,))
    return wide.reshape(head_values.shape[:-1] + (HALF, 1))


def combine(packed, way, unpack):
    near, far, farthest = [unpack(along_y(packed, way * k)) for k in (1, 2, 3)]
    return near[0] + per_row(near[1]) * (far[0] + per_row(far[1]) * farthest[0])


def pack_full(state, decay):
    return jnp.concatenate([state, jnp.broadcast_to(decay[None], (8, LANES))], axis=0)


def unpack_full(packed):
    return packed[:HALF], packed[HALF]


def chunked(value):
    return value.reshape(CHUNKS, CHUNK, value.shape[-1])


def flat(value):
    return value.reshape(TOKENS, value.shape[-1])


def sum_all_chips(value):
    for axis in CHIPS:
        for turn in range(2):
            value = value + exchange(value, axis, turn)
    return value


def on_device(
    block_in,
    cotangent,
    in_master,
    in_moment1,
    in_moment2,
    out_master,
    out_moment1,
    out_moment2,
    conv_master,
    conv_moment1,
    conv_moment2,
    gain_master,
    gain_moment1,
    gain_moment2,
    head_master,
    head_moment1,
    head_moment2,
):
    core = lax.axis_index("c")
    x_at = lax.axis_index("x")
    first_core = core == 0
    even_x = x_at % 2 == 0

    def ordered(flag, mine, other, axis=0):
        return jnp.where(
            flag, jnp.concatenate([mine, other], axis=axis), jnp.concatenate([other, mine], axis=axis)
        )

    riders_out = jnp.concatenate(
        [
            jnp.pad(conv_master, ((0, 0), (0, LANES - HALF_HEADS - 26))),
            jnp.pad(gain_master[None], ((0, 6), (0, LANES - HALF_HEADS - 36))),
        ],
        axis=0,
    )

    def half_columns(c):
        return jnp.concatenate(
            [
                in_master[:, INNER + c * HALF : INNER + (c + 1) * HALF],
                in_master[:, 2 * INNER : INNER + CONV],
                in_master[:, INNER + CONV + c * HALF_HEADS : INNER + CONV + (c + 1) * HALF_HEADS],
                riders_out,
                in_master[:, c * HALF : (c + 1) * HALF],
            ],
            axis=1,
        )

    halves = [half_columns(0), half_columns(1)]
    mine = jnp.where(first_core, halves[0], halves[1])
    theirs = jnp.where(first_core, halves[1], halves[0])
    in_rows_low = ordered(first_core, mine, swap_cores(theirs)).astype(BF16)
    out_rows_low = cross_halves(out_master).astype(BF16)
    w_crit = lax.all_gather(in_rows_low[:, :CRIT], CHIPS, axis=0, tiled=True)
    rest_low = jnp.concatenate([in_rows_low[:, CRIT:], out_rows_low], axis=1)
    rest_low, w_crit = hold(rest_low, w_crit)
    w_rest = lax.all_gather(rest_low, CHIPS, axis=0, tiled=True)
    w_gate = w_rest[:, :HALF]
    w_out = (
        w_rest[:, HALF:]
        .reshape(2, 2, 16, ROWS, WIDTH)
        .transpose(1, 2, 0, 3, 4)
        .reshape(HALF, WIDTH)
    )
    smalls = w_crit[:, ACT:]
    device_at, slot_at = iota((1536, 1), 0) // 12, iota((1536, 1), 0) % 12

    def gather_small(columns, width, slots):
        unfold = (HALF_HEADS + columns % width == iota((LANES, columns.shape[1]), 0)).astype(BF16)
        wide = jnp.where(device_at == columns // width, mm(smalls, unfold), 0.0)
        return mm((slot_at == slots).astype(BF16), wide, TN)

    norm_gain = gather_small(iota((1, WIDTH), 1), 36, 5 + iota((1, 8), 1))[0]
    gate_gain = gather_small(WIDTH + core * HALF + iota((1, HALF), 1), 36, 5 + iota((1, 8), 1))[0]
    conv_at = iota((1, ACT), 1)
    conv_at = jnp.where(conv_at < HALF, core * HALF + conv_at, INNER - HALF + conv_at)
    conv_weights = gather_small(conv_at, 26, iota((1, 8), 1))
    head_half = jnp.pad(
        lax.dynamic_slice(head_master, (0, core * HALF_HEADS), (3, HALF_HEADS)),
        ((0, 0), (0, LANES - HALF_HEADS)),
    )
    decay_rate = -jnp.exp(head_half[0])

    both = jnp.stack([block_in, cotangent], axis=1)
    flipped = both[::-1]
    got = [regroup(jnp.where(even_x, both, flipped)[k], k) for k in range(2)]
    own_both = ordered(even_x, got[0], got[1], axis=1)
    all_both = ordered(first_core, own_both, swap_cores(own_both), axis=1)
    own_in, own_cot = own_both[0], own_both[1]
    tokens, cot = all_both[0], all_both[1]
    halo = along_y(tokens[TOKENS - HALO :], 1)
    extended = jnp.concatenate([tokens, halo], axis=0).astype(F32)
    inv = lax.rsqrt(jnp.mean(extended * extended, axis=1, keepdims=True) + NORM_EPS)
    normed = (extended * inv * norm_gain).astype(BF16)

    crit = mm(normed, w_crit)
    ext = jnp.concatenate([crit[TOKENS + 8 :, :ACT], crit[:TOKENS, :ACT]], axis=0)
    preact = conv_weights[KERNEL] + sum(
        conv_weights[k] * ext[5 + k : 5 + k + TOKENS] for k in range(KERNEL)
    )
    gate_of_act = sigmoid(preact)
    act = preact * gate_of_act
    head_x = act[:, :HALF]
    bc = act[:, HALF:]
    dt_in = crit[:TOKENS, ACT:] + head_half[1]
    real = iota((1, LANES), 1) < HALF_HEADS
    dt = jnp.where(real, jax.nn.softplus(dt_in), 0.0)
    log_decay = dt * decay_rate
    below = (iota((CHUNK, CHUNK), 0) >= iota((CHUNK, CHUNK), 1)).astype(F32)
    below = jnp.broadcast_to(below[None], (CHUNKS, CHUNK, CHUNK))
    cl = jnp.einsum("kts,ksh->kth", below, chunked(log_decay), precision=EXACT)
    spread = spread_matrix()
    u = head_x * exact(dt, spread)
    u_low = rounded(u)
    lasts = cl[:, -1]
    to_end = flat(jnp.exp(lasts[:, None] - cl))
    cl = flat(cl)
    to_end_wide = exact(to_end, spread)
    from_start_wide = exact(jnp.exp(cl), spread)
    u_wide = u * to_end_wide
    b_proj, c_proj = chunked(bc[:, :STATE]), chunked(bc[:, STATE:])
    b_low, c_low = b_proj.astype(BF16), c_proj.astype(BF16)
    own = jnp.einsum("ktr,ktn->krn", chunked(u_wide), b_proj, precision=PRECISE)
    def between(i, j):
        return per_row(jnp.exp(sum(lasts[i:j])) if j > i else jnp.ones((LANES,), F32))

    local = [jnp.zeros_like(own[0])]
    for k in range(CHUNKS):
        local.append(sum(between(i + 1, k + 1) * own[i] for i in range(k + 1)))
    piece_decay = jnp.exp(jnp.sum(lasts, axis=0))
    incoming = combine(pack_full(local[CHUNKS], piece_decay), 1, unpack_full)
    decay = decays(cl)
    scores = jnp.einsum("ktn,ksn->kts", c_proj, b_proj, precision=PRECISE)
    mixes = (scores[:, None, None] * decay).astype(BF16)
    u_pairs = one_head(by_pair(u_low.astype(BF16)))
    y_chunk = from_pairs(product("kpjts,kpjsc->kptc", mixes, u_pairs))

    starts = jnp.stack([between(0, k) * incoming + local[k] for k in range(CHUNKS)])
    state_end = between(0, CHUNKS) * incoming + local[CHUNKS]
    y_state = flat(jnp.einsum("ktn,krn->ktr", c_proj, starts, precision=PRECISE)) * from_start_wide
    y_ssd = y_chunk + y_state
    skip_wide = exact(head_half[2:3], spread)
    mixed = y_ssd + skip_wide * head_x

    gate = mm(normed[:TOKENS], w_gate)
    gate_sig = sigmoid(gate)
    gate_silu = gate * gate_sig
    d_gated = mm(cot, w_out, NT)
    g = mixed * gate_silu
    e = d_gated * gate_gain
    sums = jnp.concatenate(
        [jnp.sum(g * g, axis=1, keepdims=True), jnp.sum(e * g, axis=1, keepdims=True)], axis=1
    )
    sums = (sums + swap_cores(sums)) / INNER
    r = lax.rsqrt(sums[:, :1] + NORM_EPS)
    gated_low = (g * r * gate_gain).astype(BF16)
    d_g = r * e - (r * r * r) * g * sums[:, 1:]
    d_gate_gain = jnp.sum(d_gated * g * r, axis=0)
    dy = d_g * gate_silu
    d_gate = (d_g * mixed * (gate_sig * (1.0 + gate * (1.0 - gate_sig)))).astype(BF16)
    dy_low = rounded(dy)

    dy_start = chunked(dy * from_start_wide)
    chunk_backs = jnp.einsum("ktr,ktn->krn", dy_start, c_proj, precision=PRECISE)
    back = [None] * CHUNKS
    for k in range(CHUNKS):
        back[k] = sum((between(k + 1, i) * chunk_backs[i] for i in range(k + 1, CHUNKS)), jnp.zeros_like(own[0]))
    to_before = sum(between(0, i) * chunk_backs[i] for i in range(CHUNKS))
    leaving = combine(pack_state(to_before, piece_decay), -1, unpack_state)
    def own_rows(value):
        return jnp.where(first_core, value[:OWN], value[OWN:]), jnp.where(
            first_core, value[OWN:], value[:OWN]
        )

    def to_owner(value):
        low, high = value[:CHUNK], value[CHUNK:]
        sent = [jnp.where(even_x, low, high), jnp.where(even_x, high, low)]
        back0, back1 = regroup(sent[0], 0), regroup(sent[1], 1)
        return jnp.where(even_x, jnp.stack([back0, back1]), jnp.stack([back1, back0]))

    order_a, order_b = ("y", "x", "z"), ("x", "y", "z")
    pick_in_a, pick_in_b = pick(in_rows(order_a)), pick(in_rows(order_b))
    pick_out_b = pick(out_rows(order_b))
    normed_a = mm(pick_in_a, normed, NT).astype(BF16)
    normed_b = mm(pick_in_b, normed, NT).astype(BF16)
    gated_b = mm(pick_out_b, gated_low, NT).astype(BF16)
    middle = WIDTH // 2
    first = Halving(
        [mm(normed_a[middle:, :TOKENS], d_gate), mm(gated_b[middle:], cot)],
        [mm(normed_a[:middle, :TOKENS], d_gate), mm(gated_b[:middle], cot)],
        [order_a, order_b],
    )

    dy_pairs = by_pair(dy_low.astype(BF16))
    du_chunk = from_pairs(product("kpjts,kpjtc->kpsc", mixes, one_head(dy_pairs)))
    both = product("kptc,kpjsc->kpjts", dy_pairs, u_pairs)
    d_scores = jnp.sum(decay * both, axis=(1, 2)).astype(BF16)
    db_chunk = product("kts,ktn->ksn", d_scores, c_low)
    dc_chunk = product("kts,ksn->ktn", d_scores, b_low)

    part_out = mm(gated_low, w_out)
    kept, other = own_rows(part_out)
    own_out = own_in.astype(F32) + (kept + swap_cores(other))
    block_out = to_owner(own_out.astype(BF16))

    leaving, du_chunk, db_chunk, dc_chunk = wait([first], leaving, du_chunk, db_chunk, dc_chunk)

    ends = jnp.stack([between(k + 1, CHUNKS) * leaving + back[k] for k in range(CHUNKS)])
    du = du_chunk + flat(jnp.einsum("ktn,krn->ktr", b_proj, ends, precision=PRECISE)) * to_end_wide
    d_b = flat(db_chunk + jnp.einsum("ktr,krn->ktn", chunked(u_wide), ends, precision=PRECISE))
    d_c = flat(dc_chunk + jnp.einsum("ktr,krn->ktn", dy_start, starts, precision=PRECISE))
    du, d_b, d_c = wait([first], du, d_b, d_c)
    d_bc = jnp.concatenate([d_b, d_c], axis=1)
    nexts = jnp.concatenate([starts[1:], state_end[None]], axis=0)
    carries = exact(jnp.sum(ends * nexts, axis=2), spread, NT)
    d_cl = chunked(exact(dy_low * y_ssd - u_low * du, spread, NT))
    d_log_decay = flat(jnp.einsum("kts,kth->ksh", below, d_cl, precision=PRECISE) + carries[:, None])
    d_dt = exact(head_x * du, spread, NT) + d_log_decay * decay_rate
    d_dt_raw = jnp.where(real, d_dt * sigmoid(dt_in), 0.0)
    d_head = jnp.stack(
        [
            jnp.sum(d_log_decay * log_decay, axis=0),
            jnp.sum(d_dt_raw, axis=0),
            exact(jnp.sum(dy * head_x, axis=0, keepdims=True), spread, NT)[0],
        ]
    )
    d_x = exact(dt, spread) * du + skip_wide * dy
    d_act = jnp.concatenate([d_x, d_bc], axis=1)
    d_pre = d_act * (gate_of_act * (1.0 + preact * (1.0 - gate_of_act)))
    (d_pre,) = wait([first], d_pre)
    d_ext = sum(
        conv_weights[k] * jnp.pad(d_pre, ((5 + k, 3 - k), (0, 0))) for k in range(KERNEL)
    )
    d_conv = jnp.where(iota((8, ACT), 0) == KERNEL, jnp.sum(d_pre, axis=0)[None], 0.0)
    for k in range(KERNEL):
        tap = jnp.sum(d_pre * ext[5 + k : 5 + k + TOKENS], axis=0)
        d_conv = jnp.where(iota((8, ACT), 0) == k, tap[None], d_conv)
    d_ext = jnp.concatenate([d_ext[8:], jnp.zeros((8, ACT), F32), d_ext[:8]], axis=0)
    d_crit = jnp.concatenate(
        [d_ext, jnp.pad(d_dt_raw, ((0, HALO), (0, 0)))], axis=1
    ).astype(BF16)
    (d_crit,) = wait([first], d_crit)

    y_of, x_of, z_of = block_order(order_b)
    row_at = rows_of((y_of * 4 + x_of) * 4 + z_of)[:, None]
    device_of, slot_of = row_at // 12, row_at % 12
    conv_x = d_conv[:, :HALF]
    conv_full = jnp.concatenate(
        [ordered(first_core, conv_x, jnp.zeros_like(conv_x), axis=1), d_conv[:, HALF:]], axis=1
    )
    slot_pick = (slot_of == iota((1536, 8), 1)).astype(F32)
    conv_cols = iota((1536, CONV), 1)
    conv_spread = jnp.where(conv_cols // 26 == device_of, exact(slot_pick, conv_full), 0.0)
    fold = (iota((CONV, LANES), 0) % 26 + HALF_HEADS == iota((CONV, LANES), 1)).astype(BF16)
    gain_at = WIDTH + core * HALF + iota((1536, HALF), 1)
    gain_spread = jnp.where((gain_at // 36 == device_of) & (slot_of == 5), d_gate_gain[None, :], 0.0)
    gain_fold = (
        (WIDTH + core * HALF + iota((HALF, LANES), 0)) % 36 + HALF_HEADS == iota((HALF, LANES), 1)
    ).astype(BF16)
    riders = mm(conv_spread, fold) + mm(gain_spread, gain_fold)

    crit_b = jnp.concatenate([d_crit[:, PART:]], axis=1)

    def part_b(rows):
        with_riders = jnp.pad(riders[rows], ((0, 0), (CRIT - PART - LANES, 0)))
        return mm(normed_b[rows], crit_b) + with_riders

    second = Halving(
        [mm(normed_a[middle:], d_crit[:, :PART]), part_b(slice(middle, None))],
        [mm(normed_a[:middle], d_crit[:, :PART]), part_b(slice(0, middle))],
        [order_a, order_b],
    )
    head_own = sum_all_chips(jnp.pad(d_head, ((0, 5), (0, 0))))
    head_other = swap_cores(head_own)

    d_normed = mm(d_crit, w_crit, NT)
    d_halo = along_y(d_normed[TOKENS:], -1)
    d_normed = d_normed[:TOKENS] + mm(d_gate, w_gate, NT)
    d_normed = jnp.concatenate(
        [d_normed[: TOKENS - HALO], d_normed[TOKENS - HALO :] + d_halo], axis=0
    )
    kept, other = own_rows(d_normed)
    d_own = kept + swap_cores(other)
    own = own_in.astype(F32)
    own_inv = lax.rsqrt(jnp.mean(own * own, axis=1, keepdims=True) + NORM_EPS)
    d_own = d_own * norm_gain
    d_tokens = own_inv * d_own - (own_inv * own_inv * own_inv) * own * jnp.mean(
        own * d_own, axis=1, keepdims=True
    )
    input_grad = to_owner(own_cot.astype(F32) + d_tokens)

    wait([second, first])
    wait([second, first])
    for _ in range(4):
        wait([second])
    rows_a, rows_b = second.totals
    gate_rows, out_rows_grad = first.totals

    rows = jnp.concatenate([rows_a, rows_b, gate_rows], axis=1)
    mine = jnp.where(first_core, rows[:12], rows[12:])
    theirs = jnp.where(first_core, rows[12:], rows[:12])
    theirs = swap_cores(theirs)
    h0 = jnp.where(first_core, mine, theirs)
    h1 = jnp.where(first_core, theirs, mine)
    in_share = jnp.concatenate(
        [
            h0[:, CRIT:],
            h1[:, CRIT:],
            h0[:, :HALF],
            h1[:, :HALF],
            h0[:, HALF:ACT] + h1[:, HALF:ACT],
            h0[:, ACT : ACT + HALF_HEADS],
            h1[:, ACT : ACT + HALF_HEADS],
        ],
        axis=1,
    )
    riding = h0[:, ACT + HALF_HEADS : CRIT] + h1[:, ACT + HALF_HEADS : CRIT]
    conv_share = riding[:5, :26]
    out_share = cross_halves(out_rows_grad)
    at_device = ((lax.axis_index("y") * 4 + x_at) * 4 + lax.axis_index("z")) * 2 + core
    w_own = rounded(in_master)
    own_gain = lax.dynamic_slice(norm_gain, (at_device * 12,), (12,))
    gain_rows = jnp.sum(w_own * in_share, axis=1) / own_gain
    thirds = [
        lax.ppermute(gain_rows, ALL, [(3 * d + k, d) for d in range(128) if 3 * d + k < 128])
        for k in range(3)
    ]
    gain_share = jnp.concatenate(thirds) + riding[5, :36]
    head_share = ordered(
        first_core, head_own[:3, :HALF_HEADS], head_other[:3, :HALF_HEADS], axis=1
    )

    in_next = adamw_step(in_master, in_share, in_moment1, in_moment2, MATRIX_RATE, MATRIX_DECAY)
    out_next = adamw_step(
        out_master, out_share, out_moment1, out_moment2, MATRIX_RATE, MATRIX_DECAY
    )
    conv_next = adamw_step(conv_master, conv_share, conv_moment1, conv_moment2, SMALL_RATE, 0.0)
    gain_next = adamw_step(gain_master, gain_share, gain_moment1, gain_moment2, SMALL_RATE, 0.0)
    head_next = adamw_step(head_master, head_share, head_moment1, head_moment2, SMALL_RATE, 0.0)
    return (
        block_out,
        input_grad,
        *in_next,
        *out_next,
        *conv_next,
        *gain_next,
        *head_next,
    )


def solution(mesh):
    fine = Mesh(mesh.devices.reshape(4, 4, 4, 2), ALL)
    tokens = P(("z", "c"), ("y", "x"), None)
    rows = P(ALL, None)
    columns = P(None, ALL)
    flat = P(ALL)
    return jax.shard_map(
        on_device,
        mesh=fine,
        in_specs=(tokens, tokens) + (rows,) * 6 + (columns,) * 3 + (flat,) * 3 + (P(),) * 3,
        out_specs=(tokens, tokens) + (rows,) * 6 + (columns,) * 3 + (flat,) * 3 + (P(),) * 3,
        check_vma=False,
    )
```

```python
import jax
import jax.numpy as jnp
from jax import lax
from jax.sharding import Mesh
from jax.sharding import PartitionSpec as P

WIDTH = 1536
INNER = 3072
STATE = 128
HEADDIM = 64
KERNEL = 4
STEP = 5
HEADS = 48
CONV = 3328
PROJ = 6448

HALF = INNER // 2
HALF_HEADS = HEADS // 2
TOKENS = 512
OWN = TOKENS // 2
HALO = 16
ROWS_IN = TOKENS + HALO
CHUNK = 128
CHUNKS = TOKENS // CHUNK
LANES = 128
ACT = HALF + 2 * STATE
CRIT = ACT + LANES
PART = 1024
ROWS = 24

NORM_EPS = 1e-05
PRECISE = lax.Precision.HIGH
EXACT = lax.Precision.HIGHEST
BETA_ONE = 0.9
BETA_TWO = 0.95
ADAM_EPS = 1e-08
MATRIX_RATE = 0.05
SMALL_RATE = 0.5
MATRIX_DECAY = 0.1
BF16 = jnp.bfloat16
F32 = jnp.float32
CHIPS = ("y", "x", "z")
ALL = ("y", "x", "z", "c")


def mm(a, b, dims=((1,), (0,))):
    return lax.dot_general(
        a.astype(BF16), b.astype(BF16), (dims, ((), ())), preferred_element_type=F32
    )


def exact(a, b, dims=((1,), (0,))):
    return lax.dot_general(a, b, (dims, ((), ())), precision=PRECISE, preferred_element_type=F32)


NT = ((1,), (1,))
TN = ((0,), (0,))


def rounded(v):
    return lax.reduce_precision(v, 8, 7)


def iota(shape, dim):
    return lax.broadcasted_iota(jnp.int32, shape, dim)


def sigmoid(v):
    return 1.0 / (1.0 + jnp.exp(-v))


def spread_matrix():
    return (iota((LANES, HALF), 1) // HEADDIM == iota((LANES, HALF), 0)).astype(F32)


def adamw_step(weight, gradient, moment_one, moment_two, step_rate, weight_decay):
    one_next = BETA_ONE * moment_one + (1.0 - BETA_ONE) * gradient
    two_next = BETA_TWO * moment_two + (1.0 - BETA_TWO) * gradient * gradient
    corrected = one_next / (1.0 - BETA_ONE**STEP)
    scale_next = jnp.sqrt(two_next / (1.0 - BETA_TWO**STEP)) + ADAM_EPS
    weight_next = weight - step_rate * (corrected / scale_next + weight_decay * weight)
    return (one_next, two_next, weight_next)


def swap_cores(value):
    return lax.ppermute(value, "c", [(0, 1), (1, 0)])


def regroup(value, turn):
    pairs = [
        (x * 2 + c, (2 * c + (x + turn) % 2) * 2 + x // 2) for x in range(4) for c in range(2)
    ]
    return lax.ppermute(value, ("x", "c"), pairs)


def cross_halves(value):
    pairs = []
    for y in range(4):
        for c in range(2):
            to = (y, c) if y // 2 == c else (y ^ 2, 1 - c)
            pairs.append((y * 2 + c, to[0] * 2 + to[1]))
    return lax.ppermute(value, ("y", "c"), pairs)


def along_y(value, steps):
    return lax.ppermute(value, "y", [(y, y + steps) for y in range(4) if 0 <= y + steps < 4])


def partner(axis, turn):
    pairs = []
    for i in range(4):
        for c in range(2):
            pairs.append((i * 2 + c, (i ^ (1 if (turn + c) % 2 == 0 else 3)) * 2 + c))
    return (axis, "c"), pairs


def exchange(value, axis, turn):
    axes, pairs = partner(axis, turn)
    return lax.ppermute(value, axes, pairs)


def block_order(order):
    first = jnp.where(lax.axis_index("c") == 0, 1, 3)
    second = 4 - first
    block = jnp.arange(64)
    place = {a: lax.axis_index(a) for a in CHIPS}
    for at, axis in enumerate(order):
        high = (block >> (5 - 2 * at)) & 1
        low = (block >> (4 - 2 * at)) & 1
        place[axis] = place[axis] ^ (high * first) ^ (low * second)
    return [place[a] + jnp.zeros((64,), jnp.int32) for a in CHIPS]


def rows_of(blocks):
    return (blocks[:, None] * ROWS + jnp.arange(ROWS)[None, :]).reshape(-1)


def in_rows(order):
    y, x, z = block_order(order)
    return rows_of((y * 4 + x) * 4 + z)


def out_rows(order):
    y, x, z = block_order(order)
    return rows_of((((y % 2) * 4 + x) * 4 + z) * 2 + y // 2)


def pick(rows):
    return (rows[:, None] == iota((1536, 1536), 1)).astype(BF16)


class Halving:
    def __init__(self, sends, keeps, orders):
        self.sends = [v.astype(BF16) for v in sends]
        self.keeps, self.orders, self.step = keeps, orders, 0
        self.start()

    def start(self):
        self.arrived = [
            exchange(v, order[self.step // 2], self.step % 2)
            for v, order in zip(self.sends, self.orders)
        ]

    def add(self):
        totals = [keep + got.astype(F32) for keep, got in zip(self.keeps, self.arrived)]
        self.step += 1
        if self.step == 6:
            self.totals = totals
            return
        half = totals[0].shape[0] // 2
        self.sends = [t[half:].astype(BF16) for t in totals]
        self.keeps = [t[:half] for t in totals]
        self.start()


def wait(halvings, *values):
    held = [h.arrived for h in halvings], [h.keeps for h in halvings], values
    arrived, keeps, values = lax.optimization_barrier(held)
    for h, a, k in zip(halvings, arrived, keeps):
        h.arrived, h.keeps = a, k
        h.add()
    return values


PAIRS = HALF_HEADS // 2


def product(terms, a, b):
    return jnp.einsum(terms, a, b, preferred_element_type=F32)


def by_pair(value):
    return value.reshape(CHUNKS, CHUNK, PAIRS, LANES).transpose(0, 2, 1, 3)


def from_pairs(value):
    return value.transpose(0, 2, 1, 3).reshape(TOKENS, HALF)


def one_head(value):
    left = iota((2, 1, LANES), 2) // HEADDIM == iota((2, 1, LANES), 0)
    return jnp.where(left, value[:, :, None], jnp.zeros((), value.dtype))


def decays(cl):
    heads = cl[:, :HALF_HEADS].reshape(CHUNKS, CHUNK, PAIRS, 2).transpose(0, 2, 3, 1)
    causal = iota((CHUNK, CHUNK), 0) >= iota((CHUNK, CHUNK), 1)
    differ = jnp.where(causal, heads[..., :, None] - heads[..., None, :], 0.0)
    return jnp.where(causal, jnp.exp(differ), 0.0)


def pack_state(state, decay):
    high = rounded(decay)
    middle = rounded(decay - high)
    low = rounded(decay - high - middle)
    at = iota((16, LANES), 0)
    rows = jnp.where(at == 0, high, jnp.where(at == 1, middle, 0.0))
    rows = jnp.where(at == 2, low, rows)
    return jnp.concatenate([state, rows], axis=0).astype(BF16)


def unpack_state(packed):
    rows = packed[HALF : HALF + 3].astype(F32)
    return packed[:HALF].astype(F32), rows[0] + rows[1] + rows[2]


def per_row(head_values):
    heads = head_values[..., :HALF_HEADS, None]
    wide = jnp.broadcast_to(heads, heads.shape[:-1] + (HEADDIM,))
    return wide.reshape(head_values.shape[:-1] + (HALF, 1))


def combine(packed, way, unpack):
    near, far, farthest = [unpack(along_y(packed, way * k)) for k in (1, 2, 3)]
    return near[0] + per_row(near[1]) * (far[0] + per_row(far[1]) * farthest[0])


def pack_full(state, decay):
    return jnp.concatenate([state, jnp.broadcast_to(decay[None], (8, LANES))], axis=0)


def unpack_full(packed):
    return packed[:HALF], packed[HALF]


def chunked(value):
    return value.reshape(CHUNKS, CHUNK, value.shape[-1])


def flat(value):
    return value.reshape(TOKENS, value.shape[-1])


def on_device(
    block_in,
    cotangent,
    in_master,
    in_moment1,
    in_moment2,
    out_master,
    out_moment1,
    out_moment2,
    conv_master,
    conv_moment1,
    conv_moment2,
    gain_master,
    gain_moment1,
    gain_moment2,
    head_master,
    head_moment1,
    head_moment2,
):
    core = lax.axis_index("c")
    x_at = lax.axis_index("x")
    first_core = core == 0
    even_x = x_at % 2 == 0

    def ordered(flag, mine, other, axis=0):
        return jnp.where(
            flag, jnp.concatenate([mine, other], axis=axis), jnp.concatenate([other, mine], axis=axis)
        )

    riders_out = jnp.concatenate(
        [
            jnp.pad(conv_master, ((0, 0), (0, LANES - HALF_HEADS - 26))),
            jnp.pad(gain_master[None], ((0, 6), (0, LANES - HALF_HEADS - 36))),
        ],
        axis=0,
    )

    def half_columns(c):
        return jnp.concatenate(
            [
                in_master[:, INNER + c * HALF : INNER + (c + 1) * HALF],
                in_master[:, 2 * INNER : INNER + CONV],
                in_master[:, INNER + CONV + c * HALF_HEADS : INNER + CONV + (c + 1) * HALF_HEADS],
                riders_out,
                in_master[:, c * HALF : (c + 1) * HALF],
            ],
            axis=1,
        )

    halves = [half_columns(0), half_columns(1)]
    mine = jnp.where(first_core, halves[0], halves[1])
    theirs = jnp.where(first_core, halves[1], halves[0])
    in_rows_low = ordered(first_core, mine, swap_cores(theirs)).astype(BF16)
    out_rows_low = cross_halves(out_master).astype(BF16)
    w_crit = lax.all_gather(in_rows_low[:, :CRIT], CHIPS, axis=0, tiled=True)
    rest_low = jnp.concatenate([in_rows_low[:, CRIT:], out_rows_low], axis=1)
    w_rest = lax.all_gather(rest_low, CHIPS, axis=0, tiled=True)
    w_gate = w_rest[:, :HALF]
    w_out = (
        w_rest[:, HALF:]
        .reshape(2, 2, 16, ROWS, WIDTH)
        .transpose(1, 2, 0, 3, 4)
        .reshape(HALF, WIDTH)
    )
    smalls = w_crit[:, ACT:]
    device_at, slot_at = iota((1536, 1), 0) // 12, iota((1536, 1), 0) % 12

    def gather_small(columns, width, slots):
        unfold = (HALF_HEADS + columns % width == iota((LANES, columns.shape[1]), 0)).astype(BF16)
        wide = jnp.where(device_at == columns // width, mm(smalls, unfold), 0.0)
        return mm((slot_at == slots).astype(BF16), wide, TN)

    norm_gain = gather_small(iota((1, WIDTH), 1), 36, 5 + iota((1, 8), 1))[0]
    gate_gain = gather_small(WIDTH + core * HALF + iota((1, HALF), 1), 36, 5 + iota((1, 8), 1))[0]
    conv_at = iota((1, ACT), 1)
    conv_at = jnp.where(conv_at < HALF, core * HALF + conv_at, INNER - HALF + conv_at)
    conv_weights = gather_small(conv_at, 26, iota((1, 8), 1))
    head_half = jnp.pad(
        lax.dynamic_slice(head_master, (0, core * HALF_HEADS), (3, HALF_HEADS)),
        ((0, 0), (0, LANES - HALF_HEADS)),
    )
    decay_rate = -jnp.exp(head_half[0])

    both = jnp.stack([block_in, cotangent], axis=1)
    flipped = both[::-1]
    got = [regroup(jnp.where(even_x, both, flipped)[k], k) for k in range(2)]
    own_both = ordered(even_x, got[0], got[1], axis=1)
    all_both = ordered(first_core, own_both, swap_cores(own_both), axis=1)
    own_in, own_cot = own_both[0], own_both[1]
    tokens, cot = all_both[0], all_both[1]
    halo = along_y(tokens[TOKENS - HALO :], 1)
    extended = jnp.concatenate([tokens, halo], axis=0).astype(F32)
    inv = lax.rsqrt(jnp.mean(extended * extended, axis=1, keepdims=True) + NORM_EPS)
    normed = (extended * inv * norm_gain).astype(BF16)

    crit = mm(normed, w_crit)
    ext = jnp.concatenate([crit[TOKENS + 8 :, :ACT], crit[:TOKENS, :ACT]], axis=0)
    preact = conv_weights[KERNEL] + sum(
        conv_weights[k] * ext[5 + k : 5 + k + TOKENS] for k in range(KERNEL)
    )
    gate_of_act = sigmoid(preact)
    act = preact * gate_of_act
    head_x = act[:, :HALF]
    bc = act[:, HALF:]
    dt_in = crit[:TOKENS, ACT:] + head_half[1]
    real = iota((1, LANES), 1) < HALF_HEADS
    dt = jnp.where(real, jax.nn.softplus(dt_in), 0.0)
    log_decay = dt * decay_rate
    below = (iota((CHUNK, CHUNK), 0) >= iota((CHUNK, CHUNK), 1)).astype(F32)
    below = jnp.broadcast_to(below[None], (CHUNKS, CHUNK, CHUNK))
    cl = jnp.einsum("kts,ksh->kth", below, chunked(log_decay), precision=EXACT)
    spread = spread_matrix()
    u = head_x * exact(dt, spread)
    u_low = rounded(u)
    lasts = cl[:, -1]
    to_end = flat(jnp.exp(lasts[:, None] - cl))
    cl = flat(cl)
    to_end_wide = exact(to_end, spread)
    from_start_wide = exact(jnp.exp(cl), spread)
    u_wide = u * to_end_wide
    b_proj, c_proj = chunked(bc[:, :STATE]), chunked(bc[:, STATE:])
    b_low, c_low = b_proj.astype(BF16), c_proj.astype(BF16)
    own = jnp.einsum("ktr,ktn->krn", chunked(u_wide), b_proj, precision=PRECISE)
    def between(i, j):
        return per_row(jnp.exp(sum(lasts[i:j])) if j > i else jnp.ones((LANES,), F32))

    local = [jnp.zeros_like(own[0])]
    for k in range(CHUNKS):
        local.append(sum(between(i + 1, k + 1) * own[i] for i in range(k + 1)))
    piece_decay = jnp.exp(jnp.sum(lasts, axis=0))
    incoming = combine(pack_full(local[CHUNKS], piece_decay), 1, unpack_full)
    decay = decays(cl)
    scores = jnp.einsum("ktn,ksn->kts", c_proj, b_proj, precision=PRECISE)
    mixes = (scores[:, None, None] * decay).astype(BF16)
    u_pairs = one_head(by_pair(u_low.astype(BF16)))
    y_chunk = from_pairs(product("kpjts,kpjsc->kptc", mixes, u_pairs))

    starts = jnp.stack([between(0, k) * incoming + local[k] for k in range(CHUNKS)])
    state_end = between(0, CHUNKS) * incoming + local[CHUNKS]
    y_state = flat(jnp.einsum("ktn,krn->ktr", c_proj, starts, precision=PRECISE)) * from_start_wide
    y_ssd = y_chunk + y_state
    skip_wide = exact(head_half[2:3], spread)
    mixed = y_ssd + skip_wide * head_x

    gate = mm(normed[:TOKENS], w_gate)
    gate_sig = sigmoid(gate)
    gate_silu = gate * gate_sig
    d_gated = mm(cot, w_out, NT)
    g = mixed * gate_silu
    e = d_gated * gate_gain
    sums = jnp.concatenate(
        [jnp.sum(g * g, axis=1, keepdims=True), jnp.sum(e * g, axis=1, keepdims=True)], axis=1
    )
    sums = (sums + swap_cores(sums)) / INNER
    r = lax.rsqrt(sums[:, :1] + NORM_EPS)
    gated_low = (g * r * gate_gain).astype(BF16)
    d_g = r * e - (r * r * r) * g * sums[:, 1:]
    d_gate_gain = jnp.sum(d_gated * g * r, axis=0)
    dy = d_g * gate_silu
    d_gate = (d_g * mixed * (gate_sig * (1.0 + gate * (1.0 - gate_sig)))).astype(BF16)
    dy_low = rounded(dy)

    dy_start = chunked(dy * from_start_wide)
    chunk_backs = jnp.einsum("ktr,ktn->krn", dy_start, c_proj, precision=PRECISE)
    back = [None] * CHUNKS
    for k in range(CHUNKS):
        back[k] = sum((between(k + 1, i) * chunk_backs[i] for i in range(k + 1, CHUNKS)), jnp.zeros_like(own[0]))
    to_before = sum(between(0, i) * chunk_backs[i] for i in range(CHUNKS))
    leaving = combine(pack_state(to_before, piece_decay), -1, unpack_state)
    def own_rows(value):
        return jnp.where(first_core, value[:OWN], value[OWN:]), jnp.where(
            first_core, value[OWN:], value[:OWN]
        )

    def to_owner(value):
        low, high = value[:CHUNK], value[CHUNK:]
        sent = [jnp.where(even_x, low, high), jnp.where(even_x, high, low)]
        back0, back1 = regroup(sent[0], 0), regroup(sent[1], 1)
        return jnp.where(even_x, jnp.stack([back0, back1]), jnp.stack([back1, back0]))

    order_gate, order_out = ("x", "z", "y"), ("z", "x", "y")
    order_a, order_b = ("y", "z", "x"), ("z", "y", "x")
    normed_gate = mm(pick(in_rows(order_gate)), normed, NT).astype(BF16)
    normed_a = mm(pick(in_rows(order_a)), normed, NT).astype(BF16)
    normed_b = mm(pick(in_rows(order_b)), normed, NT).astype(BF16)
    gated_b = mm(pick(out_rows(order_out)), gated_low, NT).astype(BF16)
    middle = WIDTH // 2
    first = Halving(
        [mm(normed_gate[middle:, :TOKENS], d_gate), mm(gated_b[middle:], cot)],
        [mm(normed_gate[:middle, :TOKENS], d_gate), mm(gated_b[:middle], cot)],
        [order_gate, order_out],
    )

    dy_pairs = by_pair(dy_low.astype(BF16))
    du_chunk = from_pairs(product("kpjts,kpjtc->kpsc", mixes, one_head(dy_pairs)))
    both = product("kptc,kpjsc->kpjts", dy_pairs, u_pairs)
    d_scores = jnp.sum(decay * both, axis=(1, 2)).astype(BF16)
    db_chunk = product("kts,ktn->ksn", d_scores, c_low)
    dc_chunk = product("kts,ksn->ktn", d_scores, b_low)

    part_out = mm(gated_low, w_out)
    kept, other = own_rows(part_out)
    own_out = own_in.astype(F32) + (kept + swap_cores(other))
    block_out = to_owner(own_out.astype(BF16))

    leaving, du_chunk, db_chunk, dc_chunk = wait([first], leaving, du_chunk, db_chunk, dc_chunk)

    ends = jnp.stack([between(k + 1, CHUNKS) * leaving + back[k] for k in range(CHUNKS)])
    du = du_chunk + flat(jnp.einsum("ktn,krn->ktr", b_proj, ends, precision=PRECISE)) * to_end_wide
    d_b = flat(db_chunk + jnp.einsum("ktr,krn->ktn", chunked(u_wide), ends, precision=PRECISE))
    d_c = flat(dc_chunk + jnp.einsum("ktr,krn->ktn", dy_start, starts, precision=PRECISE))
    du, d_b, d_c = wait([first], du, d_b, d_c)
    d_bc = jnp.concatenate([d_b, d_c], axis=1)
    nexts = jnp.concatenate([starts[1:], state_end[None]], axis=0)
    carries = exact(jnp.sum(ends * nexts, axis=2), spread, NT)
    d_cl = chunked(exact(dy_low * y_ssd - u_low * du, spread, NT))
    d_log_decay = flat(jnp.einsum("kts,kth->ksh", below, d_cl, precision=PRECISE) + carries[:, None])
    d_dt = exact(head_x * du, spread, NT) + d_log_decay * decay_rate
    d_dt_raw = jnp.where(real, d_dt * sigmoid(dt_in), 0.0)
    d_head = jnp.stack(
        [
            jnp.sum(d_log_decay * log_decay, axis=0),
            jnp.sum(d_dt_raw, axis=0),
            exact(jnp.sum(dy * head_x, axis=0, keepdims=True), spread, NT)[0],
        ]
    )
    d_x = exact(dt, spread) * du + skip_wide * dy
    d_act = jnp.concatenate([d_x, d_bc], axis=1)
    d_pre = d_act * (gate_of_act * (1.0 + preact * (1.0 - gate_of_act)))
    (d_pre,) = wait([first], d_pre)
    d_ext = sum(
        conv_weights[k] * jnp.pad(d_pre, ((5 + k, 3 - k), (0, 0))) for k in range(KERNEL)
    )
    d_conv = jnp.where(iota((8, ACT), 0) == KERNEL, jnp.sum(d_pre, axis=0)[None], 0.0)
    for k in range(KERNEL):
        tap = jnp.sum(d_pre * ext[5 + k : 5 + k + TOKENS], axis=0)
        d_conv = jnp.where(iota((8, ACT), 0) == k, tap[None], d_conv)
    d_ext = jnp.concatenate([d_ext[8:], jnp.zeros((8, ACT), F32), d_ext[:8]], axis=0)
    d_crit = jnp.concatenate(
        [d_ext, jnp.pad(d_dt_raw, ((0, HALO), (0, 0)))], axis=1
    ).astype(BF16)
    (d_crit,) = wait([first], d_crit)

    y_of, x_of, z_of = block_order(order_b)
    row_at = rows_of((y_of * 4 + x_of) * 4 + z_of)[:, None]
    device_of, slot_of = row_at // 12, row_at % 12
    conv_x = d_conv[:, :HALF]
    conv_full = jnp.concatenate(
        [ordered(first_core, conv_x, jnp.zeros_like(conv_x), axis=1), d_conv[:, HALF:]], axis=1
    )
    slot_pick = (slot_of == iota((1536, 8), 1)).astype(F32)
    conv_cols = iota((1536, CONV), 1)
    conv_spread = jnp.where(conv_cols // 26 == device_of, exact(slot_pick, conv_full), 0.0)
    fold = (iota((CONV, LANES), 0) % 26 + HALF_HEADS == iota((CONV, LANES), 1)).astype(BF16)
    gain_at = WIDTH + core * HALF + iota((1536, HALF), 1)
    gain_spread = jnp.where((gain_at // 36 == device_of) & (slot_of == 5), d_gate_gain[None, :], 0.0)
    gain_fold = (
        (WIDTH + core * HALF + iota((HALF, LANES), 0)) % 36 + HALF_HEADS == iota((HALF, LANES), 1)
    ).astype(BF16)
    riders = mm(conv_spread, fold) + mm(gain_spread, gain_fold)

    crit_b = jnp.concatenate([d_crit[:, PART:]], axis=1)

    def part_b(rows):
        with_riders = jnp.pad(riders[rows], ((0, 0), (CRIT - PART - LANES, 0)))
        return mm(normed_b[rows], crit_b) + with_riders

    second = Halving(
        [mm(normed_a[middle:], d_crit[:, :PART]), part_b(slice(middle, None))],
        [mm(normed_a[:middle], d_crit[:, :PART]), part_b(slice(0, middle))],
        [order_a, order_b],
    )

    d_normed = mm(d_crit, w_crit, NT)
    d_halo = along_y(d_normed[TOKENS:], -1)
    d_normed = d_normed[:TOKENS] + mm(d_gate, w_gate, NT)
    d_normed = jnp.concatenate(
        [d_normed[: TOKENS - HALO], d_normed[TOKENS - HALO :] + d_halo], axis=0
    )
    kept, other = own_rows(d_normed)
    d_own = kept + swap_cores(other)
    own = own_in.astype(F32)
    own_inv = lax.rsqrt(jnp.mean(own * own, axis=1, keepdims=True) + NORM_EPS)
    d_own = d_own * norm_gain
    d_tokens = own_inv * d_own - (own_inv * own_inv * own_inv) * own * jnp.mean(
        own * d_own, axis=1, keepdims=True
    )
    input_grad = to_owner((own_cot.astype(F32) + d_tokens).astype(BF16)).astype(F32)

    head_own = jnp.pad(d_head, ((0, 5), (0, 0)))
    for step in range(6):
        head_got = exchange(head_own, CHIPS[step // 2], step % 2)
        head_own, head_got = wait([second, first] if step < 2 else [second], head_own, head_got)
        head_own = head_own + head_got
    head_other = swap_cores(head_own)
    rows_a, rows_b = second.totals
    gate_rows, out_rows_grad = first.totals

    rows = jnp.concatenate([rows_a, rows_b, gate_rows], axis=1)
    mine = jnp.where(first_core, rows[:12], rows[12:])
    theirs = jnp.where(first_core, rows[12:], rows[:12])
    theirs = swap_cores(theirs)
    h0 = jnp.where(first_core, mine, theirs)
    h1 = jnp.where(first_core, theirs, mine)
    in_share = jnp.concatenate(
        [
            h0[:, CRIT:],
            h1[:, CRIT:],
            h0[:, :HALF],
            h1[:, :HALF],
            h0[:, HALF:ACT] + h1[:, HALF:ACT],
            h0[:, ACT : ACT + HALF_HEADS],
            h1[:, ACT : ACT + HALF_HEADS],
        ],
        axis=1,
    )
    riding = h0[:, ACT + HALF_HEADS : CRIT] + h1[:, ACT + HALF_HEADS : CRIT]
    conv_share = riding[:5, :26]
    out_share = cross_halves(out_rows_grad)
    at_device = ((lax.axis_index("y") * 4 + x_at) * 4 + lax.axis_index("z")) * 2 + core
    w_own = rounded(in_master)
    own_gain = lax.dynamic_slice(norm_gain, (at_device * 12,), (12,))
    gain_rows = jnp.sum(w_own * in_share, axis=1) / own_gain
    thirds = [
        lax.ppermute(gain_rows, ALL, [(3 * d + k, d) for d in range(128) if 3 * d + k < 128])
        for k in range(3)
    ]
    gain_share = jnp.concatenate(thirds) + riding[5, :36]
    head_share = ordered(
        first_core, head_own[:3, :HALF_HEADS], head_other[:3, :HALF_HEADS], axis=1
    )

    in_next = adamw_step(in_master, in_share, in_moment1, in_moment2, MATRIX_RATE, MATRIX_DECAY)
    out_next = adamw_step(
        out_master, out_share, out_moment1, out_moment2, MATRIX_RATE, MATRIX_DECAY
    )
    conv_next = adamw_step(conv_master, conv_share, conv_moment1, conv_moment2, SMALL_RATE, 0.0)
    gain_next = adamw_step(gain_master, gain_share, gain_moment1, gain_moment2, SMALL_RATE, 0.0)
    head_next = adamw_step(head_master, head_share, head_moment1, head_moment2, SMALL_RATE, 0.0)
    return (
        block_out,
        input_grad,
        *in_next,
        *out_next,
        *conv_next,
        *gain_next,
        *head_next,
    )


def solution(mesh):
    fine = Mesh(mesh.devices.reshape(4, 4, 4, 2), ALL)
    tokens = P(("z", "c"), ("y", "x"), None)
    rows = P(ALL, None)
    columns = P(None, ALL)
    flat = P(ALL)
    return jax.shard_map(
        on_device,
        mesh=fine,
        in_specs=(tokens, tokens) + (rows,) * 6 + (columns,) * 3 + (flat,) * 3 + (P(),) * 3,
        out_specs=(tokens, tokens) + (rows,) * 6 + (columns,) * 3 + (flat,) * 3 + (P(),) * 3,
        check_vma=False,
    )
```

```python
import jax
import jax.numpy as jnp
from jax import lax
from jax.sharding import Mesh
from jax.sharding import PartitionSpec as P

WIDTH = 1536
INNER = 3072
STATE = 128
HEADDIM = 64
KERNEL = 4
STEP = 5
HEADS = 48
CONV = 3328
PROJ = 6448

HALF = INNER // 2
HALF_HEADS = HEADS // 2
TOKENS = 512
OWN = TOKENS // 2
HALO = 16
ROWS_IN = TOKENS + HALO
CHUNK = 128
CHUNKS = TOKENS // CHUNK
LANES = 128
ACT = HALF + 2 * STATE
CRIT = ACT + LANES
PART = 1024
ROWS = 24

NORM_EPS = 1e-05
PRECISE = lax.Precision.HIGH
EXACT = lax.Precision.HIGHEST
BETA_ONE = 0.9
BETA_TWO = 0.95
ADAM_EPS = 1e-08
MATRIX_RATE = 0.05
SMALL_RATE = 0.5
MATRIX_DECAY = 0.1
BF16 = jnp.bfloat16
F32 = jnp.float32
CHIPS = ("y", "x", "z")
ALL = ("y", "x", "z", "c")


def mm(a, b, dims=((1,), (0,))):
    return lax.dot_general(
        a.astype(BF16), b.astype(BF16), (dims, ((), ())), preferred_element_type=F32
    )


def exact(a, b, dims=((1,), (0,))):
    return lax.dot_general(a, b, (dims, ((), ())), precision=PRECISE, preferred_element_type=F32)


NT = ((1,), (1,))
TN = ((0,), (0,))


def rounded(v):
    return lax.reduce_precision(v, 8, 7)


def iota(shape, dim):
    return lax.broadcasted_iota(jnp.int32, shape, dim)


def sigmoid(v):
    return 1.0 / (1.0 + jnp.exp(-v))


def spread_matrix():
    return (iota((LANES, HALF), 1) // HEADDIM == iota((LANES, HALF), 0)).astype(F32)


def adamw_step(weight, gradient, moment_one, moment_two, step_rate, weight_decay):
    one_next = BETA_ONE * moment_one + (1.0 - BETA_ONE) * gradient
    two_next = BETA_TWO * moment_two + (1.0 - BETA_TWO) * gradient * gradient
    corrected = one_next / (1.0 - BETA_ONE**STEP)
    scale_next = jnp.sqrt(two_next / (1.0 - BETA_TWO**STEP)) + ADAM_EPS
    weight_next = weight - step_rate * (corrected / scale_next + weight_decay * weight)
    return (one_next, two_next, weight_next)


def swap_cores(value):
    return lax.ppermute(value, "c", [(0, 1), (1, 0)])


def regroup(value, turn):
    pairs = [
        (x * 2 + c, (2 * c + (x + turn) % 2) * 2 + x // 2) for x in range(4) for c in range(2)
    ]
    return lax.ppermute(value, ("x", "c"), pairs)


def cross_halves(value):
    pairs = []
    for y in range(4):
        for c in range(2):
            to = (y, c) if y // 2 == c else (y ^ 2, 1 - c)
            pairs.append((y * 2 + c, to[0] * 2 + to[1]))
    return lax.ppermute(value, ("y", "c"), pairs)


def along_y(value, steps):
    return lax.ppermute(value, "y", [(y, y + steps) for y in range(4) if 0 <= y + steps < 4])


def partner(axis, turn):
    pairs = []
    for i in range(4):
        for c in range(2):
            pairs.append((i * 2 + c, (i ^ (1 if (turn + c) % 2 == 0 else 3)) * 2 + c))
    return (axis, "c"), pairs


def exchange(value, axis, turn):
    axes, pairs = partner(axis, turn)
    return lax.ppermute(value, axes, pairs)


def block_order(order):
    first = jnp.where(lax.axis_index("c") == 0, 1, 3)
    second = 4 - first
    block = jnp.arange(64)
    place = {a: lax.axis_index(a) for a in CHIPS}
    for at, axis in enumerate(order):
        high = (block >> (5 - 2 * at)) & 1
        low = (block >> (4 - 2 * at)) & 1
        place[axis] = place[axis] ^ (high * first) ^ (low * second)
    return [place[a] + jnp.zeros((64,), jnp.int32) for a in CHIPS]


def rows_of(blocks):
    return (blocks[:, None] * ROWS + jnp.arange(ROWS)[None, :]).reshape(-1)


def in_rows(order):
    y, x, z = block_order(order)
    return rows_of((y * 4 + x) * 4 + z)


def out_rows(order):
    y, x, z = block_order(order)
    return rows_of((((y % 2) * 4 + x) * 4 + z) * 2 + y // 2)


def pick(rows):
    return (rows[:, None] == iota((1536, 1536), 1)).astype(BF16)


class Halving:
    def __init__(self, sends, keeps, orders):
        self.sends = [v.astype(BF16) for v in sends]
        self.keeps, self.orders, self.step = keeps, orders, 0

    def start(self):
        self.arrived = [
            exchange(v, order[self.step // 2], self.step % 2)
            for v, order in zip(self.sends, self.orders)
        ]

    def add(self):
        totals = [keep + got.astype(F32) for keep, got in zip(self.keeps, self.arrived)]
        self.step += 1
        if self.step == 6:
            self.totals = totals
            return
        half = totals[0].shape[0] // 2
        self.sends = [t[half:].astype(BF16) for t in totals]
        self.keeps = [t[:half] for t in totals]
        self.start()


def wait(halvings, *values):
    held = [h.arrived for h in halvings], [h.keeps for h in halvings], values
    arrived, keeps, values = lax.optimization_barrier(held)
    for h, a, k in zip(halvings, arrived, keeps):
        h.arrived, h.keeps = a, k
        h.add()
    return values


PAIRS = HALF_HEADS // 2


def product(terms, a, b):
    return jnp.einsum(terms, a, b, preferred_element_type=F32)


def by_pair(value):
    pairs = [value[:, p * LANES : (p + 1) * LANES] for p in range(PAIRS)]
    return jnp.stack(pairs).reshape(PAIRS, CHUNKS, CHUNK, LANES)


def from_pairs(value):
    return jnp.concatenate([value[p].reshape(TOKENS, LANES) for p in range(PAIRS)], axis=1)


def one_head(value):
    left = iota((2, 1, LANES), 2) // HEADDIM == iota((2, 1, LANES), 0)
    return jnp.where(left, value[:, :, None], jnp.zeros((), value.dtype))


def decays(cl):
    heads = cl[:, :HALF_HEADS].T.reshape(PAIRS, 2, CHUNKS, CHUNK).transpose(0, 2, 1, 3)
    causal = iota((CHUNK, CHUNK), 0) >= iota((CHUNK, CHUNK), 1)
    differ = jnp.where(causal, heads[..., :, None] - heads[..., None, :], 0.0)
    return jnp.where(causal, jnp.exp(differ), 0.0)


def pack_state(state, decay):
    high = rounded(decay)
    middle = rounded(decay - high)
    low = rounded(decay - high - middle)
    at = iota((16, LANES), 0)
    rows = jnp.where(at == 0, high, jnp.where(at == 1, middle, 0.0))
    rows = jnp.where(at == 2, low, rows)
    return jnp.concatenate([state, rows], axis=0).astype(BF16)


def unpack_state(packed):
    rows = packed[HALF : HALF + 3].astype(F32)
    return packed[:HALF].astype(F32), rows[0] + rows[1] + rows[2]


def per_row(head_values):
    heads = head_values[..., :HALF_HEADS, None]
    wide = jnp.broadcast_to(heads, heads.shape[:-1] + (HEADDIM,))
    return wide.reshape(head_values.shape[:-1] + (HALF, 1))


def combine(packed, way, unpack):
    near, far, farthest = [unpack(along_y(packed, way * k)) for k in (1, 2, 3)]
    return near[0] + per_row(near[1]) * (far[0] + per_row(far[1]) * farthest[0])


def pack_full(state, decay):
    return jnp.concatenate([state, jnp.broadcast_to(decay[None], (8, LANES))], axis=0)


def unpack_full(packed):
    return packed[:HALF], packed[HALF]


def chunked(value):
    return value.reshape(CHUNKS, CHUNK, value.shape[-1])


def flat(value):
    return value.reshape(TOKENS, value.shape[-1])


def on_device(
    block_in,
    cotangent,
    in_master,
    in_moment1,
    in_moment2,
    out_master,
    out_moment1,
    out_moment2,
    conv_master,
    conv_moment1,
    conv_moment2,
    gain_master,
    gain_moment1,
    gain_moment2,
    head_master,
    head_moment1,
    head_moment2,
):
    core = lax.axis_index("c")
    x_at = lax.axis_index("x")
    first_core = core == 0
    even_x = x_at % 2 == 0

    def ordered(flag, mine, other, axis=0):
        return jnp.where(
            flag, jnp.concatenate([mine, other], axis=axis), jnp.concatenate([other, mine], axis=axis)
        )

    riders_out = jnp.concatenate(
        [
            jnp.pad(conv_master, ((0, 0), (0, LANES - HALF_HEADS - 26))),
            jnp.pad(gain_master[None], ((0, 6), (0, LANES - HALF_HEADS - 36))),
        ],
        axis=0,
    )

    def half_columns(c):
        return jnp.concatenate(
            [
                in_master[:, INNER + c * HALF : INNER + (c + 1) * HALF],
                in_master[:, 2 * INNER : INNER + CONV],
                in_master[:, INNER + CONV + c * HALF_HEADS : INNER + CONV + (c + 1) * HALF_HEADS],
                riders_out,
                in_master[:, c * HALF : (c + 1) * HALF],
            ],
            axis=1,
        )

    halves = [half_columns(0), half_columns(1)]
    mine = jnp.where(first_core, halves[0], halves[1])
    theirs = jnp.where(first_core, halves[1], halves[0])
    in_rows_low = ordered(first_core, mine, swap_cores(theirs)).astype(BF16)
    out_rows_low = cross_halves(out_master).astype(BF16)
    w_crit = lax.all_gather(in_rows_low[:, :CRIT], CHIPS, axis=0, tiled=True)
    rest_low = jnp.concatenate([in_rows_low[:, CRIT:], out_rows_low], axis=1)
    w_rest = lax.all_gather(rest_low, CHIPS, axis=0, tiled=True)
    w_gate = w_rest[:, :HALF]
    w_out = (
        w_rest[:, HALF:]
        .reshape(2, 2, 16, ROWS, WIDTH)
        .transpose(1, 2, 0, 3, 4)
        .reshape(HALF, WIDTH)
    )
    smalls = w_crit[:, ACT:]
    device_at, slot_at = iota((1536, 1), 0) // 12, iota((1536, 1), 0) % 12

    def gather_small(columns, width, slots):
        unfold = (HALF_HEADS + columns % width == iota((LANES, columns.shape[1]), 0)).astype(BF16)
        wide = jnp.where(device_at == columns // width, mm(smalls, unfold), 0.0)
        return mm((slot_at == slots).astype(BF16), wide, TN)

    norm_gain = gather_small(iota((1, WIDTH), 1), 36, 5 + iota((1, 8), 1))[0]
    gate_gain = gather_small(WIDTH + core * HALF + iota((1, HALF), 1), 36, 5 + iota((1, 8), 1))[0]
    conv_at = iota((1, ACT), 1)
    conv_at = jnp.where(conv_at < HALF, core * HALF + conv_at, INNER - HALF + conv_at)
    conv_weights = gather_small(conv_at, 26, iota((1, 8), 1))
    head_half = jnp.pad(
        lax.dynamic_slice(head_master, (0, core * HALF_HEADS), (3, HALF_HEADS)),
        ((0, 0), (0, LANES - HALF_HEADS)),
    )
    decay_rate = -jnp.exp(head_half[0])

    both = jnp.stack([block_in, cotangent], axis=1)
    flipped = both[::-1]
    got = [regroup(jnp.where(even_x, both, flipped)[k], k) for k in range(2)]
    own_both = ordered(even_x, got[0], got[1], axis=1)
    all_both = ordered(first_core, own_both, swap_cores(own_both), axis=1)
    own_in, own_cot = own_both[0], own_both[1]
    tokens, cot = all_both[0], all_both[1]
    halo = along_y(tokens[TOKENS - HALO :], 1)
    extended = jnp.concatenate([tokens, halo], axis=0).astype(F32)
    inv = lax.rsqrt(jnp.mean(extended * extended, axis=1, keepdims=True) + NORM_EPS)
    normed = (extended * inv * norm_gain).astype(BF16)

    crit = mm(normed, w_crit)
    ext = jnp.concatenate([crit[TOKENS + 8 :, :ACT], crit[:TOKENS, :ACT]], axis=0)
    preact = conv_weights[KERNEL] + sum(
        conv_weights[k] * ext[5 + k : 5 + k + TOKENS] for k in range(KERNEL)
    )
    gate_of_act = sigmoid(preact)
    act = preact * gate_of_act
    head_x = act[:, :HALF]
    bc = act[:, HALF:]
    dt_in = crit[:TOKENS, ACT:] + head_half[1]
    real = iota((1, LANES), 1) < HALF_HEADS
    dt = jnp.where(real, jax.nn.softplus(dt_in), 0.0)
    log_decay = dt * decay_rate
    below = (iota((CHUNK, CHUNK), 0) >= iota((CHUNK, CHUNK), 1)).astype(F32)
    below = jnp.broadcast_to(below[None], (CHUNKS, CHUNK, CHUNK))
    cl = jnp.einsum("kts,ksh->kth", below, chunked(log_decay), precision=EXACT)
    spread = spread_matrix()
    u = head_x * exact(dt, spread)
    u_low = rounded(u)
    lasts = cl[:, -1]
    to_end = flat(jnp.exp(lasts[:, None] - cl))
    cl = flat(cl)
    to_end_wide = exact(to_end, spread)
    from_start_wide = exact(jnp.exp(cl), spread)
    u_wide = u * to_end_wide
    b_proj, c_proj = chunked(bc[:, :STATE]), chunked(bc[:, STATE:])
    b_low, c_low = b_proj.astype(BF16), c_proj.astype(BF16)
    own = jnp.einsum("ktr,ktn->krn", chunked(u_wide), b_proj, precision=PRECISE)
    def between(i, j):
        return per_row(jnp.exp(sum(lasts[i:j])) if j > i else jnp.ones((LANES,), F32))

    local = [jnp.zeros_like(own[0])]
    for k in range(CHUNKS):
        local.append(sum(between(i + 1, k + 1) * own[i] for i in range(k + 1)))
    piece_decay = jnp.exp(jnp.sum(lasts, axis=0))
    incoming = combine(pack_full(local[CHUNKS], piece_decay), 1, unpack_full)
    decay = decays(cl)
    scores = jnp.einsum("ktn,ksn->kts", c_proj, b_proj, precision=PRECISE)
    mixes = (scores[None, :, None] * decay).astype(BF16)
    u_pairs = one_head(by_pair(u_low.astype(BF16)))
    y_chunk = from_pairs(product("pkjts,pkjsc->pktc", mixes, u_pairs))

    starts = jnp.stack([between(0, k) * incoming + local[k] for k in range(CHUNKS)])
    state_end = between(0, CHUNKS) * incoming + local[CHUNKS]
    y_state = flat(jnp.einsum("ktn,krn->ktr", c_proj, starts, precision=PRECISE)) * from_start_wide
    y_ssd = y_chunk + y_state
    skip_wide = exact(head_half[2:3], spread)
    mixed = y_ssd + skip_wide * head_x

    gate = mm(normed[:TOKENS], w_gate)
    gate_sig = sigmoid(gate)
    gate_silu = gate * gate_sig
    (d_gated,) = lax.optimization_barrier((mm(cot, w_out, NT),))
    g = mixed * gate_silu
    e = d_gated * gate_gain
    sums = jnp.concatenate(
        [jnp.sum(g * g, axis=1, keepdims=True), jnp.sum(e * g, axis=1, keepdims=True)], axis=1
    )
    sums = (sums + swap_cores(sums)) / INNER
    r = lax.rsqrt(sums[:, :1] + NORM_EPS)
    gated_low = (g * r * gate_gain).astype(BF16)
    d_g = r * e - (r * r * r) * g * sums[:, 1:]
    d_gate_gain = jnp.sum(d_gated * g * r, axis=0)
    dy = d_g * gate_silu
    d_gate = (d_g * mixed * (gate_sig * (1.0 + gate * (1.0 - gate_sig)))).astype(BF16)
    dy_low = rounded(dy)

    dy_start = chunked(dy * from_start_wide)
    chunk_backs = jnp.einsum("ktr,ktn->krn", dy_start, c_proj, precision=PRECISE)
    back = [None] * CHUNKS
    for k in range(CHUNKS):
        back[k] = sum((between(k + 1, i) * chunk_backs[i] for i in range(k + 1, CHUNKS)), jnp.zeros_like(own[0]))
    to_before = sum(between(0, i) * chunk_backs[i] for i in range(CHUNKS))
    leaving = combine(pack_state(to_before, piece_decay), -1, unpack_state)
    def own_rows(value):
        return jnp.where(first_core, value[:OWN], value[OWN:]), jnp.where(
            first_core, value[OWN:], value[:OWN]
        )

    def to_owner(value):
        low, high = value[:CHUNK], value[CHUNK:]
        sent = [jnp.where(even_x, low, high), jnp.where(even_x, high, low)]
        back0, back1 = regroup(sent[0], 0), regroup(sent[1], 1)
        return jnp.where(even_x, jnp.stack([back0, back1]), jnp.stack([back1, back0]))

    order_gate, order_out = ("x", "z", "y"), ("z", "x", "y")
    order_a, order_b = ("y", "z", "x"), ("z", "y", "x")
    normed_gate = mm(pick(in_rows(order_gate)), normed, NT).astype(BF16)
    normed_a = mm(pick(in_rows(order_a)), normed, NT).astype(BF16)
    normed_b = mm(pick(in_rows(order_b)), normed, NT).astype(BF16)
    gated_b = mm(pick(out_rows(order_out)), gated_low, NT).astype(BF16)
    middle = WIDTH // 2
    first = Halving(
        [mm(normed_gate[middle:, :TOKENS], d_gate), mm(gated_b[middle:], cot)],
        [mm(normed_gate[:middle, :TOKENS], d_gate), mm(gated_b[:middle], cot)],
        [order_gate, order_out],
    )
    first.start()

    dy_pairs = by_pair(dy_low.astype(BF16))
    du_chunk = from_pairs(product("pkjts,pkjtc->pksc", mixes, one_head(dy_pairs)))
    both = product("pktc,pkjsc->pkjts", dy_pairs, u_pairs)
    d_scores = jnp.sum(decay * both, axis=(0, 2)).astype(BF16)
    db_chunk = product("kts,ktn->ksn", d_scores, c_low)
    dc_chunk = product("kts,ksn->ktn", d_scores, b_low)

    part_out = mm(gated_low, w_out)
    kept, other = own_rows(part_out)
    own_out = own_in.astype(F32) + (kept + swap_cores(other))
    block_out = to_owner(own_out.astype(BF16))

    leaving, du_chunk, db_chunk, dc_chunk = wait([first], leaving, du_chunk, db_chunk, dc_chunk)

    ends = jnp.stack([between(k + 1, CHUNKS) * leaving + back[k] for k in range(CHUNKS)])
    du = du_chunk + flat(jnp.einsum("ktn,krn->ktr", b_proj, ends, precision=PRECISE)) * to_end_wide
    d_b = flat(db_chunk + jnp.einsum("ktr,krn->ktn", chunked(u_wide), ends, precision=PRECISE))
    d_c = flat(dc_chunk + jnp.einsum("ktr,krn->ktn", dy_start, starts, precision=PRECISE))
    du, d_b, d_c = wait([first], du, d_b, d_c)
    d_bc = jnp.concatenate([d_b, d_c], axis=1)
    nexts = jnp.concatenate([starts[1:], state_end[None]], axis=0)
    carries = exact(jnp.sum(ends * nexts, axis=2), spread, NT)
    d_cl = chunked(exact(dy_low * y_ssd - u_low * du, spread, NT))
    d_log_decay = flat(jnp.einsum("kts,kth->ksh", below, d_cl, precision=PRECISE) + carries[:, None])
    d_dt = exact(head_x * du, spread, NT) + d_log_decay * decay_rate
    d_dt_raw = jnp.where(real, d_dt * sigmoid(dt_in), 0.0)
    d_head = jnp.stack(
        [
            jnp.sum(d_log_decay * log_decay, axis=0),
            jnp.sum(d_dt_raw, axis=0),
            exact(jnp.sum(dy * head_x, axis=0, keepdims=True), spread, NT)[0],
        ]
    )
    d_x = exact(dt, spread) * du + skip_wide * dy
    d_act = jnp.concatenate([d_x, d_bc], axis=1)
    d_pre = d_act * (gate_of_act * (1.0 + preact * (1.0 - gate_of_act)))
    (d_pre,) = wait([first], d_pre)
    d_ext = sum(
        conv_weights[k] * jnp.pad(d_pre, ((5 + k, 3 - k), (0, 0))) for k in range(KERNEL)
    )
    d_conv = jnp.where(iota((8, ACT), 0) == KERNEL, jnp.sum(d_pre, axis=0)[None], 0.0)
    for k in range(KERNEL):
        tap = jnp.sum(d_pre * ext[5 + k : 5 + k + TOKENS], axis=0)
        d_conv = jnp.where(iota((8, ACT), 0) == k, tap[None], d_conv)
    d_ext = jnp.concatenate([d_ext[8:], jnp.zeros((8, ACT), F32), d_ext[:8]], axis=0)
    d_crit = jnp.concatenate(
        [d_ext, jnp.pad(d_dt_raw, ((0, HALO), (0, 0)))], axis=1
    ).astype(BF16)
    (d_crit,) = wait([first], d_crit)

    y_of, x_of, z_of = block_order(order_b)
    row_at = rows_of((y_of * 4 + x_of) * 4 + z_of)[:, None]
    device_of, slot_of = row_at // 12, row_at % 12
    slot_pick = (slot_of == iota((1536, 8), 1)).astype(F32)
    conv_spread = jnp.where(conv_at // 26 == device_of, exact(slot_pick, d_conv), 0.0)
    fold = (conv_at.T % 26 + HALF_HEADS == iota((ACT, LANES), 1)).astype(BF16)
    gain_at = WIDTH + core * HALF + iota((1536, HALF), 1)
    gain_spread = jnp.where((gain_at // 36 == device_of) & (slot_of == 5), d_gate_gain[None, :], 0.0)
    gain_fold = (
        (WIDTH + core * HALF + iota((HALF, LANES), 0)) % 36 + HALF_HEADS == iota((HALF, LANES), 1)
    ).astype(BF16)
    riders = mm(conv_spread, fold) + mm(gain_spread, gain_fold)

    crit_b = jnp.concatenate([d_crit[:, PART:]], axis=1)

    def part_b(rows):
        with_riders = jnp.pad(riders[rows], ((0, 0), (CRIT - PART - LANES, 0)))
        return mm(normed_b[rows], crit_b) + with_riders

    second = Halving(
        [mm(normed_a[middle:], d_crit[:, :PART]), part_b(slice(middle, None))],
        [mm(normed_a[:middle], d_crit[:, :PART]), part_b(slice(0, middle))],
        [order_a, order_b],
    )

    second.sends, d_crit_late = lax.optimization_barrier((second.sends, d_crit))
    second.start()
    d_normed = mm(d_crit_late, w_crit, NT)
    d_halo = along_y(d_normed[TOKENS:], -1)
    d_normed = d_normed[:TOKENS] + mm(d_gate, w_gate, NT)
    d_normed = jnp.concatenate(
        [d_normed[: TOKENS - HALO], d_normed[TOKENS - HALO :] + d_halo], axis=0
    )
    kept, other = own_rows(d_normed)
    d_own = kept + swap_cores(other)
    own = own_in.astype(F32)
    own_inv = lax.rsqrt(jnp.mean(own * own, axis=1, keepdims=True) + NORM_EPS)
    d_own = d_own * norm_gain
    d_tokens = own_inv * d_own - (own_inv * own_inv * own_inv) * own * jnp.mean(
        own * d_own, axis=1, keepdims=True
    )
    input_grad = to_owner((own_cot.astype(F32) + d_tokens).astype(BF16))

    head_own = jnp.pad(d_head, ((0, 5), (0, 0)))
    for step in range(6):
        head_got = exchange(head_own, CHIPS[step // 2], step % 2)
        head_own, head_got = wait([second, first] if step < 2 else [second], head_own, head_got)
        head_own = head_own + head_got
        if step == 4:
            head_own, input_grad = lax.optimization_barrier((head_own, input_grad))
    input_grad = input_grad.astype(F32)
    head_other = swap_cores(head_own)
    rows_a, rows_b = second.totals
    gate_rows, out_rows_grad = first.totals

    rows = jnp.concatenate([rows_a, rows_b, gate_rows], axis=1)
    mine = jnp.where(first_core, rows[:12], rows[12:])
    theirs = jnp.where(first_core, rows[12:], rows[:12])
    theirs = swap_cores(theirs)
    h0 = jnp.where(first_core, mine, theirs)
    h1 = jnp.where(first_core, theirs, mine)
    in_share = jnp.concatenate(
        [
            h0[:, CRIT:],
            h1[:, CRIT:],
            h0[:, :HALF],
            h1[:, :HALF],
            h0[:, HALF:ACT] + h1[:, HALF:ACT],
            h0[:, ACT : ACT + HALF_HEADS],
            h1[:, ACT : ACT + HALF_HEADS],
        ],
        axis=1,
    )
    riding = h0[:, ACT + HALF_HEADS : CRIT] + h1[:, ACT + HALF_HEADS : CRIT]
    conv_share = riding[:5, :26]
    out_share = cross_halves(out_rows_grad)
    at_device = ((lax.axis_index("y") * 4 + x_at) * 4 + lax.axis_index("z")) * 2 + core
    w_own = rounded(in_master)
    own_gain = lax.dynamic_slice(norm_gain, (at_device * 12,), (12,))
    gain_rows = jnp.sum(w_own * in_share, axis=1) / own_gain
    thirds = [
        lax.ppermute(gain_rows, ALL, [(3 * d + k, d) for d in range(128) if 3 * d + k < 128])
        for k in range(3)
    ]
    gain_share = jnp.concatenate(thirds) + riding[5, :36]
    head_share = ordered(
        first_core, head_own[:3, :HALF_HEADS], head_other[:3, :HALF_HEADS], axis=1
    )

    in_next = adamw_step(in_master, in_share, in_moment1, in_moment2, MATRIX_RATE, MATRIX_DECAY)
    out_next = adamw_step(
        out_master, out_share, out_moment1, out_moment2, MATRIX_RATE, MATRIX_DECAY
    )
    conv_next = adamw_step(conv_master, conv_share, conv_moment1, conv_moment2, SMALL_RATE, 0.0)
    gain_next = adamw_step(gain_master, gain_share, gain_moment1, gain_moment2, SMALL_RATE, 0.0)
    head_next = adamw_step(head_master, head_share, head_moment1, head_moment2, SMALL_RATE, 0.0)
    return (
        block_out,
        input_grad,
        *in_next,
        *out_next,
        *conv_next,
        *gain_next,
        *head_next,
    )


def solution(mesh):
    fine = Mesh(mesh.devices.reshape(4, 4, 4, 2), ALL)
    tokens = P(("z", "c"), ("y", "x"), None)
    rows = P(ALL, None)
    columns = P(None, ALL)
    flat = P(ALL)
    return jax.shard_map(
        on_device,
        mesh=fine,
        in_specs=(tokens, tokens) + (rows,) * 6 + (columns,) * 3 + (flat,) * 3 + (P(),) * 3,
        out_specs=(tokens, tokens) + (rows,) * 6 + (columns,) * 3 + (flat,) * 3 + (P(),) * 3,
        check_vma=False,
    )
```

```python
import jax
import jax.numpy as jnp
from jax import lax
from jax.sharding import Mesh
from jax.sharding import PartitionSpec as P

WIDTH = 1536
INNER = 3072
STATE = 128
HEADDIM = 64
KERNEL = 4
STEP = 5
HEADS = 48
CONV = 3328
PROJ = 6448

HALF = INNER // 2
HALF_HEADS = HEADS // 2
TOKENS = 512
OWN = TOKENS // 2
HALO = 16
ROWS_IN = TOKENS + HALO
CHUNK = 128
CHUNKS = TOKENS // CHUNK
LANES = 128
ACT = HALF + 2 * STATE
CRIT = ACT + LANES
PART = 1024
ROWS = 24

NORM_EPS = 1e-05
PRECISE = lax.Precision.HIGH
EXACT = lax.Precision.HIGHEST
BETA_ONE = 0.9
BETA_TWO = 0.95
ADAM_EPS = 1e-08
MATRIX_RATE = 0.05
SMALL_RATE = 0.5
MATRIX_DECAY = 0.1
BF16 = jnp.bfloat16
F32 = jnp.float32
CHIPS = ("y", "x", "z")
ALL = ("y", "x", "z", "c")


def mm(a, b, dims=((1,), (0,))):
    return lax.dot_general(
        a.astype(BF16), b.astype(BF16), (dims, ((), ())), preferred_element_type=F32
    )


def exact(a, b, dims=((1,), (0,))):
    return lax.dot_general(a, b, (dims, ((), ())), precision=PRECISE, preferred_element_type=F32)


NT = ((1,), (1,))
TN = ((0,), (0,))


def rounded(v):
    return lax.reduce_precision(v, 8, 7)


def iota(shape, dim):
    return lax.broadcasted_iota(jnp.int32, shape, dim)


def sigmoid(v):
    return 1.0 / (1.0 + jnp.exp(-v))


def spread_matrix():
    return (iota((LANES, HALF), 1) // HEADDIM == iota((LANES, HALF), 0)).astype(F32)


def adamw_step(weight, gradient, moment_one, moment_two, step_rate, weight_decay):
    one_next = BETA_ONE * moment_one + (1.0 - BETA_ONE) * gradient
    two_next = BETA_TWO * moment_two + (1.0 - BETA_TWO) * gradient * gradient
    corrected = one_next / (1.0 - BETA_ONE**STEP)
    scale_next = jnp.sqrt(two_next / (1.0 - BETA_TWO**STEP)) + ADAM_EPS
    weight_next = weight - step_rate * (corrected / scale_next + weight_decay * weight)
    return (one_next, two_next, weight_next)


def swap_cores(value):
    return lax.ppermute(value, "c", [(0, 1), (1, 0)])


def regroup(value, turn):
    pairs = [
        (x * 2 + c, (2 * c + (x + turn) % 2) * 2 + x // 2) for x in range(4) for c in range(2)
    ]
    return lax.ppermute(value, ("x", "c"), pairs)


def cross_halves(value):
    pairs = []
    for y in range(4):
        for c in range(2):
            to = (y, c) if y // 2 == c else (y ^ 2, 1 - c)
            pairs.append((y * 2 + c, to[0] * 2 + to[1]))
    return lax.ppermute(value, ("y", "c"), pairs)


def along_y(value, steps):
    return lax.ppermute(value, "y", [(y, y + steps) for y in range(4) if 0 <= y + steps < 4])


def partner(axis, turn):
    pairs = []
    for i in range(4):
        for c in range(2):
            pairs.append((i * 2 + c, (i ^ (1 if (turn + c) % 2 == 0 else 3)) * 2 + c))
    return (axis, "c"), pairs


def exchange(value, axis, turn):
    axes, pairs = partner(axis, turn)
    return lax.ppermute(value, axes, pairs)


def block_order(order):
    first = jnp.where(lax.axis_index("c") == 0, 1, 3)
    second = 4 - first
    block = jnp.arange(64)
    place = {a: lax.axis_index(a) for a in CHIPS}
    for at, axis in enumerate(order):
        high = (block >> (5 - 2 * at)) & 1
        low = (block >> (4 - 2 * at)) & 1
        place[axis] = place[axis] ^ (high * first) ^ (low * second)
    return [place[a] + jnp.zeros((64,), jnp.int32) for a in CHIPS]


def rows_of(blocks):
    return (blocks[:, None] * ROWS + jnp.arange(ROWS)[None, :]).reshape(-1)


def in_rows(order):
    y, x, z = block_order(order)
    return rows_of((y * 4 + x) * 4 + z)


def out_rows(order):
    y, x, z = block_order(order)
    return rows_of((((y % 2) * 4 + x) * 4 + z) * 2 + y // 2)


def pick(rows):
    return (rows[:, None] == iota((1536, 1536), 1)).astype(BF16)


class Halving:
    def __init__(self, sends, keeps, orders):
        self.sends = [v.astype(BF16) for v in sends]
        self.keeps, self.orders, self.step = keeps, orders, 0

    def start(self):
        self.arrived = [
            exchange(v, order[self.step // 2], self.step % 2)
            for v, order in zip(self.sends, self.orders)
        ]

    def add(self):
        totals = [keep + got.astype(F32) for keep, got in zip(self.keeps, self.arrived)]
        self.step += 1
        if self.step == 6:
            self.totals = totals
            return
        half = totals[0].shape[0] // 2
        self.sends = [t[half:].astype(BF16) for t in totals]
        self.keeps = [t[:half] for t in totals]
        self.start()


def wait(halvings, *values):
    held = [h.arrived for h in halvings], [h.keeps for h in halvings], values
    arrived, keeps, values = lax.optimization_barrier(held)
    for h, a, k in zip(halvings, arrived, keeps):
        h.arrived, h.keeps = a, k
        h.add()
    return values


PAIRS = HALF_HEADS // 2


def product(terms, a, b):
    return jnp.einsum(terms, a, b, preferred_element_type=F32)


def by_pair(value):
    pairs = [value[:, p * LANES : (p + 1) * LANES] for p in range(PAIRS)]
    return jnp.stack(pairs).reshape(PAIRS, CHUNKS, CHUNK, LANES)


def from_pairs(value):
    return jnp.concatenate([value[p].reshape(TOKENS, LANES) for p in range(PAIRS)], axis=1)


def one_head(value):
    left = iota((2, 1, LANES), 2) // HEADDIM == iota((2, 1, LANES), 0)
    return jnp.where(left, value[:, :, None], jnp.zeros((), value.dtype))


def decays(cl):
    heads = cl[:, :HALF_HEADS].T.reshape(PAIRS, 2, CHUNKS, CHUNK).transpose(0, 2, 1, 3)
    causal = iota((CHUNK, CHUNK), 0) >= iota((CHUNK, CHUNK), 1)
    differ = jnp.where(causal, heads[..., :, None] - heads[..., None, :], 0.0)
    return jnp.where(causal, jnp.exp(differ), 0.0)


def pack_state(state, decay):
    high = rounded(decay)
    middle = rounded(decay - high)
    low = rounded(decay - high - middle)
    at = iota((16, LANES), 0)
    rows = jnp.where(at == 0, high, jnp.where(at == 1, middle, 0.0))
    rows = jnp.where(at == 2, low, rows)
    return jnp.concatenate([state, rows], axis=0).astype(BF16)


def unpack_state(packed):
    rows = packed[HALF : HALF + 3].astype(F32)
    return packed[:HALF].astype(F32), rows[0] + rows[1] + rows[2]


def per_row(head_values):
    heads = head_values[..., :HALF_HEADS, None]
    wide = jnp.broadcast_to(heads, heads.shape[:-1] + (HEADDIM,))
    return wide.reshape(head_values.shape[:-1] + (HALF, 1))


def combine(packed, way, unpack):
    near, far, farthest = [unpack(along_y(packed, way * k)) for k in (1, 2, 3)]
    return near[0] + per_row(near[1]) * (far[0] + per_row(far[1]) * farthest[0])


def pack_full(state, decay):
    return jnp.concatenate([state, jnp.broadcast_to(decay[None], (8, LANES))], axis=0)


def unpack_full(packed):
    return packed[:HALF], packed[HALF]


def chunked(value):
    return value.reshape(CHUNKS, CHUNK, value.shape[-1])


def flat(value):
    return value.reshape(TOKENS, value.shape[-1])


def on_device(
    block_in,
    cotangent,
    in_master,
    in_moment1,
    in_moment2,
    out_master,
    out_moment1,
    out_moment2,
    conv_master,
    conv_moment1,
    conv_moment2,
    gain_master,
    gain_moment1,
    gain_moment2,
    head_master,
    head_moment1,
    head_moment2,
):
    core = lax.axis_index("c")
    x_at = lax.axis_index("x")
    first_core = core == 0
    even_x = x_at % 2 == 0

    def ordered(flag, mine, other, axis=0):
        return jnp.where(
            flag, jnp.concatenate([mine, other], axis=axis), jnp.concatenate([other, mine], axis=axis)
        )

    riders_out = jnp.concatenate(
        [
            jnp.pad(conv_master, ((0, 0), (0, LANES - HALF_HEADS - 26))),
            jnp.pad(gain_master[None], ((0, 6), (0, LANES - HALF_HEADS - 36))),
        ],
        axis=0,
    )

    def half_columns(c):
        return jnp.concatenate(
            [
                in_master[:, INNER + c * HALF : INNER + (c + 1) * HALF],
                in_master[:, 2 * INNER : INNER + CONV],
                in_master[:, INNER + CONV + c * HALF_HEADS : INNER + CONV + (c + 1) * HALF_HEADS],
                riders_out,
                in_master[:, c * HALF : (c + 1) * HALF],
            ],
            axis=1,
        )

    halves = [half_columns(0), half_columns(1)]
    mine = jnp.where(first_core, halves[0], halves[1])
    theirs = jnp.where(first_core, halves[1], halves[0])
    in_rows_low = ordered(first_core, mine, swap_cores(theirs)).astype(BF16)
    out_rows_low = cross_halves(out_master).astype(BF16)
    order_a, order_b = ("y", "z", "x"), ("z", "y", "x")
    block = in_rows_low[:, :CRIT]
    for turn in (1, 0):
        block = jnp.concatenate([block, exchange(block, "x", turn)], axis=0)
    block_a, block_b = block[:, :PART], block[:, PART:]
    for at in (1, 0):
        for turn in (1, 0):
            got_a, got_b = exchange(block_a, order_a[at], turn), exchange(block_b, order_b[at], turn)
            if at or turn:
                block_a = jnp.concatenate([block_a, got_a], axis=0)
                block_b = jnp.concatenate([block_b, got_b], axis=0)
    w_a, w_b = (block_a, got_a), (block_b, got_b)
    rest_low = jnp.concatenate([in_rows_low[:, CRIT:], out_rows_low], axis=1)
    w_rest = lax.all_gather(rest_low, CHIPS, axis=0, tiled=True)
    w_gate = w_rest[:, :HALF]
    w_out = (
        w_rest[:, HALF:]
        .reshape(2, 2, 16, ROWS, WIDTH)
        .transpose(1, 2, 0, 3, 4)
        .reshape(HALF, WIDTH)
    )
    smalls = jnp.concatenate([w[:, ACT - PART :] for w in w_b], axis=0)
    rows_a, rows_b = in_rows(order_a), in_rows(order_b)
    device_at, slot_at = rows_b[:, None] // 12, rows_b[:, None] % 12

    def gather_small(columns, width, slots):
        unfold = (HALF_HEADS + columns % width == iota((LANES, columns.shape[1]), 0)).astype(BF16)
        wide = jnp.where(device_at == columns // width, mm(smalls, unfold), 0.0)
        return mm((slot_at == slots).astype(BF16), wide, TN)

    gain_ab = gather_small(
        jnp.concatenate([rows_a, rows_b])[None], 36, 5 + iota((1, 8), 1)
    )[0]
    norm_gain = gather_small(iota((1, WIDTH), 1), 36, 5 + iota((1, 8), 1))[0]
    gate_gain = gather_small(WIDTH + core * HALF + iota((1, HALF), 1), 36, 5 + iota((1, 8), 1))[0]
    conv_at = iota((1, ACT), 1)
    conv_at = jnp.where(conv_at < HALF, core * HALF + conv_at, INNER - HALF + conv_at)
    conv_weights = gather_small(conv_at, 26, iota((1, 8), 1))
    head_half = jnp.pad(
        lax.dynamic_slice(head_master, (0, core * HALF_HEADS), (3, HALF_HEADS)),
        ((0, 0), (0, LANES - HALF_HEADS)),
    )
    decay_rate = -jnp.exp(head_half[0])

    both = jnp.stack([block_in, cotangent], axis=1)
    flipped = both[::-1]
    got = [regroup(jnp.where(even_x, both, flipped)[k], k) for k in range(2)]
    own_both = ordered(even_x, got[0], got[1], axis=1)
    all_both = ordered(first_core, own_both, swap_cores(own_both), axis=1)
    own_in, own_cot = own_both[0], own_both[1]
    tokens, cot = all_both[0], all_both[1]
    halo = along_y(tokens[TOKENS - HALO :], 1)
    raw = jnp.concatenate([tokens, halo], axis=0)
    pick_a, pick_b = pick(rows_a), pick(rows_b)
    raw_a, raw_b = mm(raw, pick_a, NT), mm(raw, pick_b, NT)
    extended = raw.astype(F32)
    inv = lax.rsqrt(jnp.mean(extended * extended, axis=1, keepdims=True) + NORM_EPS)
    normed = (extended * inv * norm_gain).astype(BF16)
    normed_a = (raw_a * inv * gain_ab[:WIDTH]).astype(BF16)
    normed_b = (raw_b * inv * gain_ab[WIDTH:]).astype(BF16)
    middle = WIDTH // 2

    crit = jnp.concatenate(
        [
            mm(v[:, :middle], w[0]) + mm(v[:, middle:], w[1])
            for v, w in ((normed_a, w_a), (normed_b, w_b))
        ],
        axis=1,
    )
    ext = jnp.concatenate([crit[TOKENS + 8 :, :ACT], crit[:TOKENS, :ACT]], axis=0)
    preact = conv_weights[KERNEL] + sum(
        conv_weights[k] * ext[5 + k : 5 + k + TOKENS] for k in range(KERNEL)
    )
    gate_of_act = sigmoid(preact)
    act = preact * gate_of_act
    head_x = act[:, :HALF]
    bc = act[:, HALF:]
    dt_in = crit[:TOKENS, ACT:] + head_half[1]
    real = iota((1, LANES), 1) < HALF_HEADS
    dt = jnp.where(real, jax.nn.softplus(dt_in), 0.0)
    log_decay = dt * decay_rate
    below = (iota((CHUNK, CHUNK), 0) >= iota((CHUNK, CHUNK), 1)).astype(F32)
    below = jnp.broadcast_to(below[None], (CHUNKS, CHUNK, CHUNK))
    cl = jnp.einsum("kts,ksh->kth", below, chunked(log_decay), precision=EXACT)
    spread = spread_matrix()
    u = head_x * exact(dt, spread)
    u_low = rounded(u)
    lasts = cl[:, -1]
    to_end = flat(jnp.exp(lasts[:, None] - cl))
    cl = flat(cl)
    to_end_wide = exact(to_end, spread)
    from_start_wide = exact(jnp.exp(cl), spread)
    u_wide = u * to_end_wide
    b_proj, c_proj = chunked(bc[:, :STATE]), chunked(bc[:, STATE:])
    b_low, c_low = b_proj.astype(BF16), c_proj.astype(BF16)
    own = jnp.einsum("ktr,ktn->krn", chunked(u_wide), b_proj, precision=PRECISE)
    def between(i, j):
        return per_row(jnp.exp(sum(lasts[i:j])) if j > i else jnp.ones((LANES,), F32))

    local = [jnp.zeros_like(own[0])]
    for k in range(CHUNKS):
        local.append(sum(between(i + 1, k + 1) * own[i] for i in range(k + 1)))
    piece_decay = jnp.exp(jnp.sum(lasts, axis=0))
    incoming = combine(pack_full(local[CHUNKS], piece_decay), 1, unpack_full)
    decay = decays(cl)
    scores = jnp.einsum("ktn,ksn->kts", c_proj, b_proj, precision=PRECISE)
    mixes = (scores[None, :, None] * decay).astype(BF16)
    u_pairs = one_head(by_pair(u_low.astype(BF16)))
    y_chunk = from_pairs(product("pkjts,pkjsc->pktc", mixes, u_pairs))

    starts = jnp.stack([between(0, k) * incoming + local[k] for k in range(CHUNKS)])
    state_end = between(0, CHUNKS) * incoming + local[CHUNKS]
    y_state = flat(jnp.einsum("ktn,krn->ktr", c_proj, starts, precision=PRECISE)) * from_start_wide
    y_ssd = y_chunk + y_state
    skip_wide = exact(head_half[2:3], spread)
    mixed = y_ssd + skip_wide * head_x

    gate = mm(normed[:TOKENS], w_gate)
    gate_sig = sigmoid(gate)
    gate_silu = gate * gate_sig
    (d_gated,) = lax.optimization_barrier((mm(cot, w_out, NT),))
    g = mixed * gate_silu
    e = d_gated * gate_gain
    sums = jnp.concatenate(
        [jnp.sum(g * g, axis=1, keepdims=True), jnp.sum(e * g, axis=1, keepdims=True)], axis=1
    )
    sums = (sums + swap_cores(sums)) / INNER
    r = lax.rsqrt(sums[:, :1] + NORM_EPS)
    gated_low = (g * r * gate_gain).astype(BF16)
    d_g = r * e - (r * r * r) * g * sums[:, 1:]
    d_gate_gain = jnp.sum(d_gated * g * r, axis=0)
    dy = d_g * gate_silu
    d_gate = (d_g * mixed * (gate_sig * (1.0 + gate * (1.0 - gate_sig)))).astype(BF16)
    dy_low = rounded(dy)

    dy_start = chunked(dy * from_start_wide)
    chunk_backs = jnp.einsum("ktr,ktn->krn", dy_start, c_proj, precision=PRECISE)
    back = [None] * CHUNKS
    for k in range(CHUNKS):
        back[k] = sum((between(k + 1, i) * chunk_backs[i] for i in range(k + 1, CHUNKS)), jnp.zeros_like(own[0]))
    to_before = sum(between(0, i) * chunk_backs[i] for i in range(CHUNKS))
    leaving = combine(pack_state(to_before, piece_decay), -1, unpack_state)
    def own_rows(value):
        return jnp.where(first_core, value[:OWN], value[OWN:]), jnp.where(
            first_core, value[OWN:], value[:OWN]
        )

    def to_owner(value):
        low, high = value[:CHUNK], value[CHUNK:]
        sent = [jnp.where(even_x, low, high), jnp.where(even_x, high, low)]
        back0, back1 = regroup(sent[0], 0), regroup(sent[1], 1)
        return jnp.where(even_x, jnp.stack([back0, back1]), jnp.stack([back1, back0]))

    order_gate, order_out = ("x", "z", "y"), ("z", "x", "y")
    normed_gate = mm(pick(in_rows(order_gate)), normed, NT).astype(BF16)
    gated_b = mm(pick(out_rows(order_out)), gated_low, NT).astype(BF16)
    first = Halving(
        [mm(normed_gate[middle:, :TOKENS], d_gate), mm(gated_b[middle:], cot)],
        [mm(normed_gate[:middle, :TOKENS], d_gate), mm(gated_b[:middle], cot)],
        [order_gate, order_out],
    )
    first.start()

    dy_pairs = by_pair(dy_low.astype(BF16))
    du_chunk = from_pairs(product("pkjts,pkjtc->pksc", mixes, one_head(dy_pairs)))
    both = product("pktc,pkjsc->pkjts", dy_pairs, u_pairs)
    d_scores = jnp.sum(decay * both, axis=(0, 2)).astype(BF16)
    db_chunk = product("kts,ktn->ksn", d_scores, c_low)
    dc_chunk = product("kts,ksn->ktn", d_scores, b_low)

    part_out = mm(gated_low, w_out)
    kept, other = own_rows(part_out)
    own_out = own_in.astype(F32) + (kept + swap_cores(other))
    block_out = to_owner(own_out.astype(BF16))

    leaving, du_chunk, db_chunk, dc_chunk = wait([first], leaving, du_chunk, db_chunk, dc_chunk)

    ends = jnp.stack([between(k + 1, CHUNKS) * leaving + back[k] for k in range(CHUNKS)])
    du = du_chunk + flat(jnp.einsum("ktn,krn->ktr", b_proj, ends, precision=PRECISE)) * to_end_wide
    d_b = flat(db_chunk + jnp.einsum("ktr,krn->ktn", chunked(u_wide), ends, precision=PRECISE))
    d_c = flat(dc_chunk + jnp.einsum("ktr,krn->ktn", dy_start, starts, precision=PRECISE))
    du, d_b, d_c = wait([first], du, d_b, d_c)
    d_bc = jnp.concatenate([d_b, d_c], axis=1)
    nexts = jnp.concatenate([starts[1:], state_end[None]], axis=0)
    carries = exact(jnp.sum(ends * nexts, axis=2), spread, NT)
    d_cl = chunked(exact(dy_low * y_ssd - u_low * du, spread, NT))
    d_log_decay = flat(jnp.einsum("kts,kth->ksh", below, d_cl, precision=PRECISE) + carries[:, None])
    d_dt = exact(head_x * du, spread, NT) + d_log_decay * decay_rate
    d_dt_raw = jnp.where(real, d_dt * sigmoid(dt_in), 0.0)
    d_head = jnp.stack(
        [
            jnp.sum(d_log_decay * log_decay, axis=0),
            jnp.sum(d_dt_raw, axis=0),
            exact(jnp.sum(dy * head_x, axis=0, keepdims=True), spread, NT)[0],
        ]
    )
    d_x = exact(dt, spread) * du + skip_wide * dy
    d_act = jnp.concatenate([d_x, d_bc], axis=1)
    d_pre = d_act * (gate_of_act * (1.0 + preact * (1.0 - gate_of_act)))
    (d_pre,) = wait([first], d_pre)
    d_ext = sum(
        conv_weights[k] * jnp.pad(d_pre, ((5 + k, 3 - k), (0, 0))) for k in range(KERNEL)
    )
    d_conv = jnp.where(iota((8, ACT), 0) == KERNEL, jnp.sum(d_pre, axis=0)[None], 0.0)
    for k in range(KERNEL):
        tap = jnp.sum(d_pre * ext[5 + k : 5 + k + TOKENS], axis=0)
        d_conv = jnp.where(iota((8, ACT), 0) == k, tap[None], d_conv)
    d_ext = jnp.concatenate([d_ext[8:], jnp.zeros((8, ACT), F32), d_ext[:8]], axis=0)
    d_crit = jnp.concatenate(
        [d_ext, jnp.pad(d_dt_raw, ((0, HALO), (0, 0)))], axis=1
    ).astype(BF16)
    (d_crit,) = wait([first], d_crit)

    device_of, slot_of = device_at, slot_at
    slot_pick = (slot_of == iota((1536, 8), 1)).astype(F32)
    conv_spread = jnp.where(conv_at // 26 == device_of, exact(slot_pick, d_conv), 0.0)
    fold = (conv_at.T % 26 + HALF_HEADS == iota((ACT, LANES), 1)).astype(BF16)
    gain_at = WIDTH + core * HALF + iota((1536, HALF), 1)
    gain_spread = jnp.where((gain_at // 36 == device_of) & (slot_of == 5), d_gate_gain[None, :], 0.0)
    gain_fold = (
        (WIDTH + core * HALF + iota((HALF, LANES), 0)) % 36 + HALF_HEADS == iota((HALF, LANES), 1)
    ).astype(BF16)
    riders = mm(conv_spread, fold) + mm(gain_spread, gain_fold)

    crit_b = jnp.concatenate([d_crit[:, PART:]], axis=1)

    def part_b(rows):
        with_riders = jnp.pad(riders[rows], ((0, 0), (CRIT - PART - LANES, 0)))
        return mm(normed_b[:, rows], crit_b, TN) + with_riders

    second = Halving(
        [mm(normed_a[:, middle:], d_crit[:, :PART], TN), part_b(slice(middle, None))],
        [mm(normed_a[:, :middle], d_crit[:, :PART], TN), part_b(slice(0, middle))],
        [order_a, order_b],
    )

    second.sends, d_crit_late = lax.optimization_barrier((second.sends, d_crit))
    second.start()
    d_normed = 0.0
    for part, w, choose in (
        (d_crit_late[:, :PART], w_a, pick_a),
        (d_crit_late[:, PART:], w_b, pick_b),
    ):
        there = jnp.concatenate([mm(part, w[0], NT), mm(part, w[1], NT)], axis=1)
        high = rounded(there)
        d_normed = d_normed + mm(high, choose) + mm(there - high, choose)
    d_halo = along_y(d_normed[TOKENS:], -1)
    d_normed = d_normed[:TOKENS] + mm(d_gate, w_gate, NT)
    d_normed = jnp.concatenate(
        [d_normed[: TOKENS - HALO], d_normed[TOKENS - HALO :] + d_halo], axis=0
    )
    kept, other = own_rows(d_normed)
    d_own = kept + swap_cores(other)
    own = own_in.astype(F32)
    own_inv = lax.rsqrt(jnp.mean(own * own, axis=1, keepdims=True) + NORM_EPS)
    d_own = d_own * norm_gain
    d_tokens = own_inv * d_own - (own_inv * own_inv * own_inv) * own * jnp.mean(
        own * d_own, axis=1, keepdims=True
    )
    input_grad = to_owner((own_cot.astype(F32) + d_tokens).astype(BF16))

    head_own = jnp.pad(d_head, ((0, 5), (0, 0)))
    for step in range(6):
        head_got = exchange(head_own, CHIPS[step // 2], step % 2)
        head_own, head_got = wait([second, first] if step < 2 else [second], head_own, head_got)
        head_own = head_own + head_got
        if step == 4:
            head_own, input_grad = lax.optimization_barrier((head_own, input_grad))
    input_grad = input_grad.astype(F32)
    head_other = swap_cores(head_own)
    share_a, share_b = second.totals
    gate_rows, out_rows_grad = first.totals

    rows = jnp.concatenate([share_a, share_b, gate_rows], axis=1)
    mine = jnp.where(first_core, rows[:12], rows[12:])
    theirs = jnp.where(first_core, rows[12:], rows[:12])
    theirs = swap_cores(theirs)
    h0 = jnp.where(first_core, mine, theirs)
    h1 = jnp.where(first_core, theirs, mine)
    in_share = jnp.concatenate(
        [
            h0[:, CRIT:],
            h1[:, CRIT:],
            h0[:, :HALF],
            h1[:, :HALF],
            h0[:, HALF:ACT] + h1[:, HALF:ACT],
            h0[:, ACT : ACT + HALF_HEADS],
            h1[:, ACT : ACT + HALF_HEADS],
        ],
        axis=1,
    )
    riding = h0[:, ACT + HALF_HEADS : CRIT] + h1[:, ACT + HALF_HEADS : CRIT]
    conv_share = riding[:5, :26]
    out_share = cross_halves(out_rows_grad)
    at_device = ((lax.axis_index("y") * 4 + x_at) * 4 + lax.axis_index("z")) * 2 + core
    w_own = rounded(in_master)
    own_gain = lax.dynamic_slice(norm_gain, (at_device * 12,), (12,))
    gain_rows = jnp.sum(w_own * in_share, axis=1) / own_gain
    thirds = [
        lax.ppermute(gain_rows, ALL, [(3 * d + k, d) for d in range(128) if 3 * d + k < 128])
        for k in range(3)
    ]
    gain_share = jnp.concatenate(thirds) + riding[5, :36]
    head_share = ordered(
        first_core, head_own[:3, :HALF_HEADS], head_other[:3, :HALF_HEADS], axis=1
    )

    in_next = adamw_step(in_master, in_share, in_moment1, in_moment2, MATRIX_RATE, MATRIX_DECAY)
    out_next = adamw_step(
        out_master, out_share, out_moment1, out_moment2, MATRIX_RATE, MATRIX_DECAY
    )
    conv_next = adamw_step(conv_master, conv_share, conv_moment1, conv_moment2, SMALL_RATE, 0.0)
    gain_next = adamw_step(gain_master, gain_share, gain_moment1, gain_moment2, SMALL_RATE, 0.0)
    head_next = adamw_step(head_master, head_share, head_moment1, head_moment2, SMALL_RATE, 0.0)
    return (
        block_out,
        input_grad,
        *in_next,
        *out_next,
        *conv_next,
        *gain_next,
        *head_next,
    )


def solution(mesh):
    fine = Mesh(mesh.devices.reshape(4, 4, 4, 2), ALL)
    tokens = P(("z", "c"), ("y", "x"), None)
    rows = P(ALL, None)
    columns = P(None, ALL)
    flat = P(ALL)
    return jax.shard_map(
        on_device,
        mesh=fine,
        in_specs=(tokens, tokens) + (rows,) * 6 + (columns,) * 3 + (flat,) * 3 + (P(),) * 3,
        out_specs=(tokens, tokens) + (rows,) * 6 + (columns,) * 3 + (flat,) * 3 + (P(),) * 3,
        check_vma=False,
    )
```

```python
import jax
import jax.numpy as jnp
from jax import lax
from jax.sharding import Mesh
from jax.sharding import PartitionSpec as P

WIDTH = 1536
INNER = 3072
STATE = 128
HEADDIM = 64
KERNEL = 4
STEP = 5
HEADS = 48
CONV = 3328
PROJ = 6448

HALF = INNER // 2
HALF_HEADS = HEADS // 2
TOKENS = 512
OWN = TOKENS // 2
HALO = 16
ROWS_IN = TOKENS + HALO
CHUNK = 128
CHUNKS = TOKENS // CHUNK
LANES = 128
ACT = HALF + 2 * STATE
CRIT = ACT + LANES
PART = 1024
ROWS = 24

NORM_EPS = 1e-05
PRECISE = lax.Precision.HIGH
EXACT = lax.Precision.HIGHEST
BETA_ONE = 0.9
BETA_TWO = 0.95
ADAM_EPS = 1e-08
MATRIX_RATE = 0.05
SMALL_RATE = 0.5
MATRIX_DECAY = 0.1
BF16 = jnp.bfloat16
F32 = jnp.float32
CHIPS = ("y", "x", "z")
ALL = ("y", "x", "z", "c")


def mm(a, b, dims=((1,), (0,))):
    return lax.dot_general(
        a.astype(BF16), b.astype(BF16), (dims, ((), ())), preferred_element_type=F32
    )


def exact(a, b, dims=((1,), (0,))):
    return lax.dot_general(a, b, (dims, ((), ())), precision=PRECISE, preferred_element_type=F32)


NT = ((1,), (1,))
TN = ((0,), (0,))


def rounded(v):
    return lax.reduce_precision(v, 8, 7)


def iota(shape, dim):
    return lax.broadcasted_iota(jnp.int32, shape, dim)


def sigmoid(v):
    return 1.0 / (1.0 + jnp.exp(-v))


def spread_matrix():
    return (iota((LANES, HALF), 1) // HEADDIM == iota((LANES, HALF), 0)).astype(F32)


def adamw_step(weight, gradient, moment_one, moment_two, step_rate, weight_decay):
    one_next = BETA_ONE * moment_one + (1.0 - BETA_ONE) * gradient
    two_next = BETA_TWO * moment_two + (1.0 - BETA_TWO) * gradient * gradient
    corrected = one_next / (1.0 - BETA_ONE**STEP)
    scale_next = jnp.sqrt(two_next / (1.0 - BETA_TWO**STEP)) + ADAM_EPS
    weight_next = weight - step_rate * (corrected / scale_next + weight_decay * weight)
    return (one_next, two_next, weight_next)


def swap_cores(value):
    return lax.ppermute(value, "c", [(0, 1), (1, 0)])


def regroup(value, turn):
    pairs = [
        (x * 2 + c, (2 * c + (x + turn) % 2) * 2 + x // 2) for x in range(4) for c in range(2)
    ]
    return lax.ppermute(value, ("x", "c"), pairs)


def cross_halves(value):
    pairs = []
    for y in range(4):
        for c in range(2):
            to = (y, c) if y // 2 == c else (y ^ 2, 1 - c)
            pairs.append((y * 2 + c, to[0] * 2 + to[1]))
    return lax.ppermute(value, ("y", "c"), pairs)


def along_y(value, steps):
    return lax.ppermute(value, "y", [(y, y + steps) for y in range(4) if 0 <= y + steps < 4])


def partner(axis, turn):
    pairs = []
    for i in range(4):
        for c in range(2):
            pairs.append((i * 2 + c, (i ^ (1 if (turn + c) % 2 == 0 else 3)) * 2 + c))
    return (axis, "c"), pairs


def exchange(value, axis, turn):
    axes, pairs = partner(axis, turn)
    return lax.ppermute(value, axes, pairs)


def block_order(order):
    first = jnp.where(lax.axis_index("c") == 0, 1, 3)
    second = 4 - first
    block = jnp.arange(64)
    place = {a: lax.axis_index(a) for a in CHIPS}
    for at, axis in enumerate(order):
        high = (block >> (5 - 2 * at)) & 1
        low = (block >> (4 - 2 * at)) & 1
        place[axis] = place[axis] ^ (high * first) ^ (low * second)
    return [place[a] + jnp.zeros((64,), jnp.int32) for a in CHIPS]


def rows_of(blocks):
    return (blocks[:, None] * ROWS + jnp.arange(ROWS)[None, :]).reshape(-1)


def in_rows(order):
    y, x, z = block_order(order)
    return rows_of((y * 4 + x) * 4 + z)


def out_rows(order):
    y, x, z = block_order(order)
    return rows_of((((y % 2) * 4 + x) * 4 + z) * 2 + y // 2)


def pick(rows):
    return (rows[:, None] == iota((1536, 1536), 1)).astype(BF16)


class Halving:
    def __init__(self, sends, keeps, orders):
        self.sends = [v.astype(BF16) for v in sends]
        self.keeps, self.orders, self.step = keeps, orders, 0

    def start(self):
        self.arrived = [
            exchange(v, order[self.step // 2], self.step % 2)
            for v, order in zip(self.sends, self.orders)
        ]

    def add(self):
        totals = [keep + got.astype(F32) for keep, got in zip(self.keeps, self.arrived)]
        self.step += 1
        if self.step == 6:
            self.totals = totals
            return
        half = totals[0].shape[0] // 2
        self.sends = [t[half:].astype(BF16) for t in totals]
        self.keeps = [t[:half] for t in totals]
        self.start()


def wait(halvings, *values):
    held = [h.arrived for h in halvings], [h.keeps for h in halvings], values
    arrived, keeps, values = lax.optimization_barrier(held)
    for h, a, k in zip(halvings, arrived, keeps):
        h.arrived, h.keeps = a, k
        h.add()
    return values


PAIRS = HALF_HEADS // 2


def product(terms, a, b):
    return jnp.einsum(terms, a, b, preferred_element_type=F32)


def by_pair(value):
    pairs = [value[:, p * LANES : (p + 1) * LANES] for p in range(PAIRS)]
    return jnp.stack(pairs).reshape(PAIRS, CHUNKS, CHUNK, LANES)


def from_pairs(value):
    return jnp.concatenate([value[p].reshape(TOKENS, LANES) for p in range(PAIRS)], axis=1)


def one_head(value):
    left = iota((2, 1, LANES), 2) // HEADDIM == iota((2, 1, LANES), 0)
    return jnp.where(left, value[:, :, None], jnp.zeros((), value.dtype))


def decays(cl):
    heads = cl[:, :HALF_HEADS].T.reshape(PAIRS, 2, CHUNKS, CHUNK).transpose(0, 2, 1, 3)
    causal = iota((CHUNK, CHUNK), 0) >= iota((CHUNK, CHUNK), 1)
    differ = jnp.where(causal, heads[..., :, None] - heads[..., None, :], 0.0)
    return jnp.where(causal, jnp.exp(differ), 0.0)


def pack_state(state, decay):
    high = rounded(decay)
    middle = rounded(decay - high)
    low = rounded(decay - high - middle)
    at = iota((16, LANES), 0)
    rows = jnp.where(at == 0, high, jnp.where(at == 1, middle, 0.0))
    rows = jnp.where(at == 2, low, rows)
    return jnp.concatenate([state, rows], axis=0).astype(BF16)


def unpack_state(packed):
    rows = packed[HALF : HALF + 3].astype(F32)
    return packed[:HALF].astype(F32), rows[0] + rows[1] + rows[2]


def per_row(head_values):
    heads = head_values[..., :HALF_HEADS, None]
    wide = jnp.broadcast_to(heads, heads.shape[:-1] + (HEADDIM,))
    return wide.reshape(head_values.shape[:-1] + (HALF, 1))


def combine(packed, way, unpack):
    near, far, farthest = [unpack(along_y(packed, way * k)) for k in (1, 2, 3)]
    return near[0] + per_row(near[1]) * (far[0] + per_row(far[1]) * farthest[0])


def pack_full(state, decay):
    return jnp.concatenate([state, jnp.broadcast_to(decay[None], (8, LANES))], axis=0)


def unpack_full(packed):
    return packed[:HALF], packed[HALF]


def chunked(value):
    return value.reshape(CHUNKS, CHUNK, value.shape[-1])


def flat(value):
    return value.reshape(TOKENS, value.shape[-1])


def on_device(
    block_in,
    cotangent,
    in_master,
    in_moment1,
    in_moment2,
    out_master,
    out_moment1,
    out_moment2,
    conv_master,
    conv_moment1,
    conv_moment2,
    gain_master,
    gain_moment1,
    gain_moment2,
    head_master,
    head_moment1,
    head_moment2,
):
    core = lax.axis_index("c")
    x_at = lax.axis_index("x")
    first_core = core == 0
    even_x = x_at % 2 == 0

    def ordered(flag, mine, other, axis=0):
        return jnp.where(
            flag, jnp.concatenate([mine, other], axis=axis), jnp.concatenate([other, mine], axis=axis)
        )

    riders_out = jnp.concatenate(
        [
            jnp.pad(conv_master, ((0, 0), (0, LANES - HALF_HEADS - 26))),
            jnp.pad(gain_master[None], ((0, 6), (0, LANES - HALF_HEADS - 36))),
        ],
        axis=0,
    )

    def half_columns(c):
        return jnp.concatenate(
            [
                in_master[:, INNER + c * HALF : INNER + (c + 1) * HALF],
                in_master[:, 2 * INNER : INNER + CONV],
                in_master[:, INNER + CONV + c * HALF_HEADS : INNER + CONV + (c + 1) * HALF_HEADS],
                riders_out,
                in_master[:, c * HALF : (c + 1) * HALF],
            ],
            axis=1,
        )

    halves = [half_columns(0), half_columns(1)]
    mine = jnp.where(first_core, halves[0], halves[1])
    theirs = jnp.where(first_core, halves[1], halves[0])
    in_rows_low = ordered(first_core, mine, swap_cores(theirs)).astype(BF16)
    out_rows_low = cross_halves(out_master).astype(BF16)
    w_in = lax.all_gather(in_rows_low, CHIPS, axis=0, tiled=True)
    w_crit = w_in[:, :CRIT]
    w_gate = w_in[:, CRIT:]
    w_out = (
        lax.all_gather(out_rows_low, CHIPS, axis=0, tiled=True)
        .reshape(2, 2, 16, ROWS, WIDTH)
        .transpose(1, 2, 0, 3, 4)
        .reshape(HALF, WIDTH)
    )
    smalls = w_crit[:, ACT:]
    device_at, slot_at = iota((1536, 1), 0) // 12, iota((1536, 1), 0) % 12

    def gather_small(columns, width, slots):
        unfold = (HALF_HEADS + columns % width == iota((LANES, columns.shape[1]), 0)).astype(BF16)
        wide = jnp.where(device_at == columns // width, mm(smalls, unfold), 0.0)
        return mm((slot_at == slots).astype(BF16), wide, TN)

    norm_gain = gather_small(iota((1, WIDTH), 1), 36, 5 + iota((1, 8), 1))[0]
    gate_gain = gather_small(WIDTH + core * HALF + iota((1, HALF), 1), 36, 5 + iota((1, 8), 1))[0]
    conv_at = iota((1, ACT), 1)
    conv_at = jnp.where(conv_at < HALF, core * HALF + conv_at, INNER - HALF + conv_at)
    conv_weights = gather_small(conv_at, 26, iota((1, 8), 1))
    head_half = jnp.pad(
        lax.dynamic_slice(head_master, (0, core * HALF_HEADS), (3, HALF_HEADS)),
        ((0, 0), (0, LANES - HALF_HEADS)),
    )
    decay_rate = -jnp.exp(head_half[0])

    both = jnp.stack([block_in, cotangent], axis=1)
    flipped = both[::-1]
    got = [regroup(jnp.where(even_x, both, flipped)[k], k) for k in range(2)]
    own_both = ordered(even_x, got[0], got[1], axis=1)
    all_both = ordered(first_core, own_both, swap_cores(own_both), axis=1)
    own_in, own_cot = own_both[0], own_both[1]
    tokens, cot = all_both[0], all_both[1]
    halo = along_y(tokens[TOKENS - HALO :], 1)
    extended = jnp.concatenate([tokens, halo], axis=0).astype(F32)
    inv = lax.rsqrt(jnp.mean(extended * extended, axis=1, keepdims=True) + NORM_EPS)
    normed = (extended * inv * norm_gain).astype(BF16)

    crit = mm(normed, w_crit)
    ext = jnp.concatenate([crit[TOKENS + 8 :, :ACT], crit[:TOKENS, :ACT]], axis=0)
    preact = conv_weights[KERNEL] + sum(
        conv_weights[k] * ext[5 + k : 5 + k + TOKENS] for k in range(KERNEL)
    )
    gate_of_act = sigmoid(preact)
    act = preact * gate_of_act
    head_x = act[:, :HALF]
    bc = act[:, HALF:]
    dt_in = crit[:TOKENS, ACT:] + head_half[1]
    real = iota((1, LANES), 1) < HALF_HEADS
    dt = jnp.where(real, jax.nn.softplus(dt_in), 0.0)
    log_decay = dt * decay_rate
    below = (iota((CHUNK, CHUNK), 0) >= iota((CHUNK, CHUNK), 1)).astype(F32)
    below = jnp.broadcast_to(below[None], (CHUNKS, CHUNK, CHUNK))
    cl = jnp.einsum("kts,ksh->kth", below, chunked(log_decay), precision=EXACT)
    spread = spread_matrix()
    u = head_x * exact(dt, spread)
    u_low = rounded(u)
    lasts = cl[:, -1]
    to_end = flat(jnp.exp(lasts[:, None] - cl))
    cl = flat(cl)
    to_end_wide = exact(to_end, spread)
    from_start_wide = exact(jnp.exp(cl), spread)
    u_wide = u * to_end_wide
    b_proj, c_proj = chunked(bc[:, :STATE]), chunked(bc[:, STATE:])
    b_low, c_low = b_proj.astype(BF16), c_proj.astype(BF16)
    own = jnp.einsum("ktr,ktn->krn", chunked(u_wide), b_proj, precision=PRECISE)
    def between(i, j):
        return per_row(jnp.exp(sum(lasts[i:j])) if j > i else jnp.ones((LANES,), F32))

    local = [jnp.zeros_like(own[0])]
    for k in range(CHUNKS):
        local.append(sum(between(i + 1, k + 1) * own[i] for i in range(k + 1)))
    piece_decay = jnp.exp(jnp.sum(lasts, axis=0))
    incoming = combine(pack_full(local[CHUNKS], piece_decay), 1, unpack_full)
    decay = decays(cl)
    scores = jnp.einsum("ktn,ksn->kts", c_proj, b_proj, precision=PRECISE)
    mixes = (scores[None, :, None] * decay).astype(BF16)
    u_pairs = one_head(by_pair(u_low.astype(BF16)))
    y_chunk = from_pairs(product("pkjts,pkjsc->pktc", mixes, u_pairs))

    starts = jnp.stack([between(0, k) * incoming + local[k] for k in range(CHUNKS)])
    state_end = between(0, CHUNKS) * incoming + local[CHUNKS]
    y_state = flat(jnp.einsum("ktn,krn->ktr", c_proj, starts, precision=PRECISE)) * from_start_wide
    y_ssd = y_chunk + y_state
    skip_wide = exact(head_half[2:3], spread)
    mixed = y_ssd + skip_wide * head_x

    gate = mm(normed[:TOKENS], w_gate)
    gate_sig = sigmoid(gate)
    gate_silu = gate * gate_sig
    (d_gated,) = lax.optimization_barrier((mm(cot, w_out, NT),))
    g = mixed * gate_silu
    e = d_gated * gate_gain
    sums = jnp.concatenate(
        [jnp.sum(g * g, axis=1, keepdims=True), jnp.sum(e * g, axis=1, keepdims=True)], axis=1
    )
    sums = (sums + swap_cores(sums)) / INNER
    r = lax.rsqrt(sums[:, :1] + NORM_EPS)
    gated_low = (g * r * gate_gain).astype(BF16)
    d_g = r * e - (r * r * r) * g * sums[:, 1:]
    d_gate_gain = jnp.sum(d_gated * g * r, axis=0)
    dy = d_g * gate_silu
    d_gate = (d_g * mixed * (gate_sig * (1.0 + gate * (1.0 - gate_sig)))).astype(BF16)
    dy_low = rounded(dy)

    dy_start = chunked(dy * from_start_wide)
    chunk_backs = jnp.einsum("ktr,ktn->krn", dy_start, c_proj, precision=PRECISE)
    back = [None] * CHUNKS
    for k in range(CHUNKS):
        back[k] = sum((between(k + 1, i) * chunk_backs[i] for i in range(k + 1, CHUNKS)), jnp.zeros_like(own[0]))
    to_before = sum(between(0, i) * chunk_backs[i] for i in range(CHUNKS))
    leaving = combine(pack_state(to_before, piece_decay), -1, unpack_state)
    def own_rows(value):
        return jnp.where(first_core, value[:OWN], value[OWN:]), jnp.where(
            first_core, value[OWN:], value[:OWN]
        )

    def to_owner(value):
        low, high = value[:CHUNK], value[CHUNK:]
        sent = [jnp.where(even_x, low, high), jnp.where(even_x, high, low)]
        back0, back1 = regroup(sent[0], 0), regroup(sent[1], 1)
        return jnp.where(even_x, jnp.stack([back0, back1]), jnp.stack([back1, back0]))

    order_gate, order_out = ("x", "z", "y"), ("z", "x", "y")
    order_a, order_b = ("y", "z", "x"), ("z", "y", "x")
    normed_gate = mm(pick(in_rows(order_gate)), normed, NT).astype(BF16)
    normed_a = mm(pick(in_rows(order_a)), normed, NT).astype(BF16)
    normed_b = mm(pick(in_rows(order_b)), normed, NT).astype(BF16)
    gated_b = mm(pick(out_rows(order_out)), gated_low, NT).astype(BF16)
    middle = WIDTH // 2
    first = Halving(
        [mm(normed_gate[middle:, :TOKENS], d_gate), mm(gated_b[middle:], cot)],
        [mm(normed_gate[:middle, :TOKENS], d_gate), mm(gated_b[:middle], cot)],
        [order_gate, order_out],
    )
    first.start()

    dy_pairs = by_pair(dy_low.astype(BF16))
    du_chunk = from_pairs(product("pkjts,pkjtc->pksc", mixes, one_head(dy_pairs)))
    both = product("pktc,pkjsc->pkjts", dy_pairs, u_pairs)
    d_scores = jnp.sum(decay * both, axis=(0, 2)).astype(BF16)
    db_chunk = product("kts,ktn->ksn", d_scores, c_low)
    dc_chunk = product("kts,ksn->ktn", d_scores, b_low)

    part_out = mm(gated_low, w_out)
    kept, other = own_rows(part_out)
    own_out = own_in.astype(F32) + (kept + swap_cores(other))
    block_out = to_owner(own_out.astype(BF16))

    leaving, du_chunk, db_chunk, dc_chunk = wait([first], leaving, du_chunk, db_chunk, dc_chunk)

    ends = jnp.stack([between(k + 1, CHUNKS) * leaving + back[k] for k in range(CHUNKS)])
    du = du_chunk + flat(jnp.einsum("ktn,krn->ktr", b_proj, ends, precision=PRECISE)) * to_end_wide
    d_b = flat(db_chunk + jnp.einsum("ktr,krn->ktn", chunked(u_wide), ends, precision=PRECISE))
    d_c = flat(dc_chunk + jnp.einsum("ktr,krn->ktn", dy_start, starts, precision=PRECISE))
    du, d_b, d_c = wait([first], du, d_b, d_c)
    d_bc = jnp.concatenate([d_b, d_c], axis=1)
    nexts = jnp.concatenate([starts[1:], state_end[None]], axis=0)
    carries = exact(jnp.sum(ends * nexts, axis=2), spread, NT)
    d_cl = chunked(exact(dy_low * y_ssd - u_low * du, spread, NT))
    d_log_decay = flat(jnp.einsum("kts,kth->ksh", below, d_cl, precision=PRECISE) + carries[:, None])
    d_dt = exact(head_x * du, spread, NT) + d_log_decay * decay_rate
    d_dt_raw = jnp.where(real, d_dt * sigmoid(dt_in), 0.0)
    d_head = jnp.stack(
        [
            jnp.sum(d_log_decay * log_decay, axis=0),
            jnp.sum(d_dt_raw, axis=0),
            exact(jnp.sum(dy * head_x, axis=0, keepdims=True), spread, NT)[0],
        ]
    )
    d_x = exact(dt, spread) * du + skip_wide * dy
    d_act = jnp.concatenate([d_x, d_bc], axis=1)
    d_pre = d_act * (gate_of_act * (1.0 + preact * (1.0 - gate_of_act)))
    (d_pre,) = wait([first], d_pre)
    d_ext = sum(
        conv_weights[k] * jnp.pad(d_pre, ((5 + k, 3 - k), (0, 0))) for k in range(KERNEL)
    )
    d_conv = jnp.where(iota((8, ACT), 0) == KERNEL, jnp.sum(d_pre, axis=0)[None], 0.0)
    for k in range(KERNEL):
        tap = jnp.sum(d_pre * ext[5 + k : 5 + k + TOKENS], axis=0)
        d_conv = jnp.where(iota((8, ACT), 0) == k, tap[None], d_conv)
    d_ext = jnp.concatenate([d_ext[8:], jnp.zeros((8, ACT), F32), d_ext[:8]], axis=0)
    d_crit = jnp.concatenate(
        [d_ext, jnp.pad(d_dt_raw, ((0, HALO), (0, 0)))], axis=1
    ).astype(BF16)
    (d_crit,) = wait([first], d_crit)

    y_of, x_of, z_of = block_order(order_b)
    row_at = rows_of((y_of * 4 + x_of) * 4 + z_of)[:, None]
    device_of, slot_of = row_at // 12, row_at % 12
    slot_pick = (slot_of == iota((1536, 8), 1)).astype(F32)
    conv_spread = jnp.where(conv_at // 26 == device_of, exact(slot_pick, d_conv), 0.0)
    fold = (conv_at.T % 26 + HALF_HEADS == iota((ACT, LANES), 1)).astype(BF16)
    gain_at = WIDTH + core * HALF + iota((1536, HALF), 1)
    gain_spread = jnp.where((gain_at // 36 == device_of) & (slot_of == 5), d_gate_gain[None, :], 0.0)
    gain_fold = (
        (WIDTH + core * HALF + iota((HALF, LANES), 0)) % 36 + HALF_HEADS == iota((HALF, LANES), 1)
    ).astype(BF16)
    riders = mm(conv_spread, fold) + mm(gain_spread, gain_fold)

    crit_b = jnp.concatenate([d_crit[:, PART:]], axis=1)

    def part_b(rows):
        with_riders = jnp.pad(riders[rows], ((0, 0), (CRIT - PART - LANES, 0)))
        return mm(normed_b[rows], crit_b) + with_riders

    second = Halving(
        [mm(normed_a[middle:], d_crit[:, :PART]), part_b(slice(middle, None))],
        [mm(normed_a[:middle], d_crit[:, :PART]), part_b(slice(0, middle))],
        [order_a, order_b],
    )

    second.sends, d_crit_late = lax.optimization_barrier((second.sends, d_crit))
    second.start()
    d_normed = mm(d_crit_late, w_crit, NT)
    d_halo = along_y(d_normed[TOKENS:], -1)
    d_normed = d_normed[:TOKENS] + mm(d_gate, w_gate, NT)
    d_normed = jnp.concatenate(
        [d_normed[: TOKENS - HALO], d_normed[TOKENS - HALO :] + d_halo], axis=0
    )
    kept, other = own_rows(d_normed)
    d_own = kept + swap_cores(other)
    own = own_in.astype(F32)
    own_inv = lax.rsqrt(jnp.mean(own * own, axis=1, keepdims=True) + NORM_EPS)
    d_own = d_own * norm_gain
    d_tokens = own_inv * d_own - (own_inv * own_inv * own_inv) * own * jnp.mean(
        own * d_own, axis=1, keepdims=True
    )
    input_grad = to_owner((own_cot.astype(F32) + d_tokens).astype(BF16))

    head_own = jnp.pad(d_head, ((0, 5), (0, 0)))
    for step in range(6):
        head_got = exchange(head_own, CHIPS[step // 2], step % 2)
        head_own, head_got = wait([second, first] if step < 2 else [second], head_own, head_got)
        head_own = head_own + head_got
    head_other = swap_cores(head_own)
    rows_a, rows_b = second.totals
    gate_rows, out_rows_grad = first.totals

    rows = jnp.concatenate([rows_a, rows_b, gate_rows], axis=1)
    mine = jnp.where(first_core, rows[:12], rows[12:])
    theirs = jnp.where(first_core, rows[12:], rows[:12])
    theirs, input_grad = lax.optimization_barrier((swap_cores(theirs), input_grad))
    input_grad = input_grad.astype(F32)
    h0 = jnp.where(first_core, mine, theirs)
    h1 = jnp.where(first_core, theirs, mine)
    in_share = jnp.concatenate(
        [
            h0[:, CRIT:],
            h1[:, CRIT:],
            h0[:, :HALF],
            h1[:, :HALF],
            h0[:, HALF:ACT] + h1[:, HALF:ACT],
            h0[:, ACT : ACT + HALF_HEADS],
            h1[:, ACT : ACT + HALF_HEADS],
        ],
        axis=1,
    )
    riding = h0[:, ACT + HALF_HEADS : CRIT] + h1[:, ACT + HALF_HEADS : CRIT]
    conv_share = riding[:5, :26]
    out_share = cross_halves(out_rows_grad)
    at_device = ((lax.axis_index("y") * 4 + x_at) * 4 + lax.axis_index("z")) * 2 + core
    w_own = rounded(in_master)
    own_gain = lax.dynamic_slice(norm_gain, (at_device * 12,), (12,))
    gain_rows = jnp.sum(w_own * in_share, axis=1) / own_gain
    thirds = [
        lax.ppermute(gain_rows, ALL, [(3 * d + k, d) for d in range(128) if 3 * d + k < 128])
        for k in range(3)
    ]
    gain_share = jnp.concatenate(thirds) + riding[5, :36]
    head_share = ordered(
        first_core, head_own[:3, :HALF_HEADS], head_other[:3, :HALF_HEADS], axis=1
    )

    in_next = adamw_step(in_master, in_share, in_moment1, in_moment2, MATRIX_RATE, MATRIX_DECAY)
    out_next = adamw_step(
        out_master, out_share, out_moment1, out_moment2, MATRIX_RATE, MATRIX_DECAY
    )
    conv_next = adamw_step(conv_master, conv_share, conv_moment1, conv_moment2, SMALL_RATE, 0.0)
    gain_next = adamw_step(gain_master, gain_share, gain_moment1, gain_moment2, SMALL_RATE, 0.0)
    head_next = adamw_step(head_master, head_share, head_moment1, head_moment2, SMALL_RATE, 0.0)
    return (
        block_out,
        input_grad,
        *in_next,
        *out_next,
        *conv_next,
        *gain_next,
        *head_next,
    )


def solution(mesh):
    fine = Mesh(mesh.devices.reshape(4, 4, 4, 2), ALL)
    tokens = P(("z", "c"), ("y", "x"), None)
    rows = P(ALL, None)
    columns = P(None, ALL)
    flat = P(ALL)
    return jax.shard_map(
        on_device,
        mesh=fine,
        in_specs=(tokens, tokens) + (rows,) * 6 + (columns,) * 3 + (flat,) * 3 + (P(),) * 3,
        out_specs=(tokens, tokens) + (rows,) * 6 + (columns,) * 3 + (flat,) * 3 + (P(),) * 3,
        check_vma=False,
    )
```

```python
import jax
import jax.numpy as jnp
from jax import lax
from jax.sharding import Mesh
from jax.sharding import PartitionSpec as P

WIDTH = 1536
INNER = 3072
STATE = 128
HEADDIM = 64
KERNEL = 4
STEP = 5
HEADS = 48
CONV = 3328
PROJ = 6448

HALF = INNER // 2
HALF_HEADS = HEADS // 2
TOKENS = 512
OWN = TOKENS // 2
HALO = 16
ROWS_IN = TOKENS + HALO
CHUNK = 128
CHUNKS = TOKENS // CHUNK
LANES = 128
ACT = HALF + 2 * STATE
CRIT = ACT + LANES
PART = 1024
ROWS = 24

NORM_EPS = 1e-05
PRECISE = lax.Precision.HIGH
EXACT = lax.Precision.HIGHEST
BETA_ONE = 0.9
BETA_TWO = 0.95
ADAM_EPS = 1e-08
MATRIX_RATE = 0.05
SMALL_RATE = 0.5
MATRIX_DECAY = 0.1
BF16 = jnp.bfloat16
F32 = jnp.float32
CHIPS = ("y", "x", "z")
ALL = ("y", "x", "z", "c")


def mm(a, b, dims=((1,), (0,))):
    return lax.dot_general(
        a.astype(BF16), b.astype(BF16), (dims, ((), ())), preferred_element_type=F32
    )


def exact(a, b, dims=((1,), (0,))):
    return lax.dot_general(a, b, (dims, ((), ())), precision=PRECISE, preferred_element_type=F32)


NT = ((1,), (1,))
TN = ((0,), (0,))


def rounded(v):
    return lax.reduce_precision(v, 8, 7)


def iota(shape, dim):
    return lax.broadcasted_iota(jnp.int32, shape, dim)


def sigmoid(v):
    return 1.0 / (1.0 + jnp.exp(-v))


def spread_matrix():
    return (iota((LANES, HALF), 1) // HEADDIM == iota((LANES, HALF), 0)).astype(F32)


def adamw_step(weight, gradient, moment_one, moment_two, step_rate, weight_decay):
    one_next = BETA_ONE * moment_one + (1.0 - BETA_ONE) * gradient
    two_next = BETA_TWO * moment_two + (1.0 - BETA_TWO) * gradient * gradient
    corrected = one_next / (1.0 - BETA_ONE**STEP)
    scale_next = jnp.sqrt(two_next / (1.0 - BETA_TWO**STEP)) + ADAM_EPS
    weight_next = weight - step_rate * (corrected / scale_next + weight_decay * weight)
    return (one_next, two_next, weight_next)


def swap_cores(value):
    return lax.ppermute(value, "c", [(0, 1), (1, 0)])


def regroup(value, turn):
    pairs = [
        (x * 2 + c, (2 * c + (x + turn) % 2) * 2 + x // 2) for x in range(4) for c in range(2)
    ]
    return lax.ppermute(value, ("x", "c"), pairs)


def cross_halves(value):
    pairs = []
    for y in range(4):
        for c in range(2):
            to = (y, c) if y // 2 == c else (y ^ 2, 1 - c)
            pairs.append((y * 2 + c, to[0] * 2 + to[1]))
    return lax.ppermute(value, ("y", "c"), pairs)


def along_y(value, steps):
    return lax.ppermute(value, "y", [(y, y + steps) for y in range(4) if 0 <= y + steps < 4])


def partner(axis, turn):
    pairs = []
    for i in range(4):
        for c in range(2):
            pairs.append((i * 2 + c, (i ^ (1 if (turn + c) % 2 == 0 else 3)) * 2 + c))
    return (axis, "c"), pairs


def exchange(value, axis, turn):
    axes, pairs = partner(axis, turn)
    return lax.ppermute(value, axes, pairs)


def block_order(order):
    first = jnp.where(lax.axis_index("c") == 0, 1, 3)
    second = 4 - first
    block = jnp.arange(64)
    place = {a: lax.axis_index(a) for a in CHIPS}
    for at, axis in enumerate(order):
        high = (block >> (5 - 2 * at)) & 1
        low = (block >> (4 - 2 * at)) & 1
        place[axis] = place[axis] ^ (high * first) ^ (low * second)
    return [place[a] + jnp.zeros((64,), jnp.int32) for a in CHIPS]


def rows_of(blocks):
    return (blocks[:, None] * ROWS + jnp.arange(ROWS)[None, :]).reshape(-1)


def in_rows(order):
    y, x, z = block_order(order)
    return rows_of((y * 4 + x) * 4 + z)


def out_rows(order):
    y, x, z = block_order(order)
    return rows_of((((y % 2) * 4 + x) * 4 + z) * 2 + y // 2)


def pick(rows):
    return (rows[:, None] == iota((1536, 1536), 1)).astype(BF16)


class Halving:
    def __init__(self, sends, keeps, orders):
        self.sends = [v.astype(BF16) for v in sends]
        self.keeps, self.orders, self.step = keeps, orders, 0

    def start(self):
        self.arrived = [
            exchange(v, order[self.step // 2], self.step % 2)
            for v, order in zip(self.sends, self.orders)
        ]

    def add(self):
        totals = [keep + got.astype(F32) for keep, got in zip(self.keeps, self.arrived)]
        self.step += 1
        if self.step == 6:
            self.totals = totals
            return
        half = totals[0].shape[0] // 2
        self.sends = [t[half:].astype(BF16) for t in totals]
        self.keeps = [t[:half] for t in totals]
        self.start()


def wait(halvings, *values):
    held = [h.arrived for h in halvings], [h.keeps for h in halvings], values
    arrived, keeps, values = lax.optimization_barrier(held)
    for h, a, k in zip(halvings, arrived, keeps):
        h.arrived, h.keeps = a, k
        h.add()
    return values


PAIRS = HALF_HEADS // 2


def product(terms, a, b):
    return jnp.einsum(terms, a, b, preferred_element_type=F32)


def by_pair(value):
    pairs = [value[:, p * LANES : (p + 1) * LANES] for p in range(PAIRS)]
    return jnp.stack(pairs).reshape(PAIRS, CHUNKS, CHUNK, LANES)


def from_pairs(value):
    return jnp.concatenate([value[p].reshape(TOKENS, LANES) for p in range(PAIRS)], axis=1)


def one_head(value):
    left = iota((2, 1, LANES), 2) // HEADDIM == iota((2, 1, LANES), 0)
    return jnp.where(left, value[:, :, None], jnp.zeros((), value.dtype))


def decays(cl):
    heads = cl[:, :HALF_HEADS].T.reshape(PAIRS, 2, CHUNKS, CHUNK).transpose(0, 2, 1, 3)
    causal = iota((CHUNK, CHUNK), 0) >= iota((CHUNK, CHUNK), 1)
    differ = jnp.where(causal, heads[..., :, None] - heads[..., None, :], 0.0)
    return jnp.where(causal, jnp.exp(differ), 0.0)


def pack_state(state, decay):
    high = rounded(decay)
    middle = rounded(decay - high)
    low = rounded(decay - high - middle)
    at = iota((16, LANES), 0)
    rows = jnp.where(at == 0, high, jnp.where(at == 1, middle, 0.0))
    rows = jnp.where(at == 2, low, rows)
    return jnp.concatenate([state, rows], axis=0).astype(BF16)


def unpack_state(packed):
    rows = packed[HALF : HALF + 3].astype(F32)
    return packed[:HALF].astype(F32), rows[0] + rows[1] + rows[2]


def per_row(head_values):
    heads = head_values[..., :HALF_HEADS, None]
    wide = jnp.broadcast_to(heads, heads.shape[:-1] + (HEADDIM,))
    return wide.reshape(head_values.shape[:-1] + (HALF, 1))


def combine(packed, way, unpack):
    near, far, farthest = [unpack(along_y(packed, way * k)) for k in (1, 2, 3)]
    return near[0] + per_row(near[1]) * (far[0] + per_row(far[1]) * farthest[0])


def pack_full(state, decay):
    return jnp.concatenate([state, jnp.broadcast_to(decay[None], (8, LANES))], axis=0)


def unpack_full(packed):
    return packed[:HALF], packed[HALF]


def chunked(value):
    return value.reshape(CHUNKS, CHUNK, value.shape[-1])


def flat(value):
    return value.reshape(TOKENS, value.shape[-1])


def on_device(
    block_in,
    cotangent,
    in_master,
    in_moment1,
    in_moment2,
    out_master,
    out_moment1,
    out_moment2,
    conv_master,
    conv_moment1,
    conv_moment2,
    gain_master,
    gain_moment1,
    gain_moment2,
    head_master,
    head_moment1,
    head_moment2,
):
    core = lax.axis_index("c")
    x_at = lax.axis_index("x")
    first_core = core == 0
    even_x = x_at % 2 == 0

    def ordered(flag, mine, other, axis=0):
        return jnp.where(
            flag, jnp.concatenate([mine, other], axis=axis), jnp.concatenate([other, mine], axis=axis)
        )

    riders_out = jnp.concatenate(
        [
            jnp.pad(conv_master, ((0, 0), (0, LANES - HALF_HEADS - 26))),
            jnp.pad(gain_master[None], ((0, 6), (0, LANES - HALF_HEADS - 36))),
        ],
        axis=0,
    )

    def half_columns(c):
        return jnp.concatenate(
            [
                in_master[:, INNER + c * HALF : INNER + (c + 1) * HALF],
                in_master[:, 2 * INNER : INNER + CONV],
                in_master[:, INNER + CONV + c * HALF_HEADS : INNER + CONV + (c + 1) * HALF_HEADS],
                riders_out,
                in_master[:, c * HALF : (c + 1) * HALF],
            ],
            axis=1,
        )

    halves = [half_columns(0), half_columns(1)]
    mine = jnp.where(first_core, halves[0], halves[1])
    theirs = jnp.where(first_core, halves[1], halves[0])
    in_rows_low = ordered(first_core, mine, swap_cores(theirs)).astype(BF16)
    out_rows_low = cross_halves(out_master).astype(BF16)
    both = jnp.stack([block_in, cotangent], axis=1)
    flipped = both[::-1]
    got = [regroup(jnp.where(even_x, both, flipped)[k], k) for k in range(2)]
    own_both = ordered(even_x, got[0], got[1], axis=1)
    out_rows_low, own_both = lax.optimization_barrier((out_rows_low, own_both))
    w_in = lax.all_gather(in_rows_low, CHIPS, axis=0, tiled=True)
    w_crit = w_in[:, :CRIT]
    w_gate = w_in[:, CRIT:]
    w_out = (
        lax.all_gather(out_rows_low, CHIPS, axis=0, tiled=True)
        .reshape(2, 2, 16, ROWS, WIDTH)
        .transpose(1, 2, 0, 3, 4)
        .reshape(HALF, WIDTH)
    )
    smalls = w_crit[:, ACT:]
    device_at, slot_at = iota((1536, 1), 0) // 12, iota((1536, 1), 0) % 12

    def gather_small(columns, width, slots):
        unfold = (HALF_HEADS + columns % width == iota((LANES, columns.shape[1]), 0)).astype(BF16)
        wide = jnp.where(device_at == columns // width, mm(smalls, unfold), 0.0)
        return mm((slot_at == slots).astype(BF16), wide, TN)

    norm_gain = gather_small(iota((1, WIDTH), 1), 36, 5 + iota((1, 8), 1))[0]
    gate_gain = gather_small(WIDTH + core * HALF + iota((1, HALF), 1), 36, 5 + iota((1, 8), 1))[0]
    conv_at = iota((1, ACT), 1)
    conv_at = jnp.where(conv_at < HALF, core * HALF + conv_at, INNER - HALF + conv_at)
    conv_weights = gather_small(conv_at, 26, iota((1, 8), 1))
    head_half = jnp.pad(
        lax.dynamic_slice(head_master, (0, core * HALF_HEADS), (3, HALF_HEADS)),
        ((0, 0), (0, LANES - HALF_HEADS)),
    )
    decay_rate = -jnp.exp(head_half[0])

    all_both = ordered(first_core, own_both, swap_cores(own_both), axis=1)
    own_in, own_cot = own_both[0], own_both[1]
    tokens, cot = all_both[0], all_both[1]
    halo = along_y(tokens[TOKENS - HALO :], 1)
    extended = jnp.concatenate([tokens, halo], axis=0).astype(F32)
    inv = lax.rsqrt(jnp.mean(extended * extended, axis=1, keepdims=True) + NORM_EPS)
    normed = (extended * inv * norm_gain).astype(BF16)

    crit = mm(normed, w_crit)
    ext = jnp.concatenate([crit[TOKENS + 8 :, :ACT], crit[:TOKENS, :ACT]], axis=0)
    preact = conv_weights[KERNEL] + sum(
        conv_weights[k] * ext[5 + k : 5 + k + TOKENS] for k in range(KERNEL)
    )
    gate_of_act = sigmoid(preact)
    act = preact * gate_of_act
    head_x = act[:, :HALF]
    bc = act[:, HALF:]
    dt_in = crit[:TOKENS, ACT:] + head_half[1]
    real = iota((1, LANES), 1) < HALF_HEADS
    dt = jnp.where(real, jax.nn.softplus(dt_in), 0.0)
    log_decay = dt * decay_rate
    below = (iota((CHUNK, CHUNK), 0) >= iota((CHUNK, CHUNK), 1)).astype(F32)
    below = jnp.broadcast_to(below[None], (CHUNKS, CHUNK, CHUNK))
    cl = jnp.einsum("kts,ksh->kth", below, chunked(log_decay), precision=EXACT)
    spread = spread_matrix()
    u = head_x * exact(dt, spread)
    u_low = rounded(u)
    lasts = cl[:, -1]
    to_end = flat(jnp.exp(lasts[:, None] - cl))
    cl = flat(cl)
    to_end_wide = exact(to_end, spread)
    from_start_wide = exact(jnp.exp(cl), spread)
    u_wide = u * to_end_wide
    b_proj, c_proj = chunked(bc[:, :STATE]), chunked(bc[:, STATE:])
    b_low, c_low = b_proj.astype(BF16), c_proj.astype(BF16)
    own = jnp.einsum("ktr,ktn->krn", chunked(u_wide), b_proj, precision=PRECISE)
    def between(i, j):
        return per_row(jnp.exp(sum(lasts[i:j])) if j > i else jnp.ones((LANES,), F32))

    local = [jnp.zeros_like(own[0])]
    for k in range(CHUNKS):
        local.append(sum(between(i + 1, k + 1) * own[i] for i in range(k + 1)))
    piece_decay = jnp.exp(jnp.sum(lasts, axis=0))
    incoming = combine(pack_full(local[CHUNKS], piece_decay), 1, unpack_full)
    decay = decays(cl)
    scores = jnp.einsum("ktn,ksn->kts", c_proj, b_proj, precision=PRECISE)
    mixes = (scores[None, :, None] * decay).astype(BF16)
    u_pairs = one_head(by_pair(u_low.astype(BF16)))
    y_chunk = from_pairs(product("pkjts,pkjsc->pktc", mixes, u_pairs))

    starts = jnp.stack([between(0, k) * incoming + local[k] for k in range(CHUNKS)])
    state_end = between(0, CHUNKS) * incoming + local[CHUNKS]
    y_state = flat(jnp.einsum("ktn,krn->ktr", c_proj, starts, precision=PRECISE)) * from_start_wide
    y_ssd = y_chunk + y_state
    skip_wide = exact(head_half[2:3], spread)
    mixed = y_ssd + skip_wide * head_x

    gate = mm(normed[:TOKENS], w_gate)
    gate_sig = sigmoid(gate)
    gate_silu = gate * gate_sig
    (d_gated,) = lax.optimization_barrier((mm(cot, w_out, NT),))
    g = mixed * gate_silu
    e = d_gated * gate_gain
    sums = jnp.concatenate(
        [jnp.sum(g * g, axis=1, keepdims=True), jnp.sum(e * g, axis=1, keepdims=True)], axis=1
    )
    sums = (sums + swap_cores(sums)) / INNER
    r = lax.rsqrt(sums[:, :1] + NORM_EPS)
    gated_low = (g * r * gate_gain).astype(BF16)
    d_g = r * e - (r * r * r) * g * sums[:, 1:]
    d_gate_gain = jnp.sum(d_gated * g * r, axis=0)
    dy = d_g * gate_silu
    d_gate = (d_g * mixed * (gate_sig * (1.0 + gate * (1.0 - gate_sig)))).astype(BF16)
    dy_low = rounded(dy)

    dy_start = chunked(dy * from_start_wide)
    chunk_backs = jnp.einsum("ktr,ktn->krn", dy_start, c_proj, precision=PRECISE)
    back = [None] * CHUNKS
    for k in range(CHUNKS):
        back[k] = sum((between(k + 1, i) * chunk_backs[i] for i in range(k + 1, CHUNKS)), jnp.zeros_like(own[0]))
    to_before = sum(between(0, i) * chunk_backs[i] for i in range(CHUNKS))
    leaving = combine(pack_state(to_before, piece_decay), -1, unpack_state)
    def own_rows(value):
        return jnp.where(first_core, value[:OWN], value[OWN:]), jnp.where(
            first_core, value[OWN:], value[:OWN]
        )

    def to_owner(value):
        low, high = value[:CHUNK], value[CHUNK:]
        sent = [jnp.where(even_x, low, high), jnp.where(even_x, high, low)]
        back0, back1 = regroup(sent[0], 0), regroup(sent[1], 1)
        return jnp.where(even_x, jnp.stack([back0, back1]), jnp.stack([back1, back0]))

    order_gate, order_out = ("x", "z", "y"), ("z", "x", "y")
    order_a, order_b = ("y", "z", "x"), ("z", "y", "x")
    normed_gate = mm(pick(in_rows(order_gate)), normed, NT).astype(BF16)
    normed_a = mm(pick(in_rows(order_a)), normed, NT).astype(BF16)
    normed_b = mm(pick(in_rows(order_b)), normed, NT).astype(BF16)
    gated_b = mm(pick(out_rows(order_out)), gated_low, NT).astype(BF16)
    middle = WIDTH // 2
    first = Halving(
        [mm(normed_gate[middle:, :TOKENS], d_gate), mm(gated_b[middle:], cot)],
        [mm(normed_gate[:middle, :TOKENS], d_gate), mm(gated_b[:middle], cot)],
        [order_gate, order_out],
    )
    first.start()

    dy_pairs = by_pair(dy_low.astype(BF16))
    du_chunk = from_pairs(product("pkjts,pkjtc->pksc", mixes, one_head(dy_pairs)))
    both = product("pktc,pkjsc->pkjts", dy_pairs, u_pairs)
    d_scores = jnp.sum(decay * both, axis=(0, 2)).astype(BF16)
    db_chunk = product("kts,ktn->ksn", d_scores, c_low)
    dc_chunk = product("kts,ksn->ktn", d_scores, b_low)

    part_out = mm(gated_low, w_out)
    kept, other = own_rows(part_out)
    own_out = own_in.astype(F32) + (kept + swap_cores(other))
    block_out = to_owner(own_out.astype(BF16))

    leaving, du_chunk, db_chunk, dc_chunk = wait([first], leaving, du_chunk, db_chunk, dc_chunk)

    ends = jnp.stack([between(k + 1, CHUNKS) * leaving + back[k] for k in range(CHUNKS)])
    du = du_chunk + flat(jnp.einsum("ktn,krn->ktr", b_proj, ends, precision=PRECISE)) * to_end_wide
    d_b = flat(db_chunk + jnp.einsum("ktr,krn->ktn", chunked(u_wide), ends, precision=PRECISE))
    d_c = flat(dc_chunk + jnp.einsum("ktr,krn->ktn", dy_start, starts, precision=PRECISE))
    du, d_b, d_c = wait([first], du, d_b, d_c)
    d_bc = jnp.concatenate([d_b, d_c], axis=1)
    nexts = jnp.concatenate([starts[1:], state_end[None]], axis=0)
    carries = exact(jnp.sum(ends * nexts, axis=2), spread, NT)
    d_cl = chunked(exact(dy_low * y_ssd - u_low * du, spread, NT))
    d_log_decay = flat(jnp.einsum("kts,kth->ksh", below, d_cl, precision=PRECISE) + carries[:, None])
    d_dt = exact(head_x * du, spread, NT) + d_log_decay * decay_rate
    d_dt_raw = jnp.where(real, d_dt * sigmoid(dt_in), 0.0)
    d_head = jnp.stack(
        [
            jnp.sum(d_log_decay * log_decay, axis=0),
            jnp.sum(d_dt_raw, axis=0),
            exact(jnp.sum(dy * head_x, axis=0, keepdims=True), spread, NT)[0],
        ]
    )
    d_x = exact(dt, spread) * du + skip_wide * dy
    d_act = jnp.concatenate([d_x, d_bc], axis=1)
    d_pre = d_act * (gate_of_act * (1.0 + preact * (1.0 - gate_of_act)))
    (d_pre,) = wait([first], d_pre)
    d_ext = sum(
        conv_weights[k] * jnp.pad(d_pre, ((5 + k, 3 - k), (0, 0))) for k in range(KERNEL)
    )
    d_conv = jnp.where(iota((8, ACT), 0) == KERNEL, jnp.sum(d_pre, axis=0)[None], 0.0)
    for k in range(KERNEL):
        tap = jnp.sum(d_pre * ext[5 + k : 5 + k + TOKENS], axis=0)
        d_conv = jnp.where(iota((8, ACT), 0) == k, tap[None], d_conv)
    d_ext = jnp.concatenate([d_ext[8:], jnp.zeros((8, ACT), F32), d_ext[:8]], axis=0)
    d_crit = jnp.concatenate(
        [d_ext, jnp.pad(d_dt_raw, ((0, HALO), (0, 0)))], axis=1
    ).astype(BF16)
    (d_crit,) = wait([first], d_crit)

    y_of, x_of, z_of = block_order(order_b)
    row_at = rows_of((y_of * 4 + x_of) * 4 + z_of)[:, None]
    device_of, slot_of = row_at // 12, row_at % 12
    slot_pick = (slot_of == iota((1536, 8), 1)).astype(F32)
    conv_spread = jnp.where(conv_at // 26 == device_of, exact(slot_pick, d_conv), 0.0)
    fold = (conv_at.T % 26 + HALF_HEADS == iota((ACT, LANES), 1)).astype(BF16)
    gain_at = WIDTH + core * HALF + iota((1536, HALF), 1)
    gain_spread = jnp.where((gain_at // 36 == device_of) & (slot_of == 5), d_gate_gain[None, :], 0.0)
    gain_fold = (
        (WIDTH + core * HALF + iota((HALF, LANES), 0)) % 36 + HALF_HEADS == iota((HALF, LANES), 1)
    ).astype(BF16)
    riders = mm(conv_spread, fold) + mm(gain_spread, gain_fold)

    crit_b = jnp.concatenate([d_crit[:, PART:]], axis=1)

    def part_b(rows):
        with_riders = jnp.pad(riders[rows], ((0, 0), (CRIT - PART - LANES, 0)))
        return mm(normed_b[rows], crit_b) + with_riders

    second = Halving(
        [mm(normed_a[middle:], d_crit[:, :PART]), part_b(slice(middle, None))],
        [mm(normed_a[:middle], d_crit[:, :PART]), part_b(slice(0, middle))],
        [order_a, order_b],
    )

    second.sends, d_crit_late = lax.optimization_barrier((second.sends, d_crit))
    second.start()
    d_normed = mm(d_crit_late, w_crit, NT)
    d_halo = along_y(d_normed[TOKENS:], -1)
    d_normed = d_normed[:TOKENS] + mm(d_gate, w_gate, NT)
    d_normed = jnp.concatenate(
        [d_normed[: TOKENS - HALO], d_normed[TOKENS - HALO :] + d_halo], axis=0
    )
    kept, other = own_rows(d_normed)
    d_own = kept + swap_cores(other)
    own = own_in.astype(F32)
    own_inv = lax.rsqrt(jnp.mean(own * own, axis=1, keepdims=True) + NORM_EPS)
    d_own = d_own * norm_gain
    d_tokens = own_inv * d_own - (own_inv * own_inv * own_inv) * own * jnp.mean(
        own * d_own, axis=1, keepdims=True
    )
    returning = (own_cot.astype(F32) + d_tokens).astype(BF16)

    head_own = jnp.pad(d_head, ((0, 5), (0, 0)))
    for step in range(6):
        head_got = exchange(head_own, CHIPS[step // 2], step % 2)
        head_own, head_got = wait([second, first] if step < 2 else [second], head_own, head_got)
        head_own = head_own + head_got
        if step == 3:
            head_own, returning = lax.optimization_barrier((head_own, returning))
            input_grad = to_owner(returning)
    head_other = swap_cores(head_own)
    rows_a, rows_b = second.totals
    gate_rows, out_rows_grad = first.totals

    rows = jnp.concatenate([rows_a, rows_b, gate_rows], axis=1)
    mine = jnp.where(first_core, rows[:12], rows[12:])
    theirs = jnp.where(first_core, rows[12:], rows[:12])
    theirs, input_grad = lax.optimization_barrier((swap_cores(theirs), input_grad))
    input_grad = input_grad.astype(F32)
    h0 = jnp.where(first_core, mine, theirs)
    h1 = jnp.where(first_core, theirs, mine)
    in_share = jnp.concatenate(
        [
            h0[:, CRIT:],
            h1[:, CRIT:],
            h0[:, :HALF],
            h1[:, :HALF],
            h0[:, HALF:ACT] + h1[:, HALF:ACT],
            h0[:, ACT : ACT + HALF_HEADS],
            h1[:, ACT : ACT + HALF_HEADS],
        ],
        axis=1,
    )
    riding = h0[:, ACT + HALF_HEADS : CRIT] + h1[:, ACT + HALF_HEADS : CRIT]
    conv_share = riding[:5, :26]
    out_share = cross_halves(out_rows_grad)
    at_device = ((lax.axis_index("y") * 4 + x_at) * 4 + lax.axis_index("z")) * 2 + core
    w_own = rounded(in_master)
    own_gain = lax.dynamic_slice(norm_gain, (at_device * 12,), (12,))
    gain_rows = jnp.sum(w_own * in_share, axis=1) / own_gain
    thirds = [
        lax.ppermute(gain_rows, ALL, [(3 * d + k, d) for d in range(128) if 3 * d + k < 128])
        for k in range(3)
    ]
    gain_share = jnp.concatenate(thirds) + riding[5, :36]
    head_share = ordered(
        first_core, head_own[:3, :HALF_HEADS], head_other[:3, :HALF_HEADS], axis=1
    )

    in_next = adamw_step(in_master, in_share, in_moment1, in_moment2, MATRIX_RATE, MATRIX_DECAY)
    out_next = adamw_step(
        out_master, out_share, out_moment1, out_moment2, MATRIX_RATE, MATRIX_DECAY
    )
    conv_next = adamw_step(conv_master, conv_share, conv_moment1, conv_moment2, SMALL_RATE, 0.0)
    gain_next = adamw_step(gain_master, gain_share, gain_moment1, gain_moment2, SMALL_RATE, 0.0)
    head_next = adamw_step(head_master, head_share, head_moment1, head_moment2, SMALL_RATE, 0.0)
    return (
        block_out,
        input_grad,
        *in_next,
        *out_next,
        *conv_next,
        *gain_next,
        *head_next,
    )


def solution(mesh):
    fine = Mesh(mesh.devices.reshape(4, 4, 4, 2), ALL)
    tokens = P(("z", "c"), ("y", "x"), None)
    rows = P(ALL, None)
    columns = P(None, ALL)
    flat = P(ALL)
    return jax.shard_map(
        on_device,
        mesh=fine,
        in_specs=(tokens, tokens) + (rows,) * 6 + (columns,) * 3 + (flat,) * 3 + (P(),) * 3,
        out_specs=(tokens, tokens) + (rows,) * 6 + (columns,) * 3 + (flat,) * 3 + (P(),) * 3,
        check_vma=False,
    )
```
